128 devices in a mesh: seq: 16 (over z_hi, y, core), batch: 8 (over x, z_lo).
Axes of the slice: x: 4, y: 4, z: 4 (z_hi: 2, z_lo: 2; z = z_hi * 2 + z_lo), core: 2. Of those that a mesh axis runs over, the one named last changes fastest.
Arguments:
- tokens: bfloat16 [16, 1024, 1088], P('batch', 'seq'), may hold values from -6 to 6
- segments: int32 [16, 1024], P('batch', 'seq'), may hold values from 0 to 256, as said below
- adapter_pick: int32 [16], P('batch'), may hold values from 0 to 7
- norm_gain: float32 [2, 2, 1088], replicated, may hold values from 0.1 to 1.9
- w_qkv: bfloat16 [2, 3551232], P(None, ('seq', 'batch')), may hold values from -0.1875 to 0.1875
- w_out: bfloat16 [2, 1183744], P(None, ('seq', 'batch')), may hold values from -0.75 to 0.75
- w_up: bfloat16 [2, 4734976], P(None, ('seq', 'batch')), may hold values from -0.1875 to 0.1875
- w_down: bfloat16 [2, 4734976], P(None, ('seq', 'batch')), may hold values from -0.09375 to 0.09375
- a_qkv: bfloat16 [2, 1088, 128], replicated, may hold values from -0.1875 to 0.1875
- b_qkv: bfloat16 [2, 128, 3264], replicated, may hold values from -0.75 to 0.75
- a_out: bfloat16 [2, 1088, 128], replicated, may hold values from -0.1875 to 0.1875
- b_out: bfloat16 [2, 128, 1088], replicated, may hold values from -0.75 to 0.75
- a_up: bfloat16 [2, 1088, 128], replicated, may hold values from -0.1875 to 0.1875
- b_up: bfloat16 [2, 128, 4352], replicated, may hold values from -0.75 to 0.75
- a_down: bfloat16 [2, 4352, 128], replicated, may hold values from -0.09375 to 0.09375
- b_down: bfloat16 [2, 128, 1088], replicated, may hold values from -0.75 to 0.75
- grad_out: bfloat16 [16, 1024, 1088], P('batch', 'seq'), may hold values from -6 to 6
Outputs:
- out: bfloat16 [16, 1024, 1088], P('batch', 'seq')
- grad_tokens: float32 [16, 1024, 1088], P('batch', 'seq')
- grad_a_qkv: float32 [2, 1088, 128], replicated
- grad_b_qkv: float32 [2, 128, 3264], replicated
- grad_a_out: float32 [2, 1088, 128], replicated
- grad_b_out: float32 [2, 128, 1088], replicated
- grad_a_up: float32 [2, 1088, 128], replicated
- grad_b_up: float32 [2, 128, 4352], replicated
- grad_a_down: float32 [2, 4352, 128], replicated
- grad_b_down: float32 [2, 128, 1088], replicated
The draws below stay inside these ranges and needn't reach their ends.
Inputs may be any that keep to these rules, and one draw needn't show every extreme that they name: `segments`: along each sequence the numbers start at 0 and rise by 0 or 1 from one position to the next; equal numbers mark one document. In one sequence of each group of 2 that share an index of batch, one document begins within the first 64 positions and ends within the last 64.
All inputs are finite; a program needn't handle non-finite values.
Results may differ from the reference program's by a relative error of at most 0.024.
Values may be sent and summed in bfloat16 or wider, within the bound.
No kernel may reach another device: no remote copies, remote signals or barrier semaphores. Data moves between devices by JAX's collectives and lax.ppermute only.
A program may use at most 320 MiB of HBM per device.

```python
import math
import jax
import jax.numpy as jnp
from jax import lax

D = 1088
HEADS = 17
HEAD_DIM = 64
FF = 4352
LAYERS = 2
ADAPTERS = 8
RANK = 16
MICRO = 2
SEQ_LEN = 1024
ROWS = 64
SEQS = 16
QBLOCK = 512


def draw_segments(key, part):
    key = jax.random.fold_in(key, 7)
    key_rate, key_flags, key_pick, key_begin, key_end = jax.random.split(key, 5)
    positions = jnp.arange(SEQ_LEN, dtype=jnp.int32)
    levels = jax.random.randint(key_rate, (SEQS, 1), 0, 4)
    period = 8 * 4 ** levels
    boundary = (jax.random.randint(key_flags, (SEQS, SEQ_LEN), 0, period) == 0).astype(jnp.int32)
    boundary = jnp.where(positions[None, :] == 0, 0, boundary)
    groups = SEQS // MICRO
    chosen = jax.random.randint(key_pick, (groups, 1), 0, MICRO)
    micro_index = jnp.arange(MICRO, dtype=jnp.int32)[None, :]
    spanning = (micro_index == chosen).reshape(SEQS, 1)
    dense_row = (micro_index == (chosen + 1) % MICRO) & (jnp.arange(groups, dtype=jnp.int32)[:, None] == 0)
    dense_row = dense_row.reshape(SEQS, 1)
    dense_flags = (positions[None, :] % 2 == 0) & (positions[None, :] > 0)
    boundary = jnp.where(dense_row & dense_flags, 1, boundary)
    doc_begin = jax.random.randint(key_begin, (SEQS, 1), 1, ROWS)
    finish = jax.random.randint(key_end, (SEQS, 1), SEQ_LEN - ROWS + 1, SEQ_LEN)
    inside = (positions[None, :] > doc_begin) & (positions[None, :] < finish)
    doc_edges = (positions[None, :] == doc_begin) | (positions[None, :] == finish)
    boundary = jnp.where(spanning & inside, 0, boundary)
    boundary = jnp.where(spanning & doc_edges, 1, boundary)
    counted = jnp.cumsum(boundary, axis=1)
    return jnp.minimum(counted, SEQ_LEN // 4).astype(jnp.int32)


def set_ends(values, key, smallest, largest):
    extent = values.shape
    spot = [jax.random.randint(jax.random.fold_in(key, axis), (), 0, extent[axis]) for axis in range(len(extent))]
    values = values.at[tuple(spot)].set(smallest)
    longest = extent.index(max(extent))
    spot[longest] = (spot[longest] + 1) % extent[longest]
    return values.at[tuple(spot)].set(largest)


def shard_levels(key, shape, shards, smallest, high):
    factor_of = 1.0
    for axis_at, blocks in shards:
        draws = jax.random.uniform(jax.random.fold_in(jax.random.fold_in(key, 6), axis_at), (blocks,), jnp.float32, smallest / len(shards), high / len(shards))
        factor_of = factor_of * jnp.repeat(jnp.exp(draws), shape[axis_at] // blocks).reshape((-1,) + (1,) * (len(shape) - 1 - axis_at))
    return factor_of


def noise(key, extent, scale, limit, shards=(), kind=jnp.bfloat16):
    entries = jax.random.normal(key, extent, jnp.float32) * scale
    if len(shards) > 0:
        entries = shard_levels(key, extent, shards, -0.22, 0.18) * entries
    return jnp.clip(entries, min=-limit, max=limit).astype(kind)


def setup_inputs(seed: int = 0) -> dict:
    arg_keys = jax.random.split(jax.random.key(seed), 18)
    tokens = noise(arg_keys[0], (SEQS, SEQ_LEN, D), 1.0, 6.0, ((0, 8), (1, 16)))
    segments = draw_segments(jax.random.fold_in(arg_keys[17], 71), 0)
    adapter_pick = set_ends(jax.random.randint(arg_keys[2], (SEQS,), 0, ADAPTERS), jax.random.fold_in(arg_keys[2], 1), 0, ADAPTERS - 1).astype(jnp.int32)
    norm_gain = jnp.clip(1.0 + 0.18 * jax.random.normal(arg_keys[3], (LAYERS, 2, D), jnp.float32), 0.1, 1.9)
    w_qkv = noise(arg_keys[4], (LAYERS, 3 * D * D), D ** -0.5, 0.1875, ((1, 128),))
    w_out = noise(arg_keys[5], (LAYERS, D * D), (D // 16) ** -0.5, 0.75, ((1, 128),))
    w_up = noise(arg_keys[6], (LAYERS, D * FF), D ** -0.5, 0.1875, ((1, 128),))
    w_down = noise(arg_keys[7], (LAYERS, FF * D), FF ** -0.5, 0.09375, ((1, 128),))
    a_qkv = noise(arg_keys[8], (LAYERS, D, ADAPTERS * RANK), D ** -0.5, 0.1875)
    b_qkv = noise(arg_keys[9], (LAYERS, ADAPTERS * RANK, 3 * D), (4 * RANK) ** -0.5, 0.75)
    a_out = noise(arg_keys[10], (LAYERS, D, ADAPTERS * RANK), D ** -0.5, 0.1875)
    b_out = noise(arg_keys[11], (LAYERS, ADAPTERS * RANK, D), (4 * RANK) ** -0.5, 0.75)
    a_up = noise(arg_keys[12], (LAYERS, D, ADAPTERS * RANK), D ** -0.5, 0.1875)
    b_up = noise(arg_keys[13], (LAYERS, ADAPTERS * RANK, FF), (4 * RANK) ** -0.5, 0.75)
    a_down = noise(arg_keys[14], (LAYERS, FF, ADAPTERS * RANK), FF ** -0.5, 0.09375)
    b_down = noise(arg_keys[15], (LAYERS, ADAPTERS * RANK, D), (4 * RANK) ** -0.5, 0.75)
    grad_out = noise(arg_keys[16], (SEQS, SEQ_LEN, D), 1.0, 6.0, ((0, 8), (1, 16)))
    return {"tokens": tokens, "segments": segments, "adapter_pick": adapter_pick, "norm_gain": norm_gain, "w_qkv": w_qkv, "w_out": w_out, "w_up": w_up, "w_down": w_down, "a_qkv": a_qkv, "b_qkv": b_qkv, "a_out": a_out, "b_out": b_out, "a_up": a_up, "b_up": b_up, "a_down": a_down, "b_down": b_down, "grad_out": grad_out}


@jax.custom_vjp
def low(v):
    return lax.optimization_barrier(v.astype(jnp.bfloat16)).astype(jnp.float32)

@jax.custom_vjp
def low_back(v):
    return v

def low_keep(v):
    return (low(v), None)

def low_pass(kept, grad):
    return (grad,)

def back_keep(v):
    return (v, None)

def back_low(kept, grad):
    return (low(grad),)
low.defvjp(low_keep, low_pass)
low_back.defvjp(back_keep, back_low)

def matmul(left_side, right_side):
    return jnp.dot(left_side, right_side, precision=lax.Precision.HIGHEST)

def layer_norm(values, gain_row):
    row_mean = lax.optimization_barrier(jnp.mean(values, axis=-1, keepdims=True))
    centred = values - row_mean
    spread = lax.optimization_barrier(jnp.mean(centred * centred, axis=-1, keepdims=True))
    return centred * lax.rsqrt(spread + 1e-05) * gain_row

def project(normed, weight, adapter_in, adapter_out, column_mask):
    lowrank = low(low_back(matmul(normed, adapter_in) * column_mask))
    return matmul(normed, weight) + matmul(lowrank, adapter_out)

def attend_block(queries, key_heads, value_heads, segment_row, first_row):
    block_rows = queries.shape[0]
    score_scale = 1.0 / math.sqrt(HEAD_DIM)
    query_pos = first_row + jnp.arange(block_rows, dtype=jnp.int32)
    key_pos = jnp.arange(key_heads.shape[0], dtype=jnp.int32)
    query_seg = lax.dynamic_slice_in_dim(segment_row, first_row, block_rows, 0)
    visible = (key_pos[None, :] <= query_pos[:, None]) & (segment_row[None, :] == query_seg[:, None])
    scores = jnp.einsum('qhd,khd->hqk', queries, key_heads, precision=lax.Precision.HIGHEST) * score_scale
    scores = low_back(scores)
    scores = jnp.where(visible[None], scores, -1e+30)
    soft_weights = low(jax.nn.softmax(scores, axis=-1))
    return jnp.einsum('hqk,khd->qhd', soft_weights, value_heads, precision=lax.Precision.HIGHEST)

def attend(queries, key_heads, value_heads, segment_row):
    checked = jax.checkpoint(attend_block)
    starts = jnp.arange(SEQ_LEN // QBLOCK, dtype=jnp.int32) * QBLOCK

    def one_block(first_row):
        return checked(lax.dynamic_slice_in_dim(queries, first_row, QBLOCK, 0), key_heads, value_heads, segment_row, first_row)
    blocks = lax.map(one_block, starts)
    return blocks.reshape(SEQ_LEN, D)

def forward(hidden, adapter_set, weights, norm_gain, segment_row, column_mask):
    for layer_idx in range(LAYERS):
        normed = low(layer_norm(hidden, norm_gain[layer_idx, 0]))
        projected = low(low_back(project(normed, weights[0][layer_idx], adapter_set[0][layer_idx], adapter_set[1][layer_idx], column_mask)))
        queries = projected[:, :D].reshape(SEQ_LEN, HEADS, HEAD_DIM)
        key_heads = projected[:, D:2 * D].reshape(SEQ_LEN, HEADS, HEAD_DIM)
        value_heads = projected[:, 2 * D:].reshape(SEQ_LEN, HEADS, HEAD_DIM)
        context = low(low_back(attend(queries, key_heads, value_heads, segment_row)))
        branch = low_back(project(context, weights[1][layer_idx], adapter_set[2][layer_idx], adapter_set[3][layer_idx], column_mask))
        middle = hidden + branch
        normed_two = low(layer_norm(middle, norm_gain[layer_idx, 1]))
        upward = low_back(project(normed_two, weights[2][layer_idx], adapter_set[4][layer_idx], adapter_set[5][layer_idx], column_mask))
        active = low(jax.nn.gelu(upward, approximate=False))
        hidden = middle + low_back(project(active, weights[3][layer_idx], adapter_set[6][layer_idx], adapter_set[7][layer_idx], column_mask))
    return hidden

def reference(tokens, segments, adapter_pick, norm_gain, w_qkv, w_out, w_up, w_down, a_qkv, b_qkv, a_out, b_out, a_up, b_up, a_down, b_down, grad_out):
    weights = (w_qkv.astype(jnp.float32).reshape(LAYERS, D, 3 * D), w_out.astype(jnp.float32).reshape(LAYERS, D, D), w_up.astype(jnp.float32).reshape(LAYERS, D, FF), w_down.astype(jnp.float32).reshape(LAYERS, FF, D))
    adapters = (a_qkv.astype(jnp.float32), b_qkv.astype(jnp.float32), a_out.astype(jnp.float32), b_out.astype(jnp.float32), a_up.astype(jnp.float32), b_up.astype(jnp.float32), a_down.astype(jnp.float32), b_down.astype(jnp.float32))
    column_group = jnp.arange(ADAPTERS * RANK, dtype=jnp.int32) // RANK

    def one_sequence(totals, inputs):
        token_rows, grad_rows, segment_row, pick_row = inputs
        column_mask = (column_group == pick_row).astype(jnp.float32)

        def run_layers(hidden, adapter_set):
            return forward(hidden, adapter_set, weights, norm_gain, segment_row, column_mask)
        result, pull_back = jax.vjp(run_layers, token_rows.astype(jnp.float32), adapters)
        grad_hidden, grad_adapters = pull_back(grad_rows.astype(jnp.float32))
        totals = jax.tree.map(jnp.add, totals, grad_adapters)
        return (totals, (result.astype(jnp.bfloat16), grad_hidden))
    zero_grads = jax.tree.map(jnp.zeros_like, adapters)
    totals, outputs = lax.scan(one_sequence, zero_grads, (tokens, grad_out, segments, adapter_pick))
    return (outputs[0], outputs[1], totals[0], totals[1], totals[2], totals[3], totals[4], totals[5], totals[6], totals[7])
```

```python
import jax
import jax.numpy as jnp
from jax import lax
from jax.experimental import pallas as pl
from jax.experimental.pallas import tpu as pltpu
from jax.sharding import PartitionSpec as P

D = 1088
HEADS = 17
HEAD_DIM = 64
FF = 4352
RANK = 16
WIDE = 1152
PAIRS = 9
HALF = 64
KEYS = 1024
BF = jnp.bfloat16
F32 = jnp.float32
NEG = -1e30

SWAP = [(i, i ^ 8) for i in range(16)]
CORE = [(i, i ^ 1) for i in range(16)]
UP = [(i, (i & 8) | ((i + 2) & 7)) for i in range(16)]
DOWN = [(i, (i & 8) | ((i - 2) & 7)) for i in range(16)]
def at_chip(z, y, x, core):
    return ((z // 2 * 4 + y) * 2 + core) * 8 + x * 2 + z % 2


ALL = [[at_chip(z, y, x, c) for z in range(4) for y in range(4) for x in range(4) for c in range(2)]]
SAME_SEQUENCE = [[at_chip(z, y, x, c) for y in range(4) for c in range(2)] for z in range(4) for x in range(4)]
SAME_PLACE = [[at_chip(z, y, x, c) for z in range(4) for x in range(4)] for y in range(4) for c in range(2)]


def z_shift(by):
    return [
        (at_chip(z, y, x, c), at_chip((z + by) % 4, y, x, c))
        for z in range(4) for y in range(4) for x in range(4) for c in range(2)
    ]


def x_shift(by):
    return [(i, (i + 2 * by) % 8) for i in range(8)]


BOTH = ("seq", "batch")
TURNED = (D, D, D, FF, 3 * D, D, D)
PART_A, PART_B = 1664, 640
PART = PART_A + PART_B

LINES = 304
AT_OUT = 224
N_QKV, N_OUT, N_UP, N_DOWN = 217, 73, 289, 289
BLOCK = 136


def dot(a, b):
    return jnp.dot(a, b, preferred_element_type=F32)


def dot_t(a, b):
    return lax.dot_general(a, b, (((1,), (1,)), ((), ())), preferred_element_type=F32)


def t_dot(a, b):
    return lax.dot_general(a, b, (((0,), (0,)), ((), ())), preferred_element_type=F32)


def norm_stats(v):
    mean = jnp.mean(v, axis=-1, keepdims=True)
    centred = v - mean
    inv = lax.rsqrt(jnp.mean(centred * centred, axis=-1, keepdims=True) + 1e-05)
    return centred * inv, inv


def norm_back(v, gain, grad):
    r, inv = norm_stats(v)
    gr = grad * gain
    return inv * (
        gr - jnp.mean(gr, axis=-1, keepdims=True) - r * jnp.mean(gr * r, axis=-1, keepdims=True)
    )


def widen(a):
    return jnp.pad(a, ((0, 0), (0, WIDE - D)))


def lanes(rows):
    return lax.broadcasted_iota(jnp.int32, (rows, 128), 1)


def two_heads(block):
    low = lanes(block.shape[0]) < HEAD_DIM
    zero = jnp.zeros_like(block)
    return jnp.concatenate([jnp.where(low, block, zero), jnp.where(low, zero, block)], axis=0)


def one_block(stacked):
    rows = stacked.shape[0] // 2
    return jnp.where(lanes(rows) < HEAD_DIM, stacked[:rows], stacked[rows:])


def pick_extra(rows, pair):
    spot = lanes(rows) - HEAD_DIM
    head = 2 * pair

    def of(h):
        return ((spot >= 3 * h) & (spot < 3 * h + 3)).astype(F32)

    return jnp.concatenate([of(head), of(head + 1)], axis=0)


def gathered(own_ref, sib_ref, half):
    width = own_ref.shape[-1]
    return jnp.concatenate(
        [own_ref[:, half].reshape(4 * HALF, width), sib_ref[:, half].reshape(4 * HALF, width)],
        axis=0,
    )


def row_terms(term):
    first = term.astype(BF).astype(F32)
    rest = term - first
    second = rest.astype(BF).astype(F32)
    third = rest - second
    turn = (lanes(term.shape[0]) - HEAD_DIM) % 3
    return jnp.where(turn == 0, first, jnp.where(turn == 1, second, third)).astype(BF)


def fwd_kernel(
    q_ref, ko_ref, ks_ref, vo_ref, vs_ref, lpos, lseg, kpos, kseg, ctx_ref, qe_ref, b_lo, b_hi, acc
):
    pair = pl.program_id(0)

    @pl.when(pair == 0)
    def _():
        ok = (kpos[...] <= lpos[...]) & (kseg[...] == lseg[...])
        bias = jnp.where(ok, 0.0, NEG)
        lo = bias[:HALF, : KEYS // 2]
        hi = bias[HALF:]
        b_lo[...] = jnp.concatenate([lo, lo], axis=0)
        b_hi[...] = jnp.concatenate([hi, hi], axis=0)
        acc[...] = jnp.zeros_like(acc)

    q = q_ref[...]
    k_lo = gathered(ko_ref, ks_ref, 0)
    k_hi = gathered(ko_ref, ks_ref, 1)
    v_lo = gathered(vo_ref, vs_ref, 0)
    v_hi = gathered(vo_ref, vs_ref, 1)
    spot = lanes(HALF) - HEAD_DIM
    head = 2 * pair

    def attend(rows, keys, values, bias, at):
        s = dot_t(two_heads(rows), keys) + bias
        top = jnp.max(s, axis=1, keepdims=True)
        e = jnp.exp(s - top)
        total = jnp.sum(e, axis=1, keepdims=True)
        p = (e * (1.0 / total)).astype(BF)
        ctx_ref[pl.ds(at, HALF), :] = one_block(dot(p, values)).astype(BF)
        lse = top + jnp.log(total)
        old = acc[pl.ds(at, HALF), :]
        new = jnp.where((spot >= 3 * head) & (spot < 3 * head + 3), -lse[:HALF], old)
        new = jnp.where((spot >= 3 * head + 3) & (spot < 3 * head + 6), -lse[HALF:], new)
        acc[pl.ds(at, HALF), :] = new

    attend(q[:HALF], k_lo, v_lo, b_lo[...], 0)
    attend(
        q[HALF:],
        jnp.concatenate([k_lo, k_hi], axis=0),
        jnp.concatenate([v_lo, v_hi], axis=0),
        b_hi[...],
        HALF,
    )
    qe_ref[...] = q

    @pl.when(pair == PAIRS - 1)
    def _():
        where = lanes(2 * HALF)
        keep = (where >= HEAD_DIM) & (where < HEAD_DIM + 3 * HEADS)
        extra = jnp.where(keep, row_terms(acc[...]), jnp.zeros((2 * HALF, 128), BF))
        qe_ref[...] = jnp.where(where < HEAD_DIM, q, extra)


def dq_kernel(
    qe_ref, ge_ref, qx_ref, gx_ref, ko_ref, ks_ref, vo_ref, vs_ref, lpos, lseg, kpos, kseg,
    gq_ref, b_lo, b_hi
):
    pair = pl.program_id(0)

    @pl.when(pair == 0)
    def _():
        ok = (kpos[...] <= lpos[...]) & (kseg[...] == lseg[...])
        bias = jnp.where(ok, 0.0, NEG)
        lo = bias[:HALF, : KEYS // 2]
        hi = bias[HALF:]
        b_lo[...] = jnp.concatenate([lo, lo], axis=0)
        b_hi[...] = jnp.concatenate([hi, hi], axis=0)

    k_lo = gathered(ko_ref, ks_ref, 0)
    k_hi = gathered(ko_ref, ks_ref, 1)
    v_lo = gathered(vo_ref, vs_ref, 0)
    v_hi = gathered(vo_ref, vs_ref, 1)
    low = lanes(HALF) < HEAD_DIM
    last = pair == PAIRS - 1

    def with_terms(rows, extra):
        rows = jnp.where(last & ~low, jnp.zeros_like(rows), rows)
        mask = pick_extra(HALF, pair).astype(BF)
        both = jnp.concatenate([extra, extra], axis=0) * mask
        return jnp.concatenate([two_heads(rows), both], axis=1)

    def back(at, keys, values, bias):
        ones = jnp.ones((keys.shape[0], 128), BF)
        q = with_terms(qe_ref[pl.ds(at, HALF), :], qx_ref[pl.ds(at, HALF), :])
        g = with_terms(ge_ref[pl.ds(at, HALF), :], gx_ref[pl.ds(at, HALF), :])
        s = dot_t(q, jnp.concatenate([keys, ones], axis=1)) + bias
        dp = dot_t(g, jnp.concatenate([values, ones], axis=1))
        ds = (jnp.exp(s) * dp).astype(BF)
        gq_ref[pl.ds(at, HALF), :] = (one_block(dot(ds, keys)) * 0.125).astype(BF)

    back(0, k_lo, v_lo, b_lo[...])
    back(
        HALF,
        jnp.concatenate([k_lo, k_hi], axis=0),
        jnp.concatenate([v_lo, v_hi], axis=0),
        b_hi[...],
    )


def dkv_kernel(
    k_ref, v_ref, qo_ref, qs_ref, go_ref, gs_ref, qxo_ref, qxs_ref, gxo_ref, gxs_ref,
    lpos, lseg, kpos, kseg, gk_ref, gv_ref, b_lo, b_hi
):
    pair = pl.program_id(0)

    @pl.when(pair == 0)
    def _():
        ok = (lpos[...] <= kpos[...]) & (kseg[...] == lseg[...])
        bias = jnp.where(ok, 0.0, NEG)
        lo = bias[:HALF]
        hi = bias[HALF:, KEYS // 2 :]
        b_lo[...] = jnp.concatenate([lo, lo], axis=0)
        b_hi[...] = jnp.concatenate([hi, hi], axis=0)

    low = lanes(HALF) < HEAD_DIM
    last = pair == PAIRS - 1
    q_lo, q_hi = gathered(qo_ref, qs_ref, 0), gathered(qo_ref, qs_ref, 1)
    g_lo, g_hi = gathered(go_ref, gs_ref, 0), gathered(go_ref, gs_ref, 1)
    qx_lo, qx_hi = gathered(qxo_ref, qxs_ref, 0), gathered(qxo_ref, qxs_ref, 1)
    gx_lo, gx_hi = gathered(gxo_ref, gxs_ref, 0), gathered(gxo_ref, gxs_ref, 1)
    terms = pick_extra(HALF, pair).astype(BF)

    def back(half, q, g, qx, gx, bias):
        k = jnp.concatenate([two_heads(k_ref[half]), terms], axis=1)
        v = jnp.concatenate([two_heads(v_ref[half]), terms], axis=1)
        p = jnp.exp(dot_t(k, jnp.concatenate([q, qx], axis=1)) + bias)
        dp = dot_t(v, jnp.concatenate([g, gx], axis=1))
        ds = (p * dp).astype(BF)
        gk = one_block(dot(ds, q)).astype(BF)
        gv = one_block(dot(p.astype(BF), g)).astype(BF)
        drop = last & ~low
        gk_ref[half] = jnp.where(drop, jnp.zeros_like(gk), gk)
        gv_ref[half] = jnp.where(drop, jnp.zeros_like(gv), gv)

    def both(a, b):
        return jnp.concatenate([a, b], axis=0)

    back(0, both(q_lo, q_hi), both(g_lo, g_hi), both(qx_lo, qx_hi), both(gx_lo, gx_hi), b_lo[...])
    back(1, q_hi, g_hi, qx_hi, gx_hi, b_hi[...])


def spec_rows(at):
    return pl.BlockSpec((2 * HALF, 128), lambda i: (0, at(i)))


def spec_all(at):
    return pl.BlockSpec((4, 2, HALF, 128), lambda i: (0, 0, 0, at(i)))


def spec_half(at):
    return pl.BlockSpec((2, HALF, 128), lambda i: (0, 0, at(i)))


def same(i):
    return i


def value_at(i):
    return i + PAIRS


def last_at(i):
    return PAIRS - 1


def spec_whole(shape):
    return pl.BlockSpec(shape, lambda i: (0, 0))


MASK_SPECS = [
    spec_whole((2 * HALF, 1)),
    spec_whole((2 * HALF, 1)),
    spec_whole((1, KEYS)),
    spec_whole((1, KEYS)),
]
BIAS_SCRATCH = [
    pltpu.VMEM((2 * HALF, KEYS // 2), F32),
    pltpu.VMEM((2 * HALF, KEYS), F32),
]
BIAS_SCRATCH_T = [
    pltpu.VMEM((2 * HALF, KEYS), F32),
    pltpu.VMEM((2 * HALF, KEYS // 2), F32),
]
PARAMS = pltpu.CompilerParams(vmem_limit_bytes=32 * 1024 * 1024)
FLAT = jax.ShapeDtypeStruct((2 * HALF, WIDE), BF)


def attend_fwd(q, kv_own, kv_sib, where):
    return pl.pallas_call(
        fwd_kernel,
        grid=(PAIRS,),
        out_shape=(FLAT, FLAT),
        in_specs=[spec_rows(same), spec_all(same), spec_all(same), spec_all(value_at)]
        + [spec_all(value_at)]
        + MASK_SPECS,
        out_specs=(spec_rows(same), spec_rows(same)),
        scratch_shapes=BIAS_SCRATCH + [pltpu.VMEM((2 * HALF, 128), F32)],
        compiler_params=PARAMS,
        cost_estimate=pl.CostEstimate(
            flops=PAIRS * 4 * 256 * KEYS * 128, bytes_accessed=6 << 20, transcendentals=PAIRS * 256 * KEYS
        ),
    )(q, kv_own, kv_sib, kv_own, kv_sib, *where)


def attend_dq(qe, ge, kv_own, kv_sib, where):
    return pl.pallas_call(
        dq_kernel,
        grid=(PAIRS,),
        out_shape=FLAT,
        in_specs=[spec_rows(same), spec_rows(same), spec_rows(last_at), spec_rows(last_at)]
        + [spec_all(same), spec_all(same), spec_all(value_at), spec_all(value_at)]
        + MASK_SPECS,
        out_specs=spec_rows(same),
        scratch_shapes=BIAS_SCRATCH,
        compiler_params=PARAMS,
        cost_estimate=pl.CostEstimate(
            flops=PAIRS * 8 * 256 * KEYS * 128, bytes_accessed=6 << 20, transcendentals=PAIRS * 256 * KEYS
        ),
    )(qe, ge, qe, ge, kv_own, kv_sib, kv_own, kv_sib, *where)


def attend_dkv(kv, qe_own, qe_sib, ge_own, ge_sib, where):
    part = jax.ShapeDtypeStruct((2, HALF, WIDE), BF)
    return pl.pallas_call(
        dkv_kernel,
        grid=(PAIRS,),
        out_shape=(part, part),
        in_specs=[spec_half(same), spec_half(value_at)]
        + [spec_all(same)] * 4
        + [spec_all(last_at)] * 4
        + MASK_SPECS,
        out_specs=(spec_half(same), spec_half(same)),
        scratch_shapes=BIAS_SCRATCH_T,
        compiler_params=PARAMS,
        cost_estimate=pl.CostEstimate(
            flops=PAIRS * 12 * 256 * KEYS * 128, bytes_accessed=6 << 20, transcendentals=PAIRS * 256 * KEYS
        ),
    )(kv, kv, qe_own, qe_sib, ge_own, ge_sib, qe_own, qe_sib, ge_own, ge_sib, *where)


def ring_start(block):
    return lax.ppermute(block, "seq", UP), lax.ppermute(block, "seq", DOWN)


def ring_far(block, before, after):
    far_lo = lax.ppermute(before[0], "seq", UP)
    far_hi = lax.ppermute(after[1], "seq", DOWN)
    return jnp.stack([block, before, after, jnp.stack([far_lo, far_hi])])


def other_core(own):
    return lax.ppermute(own, "seq", CORE)


def tie(*values):
    return lax.optimization_barrier(values)


def eighths(turned, straight):
    def cut(a, part):
        return jnp.pad(a, ((0, 0), (0, 8 * part - a.shape[1]))).reshape(RANK, 8, part)

    first = cut(jnp.concatenate(turned, axis=1), PART_A)
    return jnp.swapaxes(jnp.concatenate([first, cut(straight, PART_B)], axis=2), 0, 1)


def by_adapter_kernel(picks, *refs):
    parts, out_ref, acc = refs[:-2], refs[-2], refs[-1]
    acc[...] = jnp.zeros_like(acc)
    at = 0
    for ref in parts:
        for k in range(ref.shape[0]):
            rows = pl.ds(pl.multiple_of(picks[at] * RANK, RANK), RANK)
            acc[rows, :] = acc[rows, :] + ref[k].astype(F32)
            at += 1
    for j in range(PART // 128):
        square = acc[:, 128 * j : 128 * (j + 1)]
        square = square.T if 128 * j < PART_A else square
        out_ref[128 * j : 128 * (j + 1), :] = square.astype(BF)


def by_adapter(parts, picks):
    return pl.pallas_call(
        by_adapter_kernel,
        out_shape=jax.ShapeDtypeStruct((PART, 128), BF),
        in_specs=[pl.BlockSpec(memory_space=pltpu.SMEM)]
        + [pl.BlockSpec(memory_space=pltpu.VMEM)] * len(parts),
        out_specs=pl.BlockSpec(memory_space=pltpu.VMEM),
        scratch_shapes=[pltpu.VMEM((8 * RANK, PART), F32)],
        compiler_params=PARAMS,
        cost_estimate=pl.CostEstimate(flops=16 * RANK * PART, bytes_accessed=2 << 20, transcendentals=0),
    )(picks, *parts)


def unfold_kernel(place, own_ref, sib_ref, one_ref, *outs):
    turned, straight = outs[:-1], outs[-1]

    def rows(layer, e, at, n):
        if layer == 1:
            return one_ref[e, at : at + n, :].astype(F32)
        k = place[e]
        mine = own_ref[k % 4, at : at + n, :]
        other = sib_ref[k % 4, at : at + n, :]
        return jnp.where(k < 4, mine.astype(F32), other.astype(F32))

    for layer in range(2):
        start = 0
        for out, width in zip(turned, TURNED):
            at = start
            while at < start + width:
                n = min(start + width, (at // PART_A + 1) * PART_A) - at
                out[layer, at - start : at - start + n, :] = rows(layer, at // PART_A, at % PART_A, n)
                at += n
            start += width
        squares = PART_B // 128
        for t in range(FF // 128):
            value = rows(layer, t // squares, PART_A + 128 * (t % squares), 128)
            straight[layer, :, 128 * t : 128 * (t + 1)] = value


def unfold(own, sib, one, place):
    shapes = [(2, w, 128) for w in TURNED] + [(2, 128, FF)]
    whole = pl.BlockSpec(memory_space=pltpu.VMEM)
    return pl.pallas_call(
        unfold_kernel,
        out_shape=tuple(jax.ShapeDtypeStruct(shape, F32) for shape in shapes),
        in_specs=[pl.BlockSpec(memory_space=pltpu.SMEM), whole, whole, whole],
        out_specs=(whole,) * 8,
        compiler_params=pltpu.CompilerParams(vmem_limit_bytes=56 * 1024 * 1024),
        cost_estimate=pl.CostEstimate(flops=0, bytes_accessed=28 << 20, transcendentals=0),
    )(place, own, sib, one)


def share(w_qkv, w_out, w_up, w_down, z_lo):
    def half_row(w, front, lines):
        size = lines * 128 - w.shape[1]
        first = jnp.pad(w, ((0, 0), (0, size)))
        second = jnp.pad(w, ((0, 0), (front, size - front)))
        return jnp.where(z_lo == 0, first, second).reshape(-1, lines, 128)

    def put(a, room):
        return jnp.pad(a, ((0, 0), (0, room - a.shape[1]), (0, 0)))

    attention = [
        put(half_row(w_qkv, 32, N_QKV), AT_OUT),
        put(half_row(w_out, 32, N_OUT), LINES - AT_OUT),
    ]
    up, down = put(w_up.reshape(-1, N_UP, 128), LINES), put(w_down.reshape(-1, N_DOWN, 128), LINES)
    return jnp.concatenate(attention, axis=1), jnp.concatenate([up, down], axis=1)


def spin(a):
    return pltpu.roll(a, HEAD_DIM, 1)


def fill(ref, base, lines):
    ref[pl.ds(base, lines.shape[0], stride=2), :] = lines


def between(ref, base, n):
    now, later = ref[pl.ds(base, n, stride=2), :], ref[pl.ds(base + 2, n, stride=2), :]
    ref[pl.ds(base + 1, n, stride=2), :] = spin(jnp.where(lanes(n) < HEAD_DIM, later, now))


def columns(ref, dst, to, start, units, step=2):
    got = ref[pl.ds(start, dst.shape[0], stride=units), :].astype(BF)
    n = min(128, dst.shape[1] - to)
    dst[:, to : to + n] = got[:, :n]


def lines_of(ref, pair, zl, start, n):
    return ref[0, zl, 0, pair % 4, pair // 4, start : start + n, :].astype(F32)


def unpack_attention_kernel(g_ref, q_ref, kv_ref, out_ref, s_qkv, s_out):
    low = lanes(1) < HEAD_DIM
    zero = jnp.zeros((1, 128), F32)
    for pair in range(8):
        qkv0, qkv1 = (lines_of(g_ref, pair, zl, 0, N_QKV) for zl in range(2))
        out0, out1 = (lines_of(g_ref, pair, zl, AT_OUT, N_OUT) for zl in range(2))
        base, base_out = pair * 867, pair * 289
        fill(s_qkv, base, qkv0)
        fill(s_qkv, base + 433, qkv1)
        between(s_qkv, base, N_QKV - 1)
        between(s_qkv, base + 433, N_QKV)
        s_qkv[pl.ds(base + 432, 1), :] = qkv0[N_QKV - 1 :] + spin(jnp.where(low, qkv1[:1], zero))
        s_qkv[pl.ds(base + 433, 1), :] = qkv1[:1] + spin(jnp.where(low, zero, qkv0[N_QKV - 1 :]))
        fill(s_out, base_out, out0)
        fill(s_out, base_out + 144, out1)
        s_out[pl.ds(base_out + 144, 1), :] = out0[N_OUT - 1 :] + out1[:1]
        between(s_out, base_out, N_OUT - 1)
        between(s_out, base_out + 144, N_OUT - 1)
    half = lanes(BLOCK) < HEAD_DIM
    for dst, to, first in ((q_ref, 0, 0), (kv_ref, 0, 17), (kv_ref, WIDE, 34)):
        for j in range(8):
            columns(s_qkv, dst, to + 128 * j, first + 2 * j, 51)
        got = s_qkv[pl.ds(first + 16, BLOCK, stride=51), :]
        dst[:, to + D - HEAD_DIM : to + WIDE] = jnp.where(half, got, 0.0).astype(BF)
    for j in range(9):
        columns(s_out, out_ref, 128 * j, 2 * j, 17)


def unpack_mlp_kernel(g_up, g_down, up_ref, down_ref, s_up, s_down):
    for pair in range(8):
        for zl in range(2):
            at = pair * 2 + zl
            s_up[pl.ds(at * N_UP, N_UP), :] = lines_of(g_up, pair, zl, 0, N_UP)
            fill(s_down, at * 2 * N_DOWN, lines_of(g_down, pair, zl, 0, N_DOWN))
    for at in range(16):
        between(s_down, at * 2 * N_DOWN, N_DOWN)
    for j in range(34):
        columns(s_up, up_ref, 128 * j, j, 34)
    for j in range(9):
        columns(s_down, down_ref, 128 * j, 2 * j, 17)


def unpack(kernel, got, at, outs, scratch_lines):
    g = got.reshape(2, 2, 4, 4, 2, -1, 128)

    def spec(k):
        return pl.BlockSpec((1, 2, 1, 4, 2, LINES, 128), lambda i: (i // 4, 0, i % 4, 0, 0, k, 0))

    return pl.pallas_call(
        kernel,
        grid=(8,),
        out_shape=tuple(jax.ShapeDtypeStruct((8 * r, w), BF) for r, w in outs),
        in_specs=[spec(k) for k in at],
        out_specs=tuple(pl.BlockSpec((r, w), lambda i: (i, 0)) for r, w in outs),
        scratch_shapes=[pltpu.VMEM((n, 128), F32) for n in scratch_lines],
        compiler_params=pltpu.CompilerParams(vmem_limit_bytes=48 * 1024 * 1024),
        cost_estimate=pl.CostEstimate(
            flops=0, bytes_accessed=len(at) * (20 << 20), transcendentals=0
        ),
    )(*[g] * len(at))


def unpack_attention(got, at):
    outs = [(BLOCK, WIDE), (BLOCK, 2 * WIDE), (BLOCK, D)]
    return unpack(unpack_attention_kernel, got, [at], outs, [8 * 867 + 8, 8 * 289 + 8])


def unpack_mlp(got, at):
    outs = [(BLOCK, FF), (4 * BLOCK, D)]
    return unpack(unpack_mlp_kernel, got, [at, at + 1], outs, [16 * N_UP, 32 * N_DOWN + 8])


def shards(
    tokens, segments, adapter_pick, norm_gain, w_qkv, w_out, w_up, w_down,
    a_qkv, b_qkv, a_out, b_out, a_up, b_up, a_down, b_down, grad_out
):
    layers = norm_gain.shape[0]
    index = lax.axis_index("seq")
    z_hi, place = index // 8, index % 8
    core, y = place % 2, place // 2

    attention, mlp = share(w_qkv, w_out, w_up, w_down, lax.axis_index("batch") % 2)

    def gather(a):
        return lax.all_gather(a, BOTH, axis=0, tiled=True, axis_index_groups=ALL)

    early = gather(jnp.concatenate([attention[0], mlp[0], attention[1]], axis=0))
    late = gather(mlp[1])

    def halves(own, other):
        return jnp.where(z_hi == 0, jnp.stack([own, other]), jnp.stack([other, own]))

    def mine(a):
        return lax.dynamic_index_in_dim(a, z_hi, 0, keepdims=False)

    def theirs(a):
        return lax.dynamic_index_in_dim(a, 1 - z_hi, 0, keepdims=False)

    sent = lax.ppermute(jnp.stack([theirs(tokens), theirs(grad_out)]), "seq", SWAP)
    hidden = halves(mine(tokens), sent[0]).reshape(2 * HALF, D).astype(F32)
    grad_hidden = halves(mine(grad_out), sent[1]).reshape(2 * HALF, D).astype(F32)
    pick = mine(adapter_pick)

    row = jnp.zeros((2, KEYS), jnp.int32)
    row = lax.dynamic_update_slice(row, segments, (0, index * HALF))
    seg = mine(lax.psum(row, "seq")).reshape(2, 8, HALF)
    offset = jnp.arange(HALF, dtype=jnp.int32)
    start = jnp.array([0, KEYS // 2], jnp.int32)[:, None]
    lpos = (start + place * HALF + offset[None]).reshape(2 * HALF, 1)
    lseg = lax.dynamic_index_in_dim(seg, place, 1, keepdims=False).reshape(2 * HALF, 1)
    ys = (y + jnp.array([0, 3, 1, 2], jnp.int32)) % 4
    order = jnp.concatenate([2 * ys + core, 2 * ys + 1 - core])
    kpos = (start[:, :, None] + (order * HALF)[None, :, None] + offset).reshape(1, KEYS)
    kseg = jnp.take(seg, order, axis=1).reshape(1, KEYS)
    where = (lpos, lseg, kpos, kseg)

    steps = jnp.array([0, 3, 1, 2], jnp.int32)
    batch = lax.axis_index("batch")
    z, x = z_hi * 2 + batch % 2, batch // 2
    picks = lax.dynamic_update_slice(jnp.zeros((16,), jnp.int32), adapter_pick, (2 * batch,))
    picks = lax.psum(picks, "batch")

    picks, where, hidden = lax.optimization_barrier((picks, where, hidden))

    def sequence(zs, xs):
        return 2 * (2 * xs + zs % 2) + zs // 2

    four = jnp.arange(4, dtype=jnp.int32)
    picks_in_order = jnp.take(picks, sequence(four[:, None], four[None, :]).reshape(16))
    zs, xs = (z + steps) % 4, (x + steps) % 4
    picks_by_step = jnp.take(picks, sequence(zs[None, :], xs[:, None]).reshape(16))
    eight = jnp.arange(8, dtype=jnp.int32)
    back = jnp.array([0, 2, 3, 1], jnp.int32)
    place_by_step = 4 * ((eight % 2) ^ core) + jnp.take(back, (eight // 2 - y) % 4)

    def low_in(a, l):
        return lax.dynamic_slice_in_dim(a[l], pick * RANK, RANK, 1)

    def low_out(b, l):
        return lax.dynamic_slice_in_dim(b[l], pick * RANK, RANK, 0)

    def project(x, w, a, b):
        low = dot(x, a).astype(BF)
        return dot(x, w) + dot(low, b), low

    def pull(gz, x, low, w, a, b):
        glow = dot_t(gz, b).astype(BF)
        return dot_t(gz, w) + dot_t(glow, a), t_dot(glow, x), t_dot(low, gz)

    saved = []
    first = unpack_attention(early, 0)
    for l in range(layers):
        a_first = low_in(a_qkv, l)
        b_first = low_out(b_qkv, l)
        b_q = widen(b_first[:, :D])
        b_kv = jnp.concatenate([widen(b_first[:, D : 2 * D]), widen(b_first[:, 2 * D :])], axis=1)
        ad = [(low_in(a, l), low_out(b, l)) for a, b in ((a_out, b_out), (a_up, b_up), (a_down, b_down))]
        wq, wkv, wout = first
        n1 = (norm_stats(hidden)[0] * norm_gain[l, 0]).astype(BF)
        low_qkv = dot(n1, a_first).astype(BF)
        kv = (dot(n1, wkv) + dot(low_qkv, b_kv)).astype(BF).reshape(2, HALF, 2 * WIDE)
        before, after = ring_start(kv)
        q = (dot(n1, wq) + dot(low_qkv, b_q)).astype(BF) * jnp.asarray(0.125, BF)
        wup, wdown = unpack_mlp(early, 1) if l == 0 else unpack_mlp(late, 0)
        before, after, q, wup, wdown = tie(before, after, q, wup, wdown)
        kv_own = ring_far(kv, before, after)
        if l == 0:
            first = unpack_attention(early, 3)
            kv_own, *first = tie(kv_own, *first)
        kv_sib = other_core(kv_own)
        ctx, qe = attend_fwd(q, kv_own, kv_sib, where)
        ctx = ctx[:, :D]
        qe = qe.reshape(2, HALF, WIDE)
        q_before, q_after = ring_start(qe)
        proj, low_o = project(ctx, wout, *ad[0])
        middle = hidden + proj
        n2 = (norm_stats(middle)[0] * norm_gain[l, 1]).astype(BF)
        up, low_u = project(n2, wup, *ad[1])
        act = jax.nn.gelu(up, approximate=False).astype(BF)
        q_before, q_after, act = tie(q_before, q_after, act)
        qe_own = ring_far(qe, q_before, q_after)
        y_out, low_d = project(act, wdown, *ad[2])
        qe_own, y_out = tie(qe_own, y_out)
        qe_sib = other_core(qe_own)
        saved.append((hidden, n1, low_qkv, kv, kv_own, kv_sib, qe.reshape(2 * HALF, WIDE), qe_own, qe_sib, ctx, low_o, middle, n2, low_u, up, act, low_d, ad, a_first, b_q, b_kv, wq, wkv, wout, wup, wdown))
        hidden = middle + y_out

    heads_of = (jnp.arange(D, dtype=jnp.int32) // HEAD_DIM)[:, None]
    spot = jnp.arange(HEAD_DIM, dtype=jnp.int32)[None, :]
    spread = (heads_of == spot // 3).astype(F32)

    behind = None
    g = grad_hidden
    for l in reversed(range(layers)):
        (hidden_in, n1, low_qkv, kv, kv_own, kv_sib, qe, qe_own, qe_sib, ctx, low_o, middle, n2, low_u, up, act, low_d, ad, a_first, b_q, b_kv, wq, wkv, wout, wup, wdown) = saved[l]
        gact, ga_d, gb_d = pull(g.astype(BF), act, low_d, wdown, *ad[2])
        gup = jax.vjp(lambda v: jax.nn.gelu(v, approximate=False), up)[1](gact)[0].astype(BF)
        gn2, ga_u, gb_u = pull(gup, n2, low_u, wup, *ad[1])
        gh2 = g + norm_back(middle, norm_gain[l, 1], gn2)
        gctx, ga_o, gb_o = pull(gh2.astype(BF), ctx, low_o, wout, *ad[0])
        gctx = gctx.astype(BF)
        delta = -jnp.dot(
            gctx.astype(F32) * ctx.astype(F32), spread, precision=lax.Precision.HIGHEST
        )
        d1 = delta.astype(BF).astype(F32)
        d2 = (delta - d1).astype(BF).astype(F32)
        terms = jnp.where(spot % 3 == 0, d1, jnp.where(spot % 3 == 1, d2, delta - d1 - d2)).astype(BF)
        ge = jnp.concatenate([gctx, terms], axis=1)
        g_block = ge.reshape(2, HALF, WIDE)
        g_before, g_after = ring_start(g_block)
        if behind is not None:
            behind, ge = tie(behind, ge)
            behind = lax.all_gather(behind.astype(BF), BOTH, axis=0, axis_index_groups=SAME_PLACE)
        gq = attend_dq(qe, ge, kv_own, kv_sib, where)
        g_before, g_after, gq = tie(g_before, g_after, gq)
        ge_own = ring_far(g_block, g_before, g_after)
        gb_q, gx_q, glow_q = t_dot(low_qkv, gq), dot_t(gq, wq), dot_t(gq, b_q)
        ge_own, ga_d, gb_d, ga_u, gb_u, ga_o, gb_o, gb_q, gx_q, glow_q = tie(
            ge_own, ga_d, gb_d, ga_u, gb_u, ga_o, gb_o, gb_q, gx_q, glow_q
        )
        ge_sib = other_core(ge_own)
        gk, gv = attend_dkv(kv, qe_own, qe_sib, ge_own, ge_sib, where)
        gkv = jnp.concatenate([gk, gv], axis=2).reshape(2 * HALF, 2 * WIDE)
        glow = (glow_q + dot_t(gkv, b_kv)).astype(BF)
        ga_q, gb_kv = t_dot(glow, n1), t_dot(low_qkv, gkv)
        gb_q = [gb_q[:, :D], gb_kv[:, :D], gb_kv[:, WIDE : WIDE + D]]
        parts = eighths([ga_q, ga_o, ga_u, ga_d] + gb_q + [gb_o, gb_d], gb_u)
        if l == 0:
            got = lax.all_to_all(parts.astype(BF), BOTH, 0, 0, axis_index_groups=SAME_SEQUENCE)
            part = jnp.sum(got.astype(F32), axis=0).astype(BF)
            along_z = jnp.stack([part] + [lax.ppermute(part, BOTH, z_shift(by)) for by in (1, -1, 2)])
            behind, along_z = tie(behind, along_z)
            behind = by_adapter([behind], picks_in_order)
            one = lax.all_gather(behind, BOTH, axis=0, axis_index_groups=SAME_SEQUENCE)
            before = lax.ppermute(along_z, "batch", x_shift(1))
            after = lax.ppermute(along_z, "batch", x_shift(-1))
            far = [lax.ppermute(before[:2], "batch", x_shift(1)), lax.ppermute(after[2:], "batch", x_shift(-1))]
            whole = by_adapter([along_z, before, after] + far, picks_by_step)
            whole = whole.reshape(2, -1, 128)
            own = ring_far(whole, *ring_start(whole))
            sib = other_core(own).reshape(4, PART, 128)
            ga_q, ga_o, ga_u, ga_d, gb_q, gb_o, gb_d, gb_u = unfold(
                own.reshape(4, PART, 128), sib, one, place_by_step
            )
            gb_q, gb_o, gb_d = (jnp.swapaxes(a, 1, 2) for a in (gb_q, gb_o, gb_d))
        gn1 = gx_q + dot_t(gkv, wkv) + dot_t(glow, a_first)
        g = gh2 + norm_back(hidden_in, norm_gain[l, 0], gn1)
        if l > 0:
            parts, g = tie(parts, g)
            behind = lax.psum_scatter(
                parts, BOTH, scatter_dimension=0, axis_index_groups=SAME_SEQUENCE, tiled=True
            ).reshape(RANK, PART)

    def home(a):
        a = a.reshape(2, HALF, D)
        got = lax.ppermute(theirs(a), "seq", SWAP)
        return halves(mine(a), got)

    result, grad_tokens = home(hidden.astype(BF)), home(g)

    return result, grad_tokens, ga_q, gb_q, ga_o, gb_o, ga_u, gb_u, ga_d, gb_d


def solution(mesh):
    rows, flat, whole = P("batch", "seq", None), P(None, ("seq", "batch")), P()
    in_specs = (rows, P("batch", "seq"), P("batch"), whole) + (flat,) * 4 + (whole,) * 8 + (rows,)
    out_specs = (rows, rows) + (whole,) * 8
    return jax.shard_map(shards, mesh=mesh, in_specs=in_specs, out_specs=out_specs, check_vma=False)
```

```python
import jax
import jax.numpy as jnp
from jax import lax
from jax.experimental import pallas as pl
from jax.experimental.pallas import tpu as pltpu
from jax.sharding import PartitionSpec as P

D = 1088
HEADS = 17
HEAD_DIM = 64
FF = 4352
RANK = 16
WIDE = 1152
PAIRS = 9
GROUP = 3
SPAN = GROUP * 128
HALF = 64
KEYS = 1024
BF = jnp.bfloat16
F32 = jnp.float32
NEG = -1e30

SWAP = [(i, i ^ 8) for i in range(16)]
CORE = [(i, i ^ 1) for i in range(16)]
UP = [(i, (i & 8) | ((i + 2) & 7)) for i in range(16)]
DOWN = [(i, (i & 8) | ((i - 2) & 7)) for i in range(16)]
FAR = [(i, (i & 8) | ((i + 4) & 7)) for i in range(16)]
def at_chip(z, y, x, core):
    return ((z // 2 * 4 + y) * 2 + core) * 8 + x * 2 + z % 2


ALL = [[at_chip(z, y, x, c) for z in range(4) for y in range(4) for x in range(4) for c in range(2)]]
SAME_SEQUENCE = [[at_chip(z, y, x, c) for y in range(4) for c in range(2)] for z in range(4) for x in range(4)]
SAME_PLACE = [[at_chip(z, y, x, c) for z in range(4) for x in range(4)] for y in range(4) for c in range(2)]


def z_shift(by):
    return [
        (at_chip(z, y, x, c), at_chip((z + by) % 4, y, x, c))
        for z in range(4) for y in range(4) for x in range(4) for c in range(2)
    ]


def x_shift(by):
    return [(i, (i + 2 * by) % 8) for i in range(8)]


def y_shift(by):
    return [(i, (i & 8) | ((i + 2 * by) & 7)) for i in range(16)]


BOTH = ("seq", "batch")
SHIFTS = {"x": ("batch", x_shift), "y": ("seq", y_shift), "z": (BOTH, z_shift)}
TURNED = (D, D, D, FF, 3 * D, D, D)
PART_A, PART_B = 1664, 640
PART = PART_A + PART_B

LINES = 304
AT_OUT = 224
N_QKV, N_OUT, N_UP, N_DOWN = 217, 73, 289, 289
BLOCK = 136


def dot(a, b):
    return jnp.dot(a, b, preferred_element_type=F32)


def dot_t(a, b):
    return lax.dot_general(a, b, (((1,), (1,)), ((), ())), preferred_element_type=F32)


def t_dot(a, b):
    return lax.dot_general(a, b, (((0,), (0,)), ((), ())), preferred_element_type=F32)


def norm_stats(v):
    mean = jnp.mean(v, axis=-1, keepdims=True)
    centred = v - mean
    inv = lax.rsqrt(jnp.mean(centred * centred, axis=-1, keepdims=True) + 1e-05)
    return centred * inv, inv


def norm_back(v, gain, grad):
    r, inv = norm_stats(v)
    gr = grad * gain
    return inv * (
        gr - jnp.mean(gr, axis=-1, keepdims=True) - r * jnp.mean(gr * r, axis=-1, keepdims=True)
    )


def widen(a):
    return jnp.pad(a, ((0, 0), (0, WIDE - D)))


def lanes(rows):
    return lax.broadcasted_iota(jnp.int32, (rows, 128), 1)


def two_heads(block):
    low = lanes(block.shape[0]) < HEAD_DIM
    zero = jnp.zeros_like(block)
    return jnp.concatenate([jnp.where(low, block, zero), jnp.where(low, zero, block)], axis=0)


def one_block(stacked):
    rows = stacked.shape[0] // 2
    return jnp.where(lanes(rows) < HEAD_DIM, stacked[:rows], stacked[rows:])


def pick_extra(rows, pair):
    spot = lanes(rows) - HEAD_DIM
    head = 2 * pair

    def of(h):
        return ((spot >= 3 * h) & (spot < 3 * h + 3)).astype(F32)

    return jnp.concatenate([of(head), of(head + 1)], axis=0)


def gathered(own_ref, sib_ref, half, at):
    return jnp.concatenate(
        [ref[:, half, :, at : at + 128].reshape(4 * HALF, 128) for ref in (own_ref, sib_ref)], axis=0
    )


def row_terms(term):
    first = term.astype(BF).astype(F32)
    rest = term - first
    second = rest.astype(BF).astype(F32)
    third = rest - second
    turn = (lanes(term.shape[0]) - HEAD_DIM) % 3
    return jnp.where(turn == 0, first, jnp.where(turn == 1, second, third)).astype(BF)


def fwd_kernel(
    q_ref, ko_ref, ks_ref, vo_ref, vs_ref, lpos, lseg, kpos, kseg, ctx_ref, qe_ref, b_lo, b_hi, acc
):
    step = pl.program_id(0)

    @pl.when(step == 0)
    def _():
        ok = (kpos[...] <= lpos[...]) & (kseg[...] == lseg[...])
        bias = jnp.where(ok, 0.0, NEG)
        lo = bias[:HALF, : KEYS // 2]
        hi = bias[HALF:]
        b_lo[...] = jnp.concatenate([lo, lo], axis=0)
        b_hi[...] = jnp.concatenate([hi, hi], axis=0)
        acc[...] = jnp.zeros_like(acc)

    spot = lanes(HALF) - HEAD_DIM
    terms = [acc[:HALF, :], acc[HALF:, :]]
    for sub in range(GROUP):
        at = 128 * sub
        head = 2 * (step * GROUP + sub)
        k_lo = gathered(ko_ref, ks_ref, 0, at)
        k_hi = gathered(ko_ref, ks_ref, 1, at)
        v_lo = gathered(vo_ref, vs_ref, 0, at)
        v_hi = gathered(vo_ref, vs_ref, 1, at)

        def attend(half, keys, values, bias):
            s = dot_t(two_heads(q_ref[half * HALF : (half + 1) * HALF, at : at + 128]), keys) + bias
            top = jnp.max(s, axis=1, keepdims=True)
            e = jnp.exp(s - top)
            total = jnp.sum(e, axis=1, keepdims=True)
            p = (e * (1.0 / total)).astype(BF)
            ctx_ref[half * HALF : (half + 1) * HALF, at : at + 128] = one_block(dot(p, values)).astype(BF)
            lse = top + jnp.log(total)
            new = jnp.where((spot >= 3 * head) & (spot < 3 * head + 3), -lse[:HALF], terms[half])
            terms[half] = jnp.where((spot >= 3 * head + 3) & (spot < 3 * head + 6), -lse[HALF:], new)

        attend(0, k_lo, v_lo, b_lo[...])
        attend(
            1,
            jnp.concatenate([k_lo, k_hi], axis=0),
            jnp.concatenate([v_lo, v_hi], axis=0),
            b_hi[...],
        )
    acc[:HALF, :] = terms[0]
    acc[HALF:, :] = terms[1]
    qe_ref[...] = q_ref[...]

    @pl.when(step == PAIRS // GROUP - 1)
    def _():
        where = lanes(2 * HALF)
        keep = (where >= HEAD_DIM) & (where < HEAD_DIM + 3 * HEADS)
        extra = jnp.where(keep, row_terms(acc[...]), jnp.zeros((2 * HALF, 128), BF))
        qe_ref[:, SPAN - 128 :] = jnp.where(where < HEAD_DIM, q_ref[:, SPAN - 128 :], extra)


def dq_kernel(
    qe_ref, ge_ref, qx_ref, gx_ref, ko_ref, ks_ref, vo_ref, vs_ref, lpos, lseg, kpos, kseg,
    gq_ref, b_lo, b_hi
):
    step = pl.program_id(0)

    @pl.when(step == 0)
    def _():
        ok = (kpos[...] <= lpos[...]) & (kseg[...] == lseg[...])
        bias = jnp.where(ok, 0.0, NEG)
        lo = bias[:HALF, : KEYS // 2]
        hi = bias[HALF:]
        b_lo[...] = jnp.concatenate([lo, lo], axis=0)
        b_hi[...] = jnp.concatenate([hi, hi], axis=0)

    low = lanes(HALF) < HEAD_DIM
    for sub in range(GROUP):
        at = 128 * sub
        pair = step * GROUP + sub
        k_lo = gathered(ko_ref, ks_ref, 0, at)
        k_hi = gathered(ko_ref, ks_ref, 1, at)
        v_lo = gathered(vo_ref, vs_ref, 0, at)
        v_hi = gathered(vo_ref, vs_ref, 1, at)
        mask = pick_extra(HALF, pair).astype(BF)

        def with_terms(rows, extra):
            if sub == GROUP - 1:
                rows = jnp.where((pair == PAIRS - 1) & ~low, jnp.zeros_like(rows), rows)
            both = jnp.concatenate([extra, extra], axis=0) * mask
            return jnp.concatenate([two_heads(rows), both], axis=1)

        def back(half, keys, values, bias):
            rows = slice(half * HALF, (half + 1) * HALF)
            ones = jnp.ones((keys.shape[0], 128), BF)
            q = with_terms(qe_ref[rows, at : at + 128], qx_ref[rows, :])
            g = with_terms(ge_ref[rows, at : at + 128], gx_ref[rows, :])
            s = dot_t(q, jnp.concatenate([keys, ones], axis=1)) + bias
            dp = dot_t(g, jnp.concatenate([values, ones], axis=1))
            ds = (jnp.exp(s) * dp).astype(BF)
            gq_ref[rows, at : at + 128] = (one_block(dot(ds, keys)) * 0.125).astype(BF)

        back(0, k_lo, v_lo, b_lo[...])
        back(
            1,
            jnp.concatenate([k_lo, k_hi], axis=0),
            jnp.concatenate([v_lo, v_hi], axis=0),
            b_hi[...],
        )


def dkv_kernel(
    k_ref, v_ref, qo_ref, qs_ref, go_ref, gs_ref, qxo_ref, qxs_ref, gxo_ref, gxs_ref,
    lpos, lseg, kpos, kseg, gk_ref, gv_ref, b_lo, b_hi
):
    step = pl.program_id(0)

    @pl.when(step == 0)
    def _():
        ok = (lpos[...] <= kpos[...]) & (kseg[...] == lseg[...])
        bias = jnp.where(ok, 0.0, NEG)
        lo = bias[:HALF]
        hi = bias[HALF:, KEYS // 2 :]
        b_lo[...] = jnp.concatenate([lo, lo], axis=0)
        b_hi[...] = jnp.concatenate([hi, hi], axis=0)

    def both(a, b):
        return jnp.concatenate([a, b], axis=0)

    low = lanes(HALF) < HEAD_DIM
    qx_lo, qx_hi = gathered(qxo_ref, qxs_ref, 0, 0), gathered(qxo_ref, qxs_ref, 1, 0)
    gx_lo, gx_hi = gathered(gxo_ref, gxs_ref, 0, 0), gathered(gxo_ref, gxs_ref, 1, 0)
    qx_all, gx_all = both(qx_lo, qx_hi), both(gx_lo, gx_hi)
    for sub in range(GROUP):
        at = 128 * sub
        pair = step * GROUP + sub
        q_lo, q_hi = gathered(qo_ref, qs_ref, 0, at), gathered(qo_ref, qs_ref, 1, at)
        g_lo, g_hi = gathered(go_ref, gs_ref, 0, at), gathered(go_ref, gs_ref, 1, at)
        terms = pick_extra(HALF, pair).astype(BF)

        def back(half, q, g, qx, gx, bias):
            k = jnp.concatenate([two_heads(k_ref[half, :, at : at + 128]), terms], axis=1)
            v = jnp.concatenate([two_heads(v_ref[half, :, at : at + 128]), terms], axis=1)
            p = jnp.exp(dot_t(k, jnp.concatenate([q, qx], axis=1)) + bias)
            dp = dot_t(v, jnp.concatenate([g, gx], axis=1))
            ds = (p * dp).astype(BF)
            gk = one_block(dot(ds, q)).astype(BF)
            gv = one_block(dot(p.astype(BF), g)).astype(BF)
            if sub == GROUP - 1:
                drop = (pair == PAIRS - 1) & ~low
                gk = jnp.where(drop, jnp.zeros_like(gk), gk)
                gv = jnp.where(drop, jnp.zeros_like(gv), gv)
            gk_ref[half, :, at : at + 128] = gk
            gv_ref[half, :, at : at + 128] = gv

        back(0, both(q_lo, q_hi), both(g_lo, g_hi), qx_all, gx_all, b_lo[...])
        back(1, q_hi, g_hi, qx_hi, gx_hi, b_hi[...])


def spec_rows(at, span=SPAN):
    return pl.BlockSpec((2 * HALF, span), lambda i: (0, at(i)))


def spec_all(at, span=SPAN):
    return pl.BlockSpec((4, 2, HALF, span), lambda i: (0, 0, 0, at(i)))


def spec_half(at):
    return pl.BlockSpec((2, HALF, SPAN), lambda i: (0, 0, at(i)))


def same(i):
    return i


def value_at(i):
    return i + PAIRS // GROUP


def last_at(i):
    return PAIRS - 1


def spec_whole(shape):
    return pl.BlockSpec(shape, lambda i: (0, 0))


MASK_SPECS = [
    spec_whole((2 * HALF, 1)),
    spec_whole((2 * HALF, 1)),
    spec_whole((1, KEYS)),
    spec_whole((1, KEYS)),
]
BIAS_SCRATCH = [
    pltpu.VMEM((2 * HALF, KEYS // 2), F32),
    pltpu.VMEM((2 * HALF, KEYS), F32),
]
BIAS_SCRATCH_T = [
    pltpu.VMEM((2 * HALF, KEYS), F32),
    pltpu.VMEM((2 * HALF, KEYS // 2), F32),
]
ATTENTION_COST = pl.CostEstimate(
    flops=8_000_000_000, bytes_accessed=6 << 20, transcendentals=PAIRS * 256 * KEYS
)
PARAMS = pltpu.CompilerParams(vmem_limit_bytes=16 * 1024 * 1024)
FLAT = jax.ShapeDtypeStruct((2 * HALF, WIDE), BF)


def attend_fwd(q, kv_own, kv_sib, where):
    return pl.pallas_call(
        fwd_kernel,
        grid=(PAIRS // GROUP,),
        out_shape=(FLAT, FLAT),
        in_specs=[spec_rows(same), spec_all(same), spec_all(same), spec_all(value_at)]
        + [spec_all(value_at)]
        + MASK_SPECS,
        out_specs=(spec_rows(same), spec_rows(same)),
        scratch_shapes=BIAS_SCRATCH + [pltpu.VMEM((2 * HALF, 128), F32)],
        compiler_params=PARAMS,
        cost_estimate=ATTENTION_COST,
    )(q, kv_own, kv_sib, kv_own, kv_sib, *where)


def attend_dq(qe, ge, kv_own, kv_sib, where):
    return pl.pallas_call(
        dq_kernel,
        grid=(PAIRS // GROUP,),
        out_shape=FLAT,
        in_specs=[spec_rows(same), spec_rows(same), spec_rows(last_at, 128), spec_rows(last_at, 128)]
        + [spec_all(same), spec_all(same), spec_all(value_at), spec_all(value_at)]
        + MASK_SPECS,
        out_specs=spec_rows(same),
        scratch_shapes=BIAS_SCRATCH,
        compiler_params=PARAMS,
        cost_estimate=ATTENTION_COST,
    )(qe, ge, qe, ge, kv_own, kv_sib, kv_own, kv_sib, *where)


def attend_dkv(kv, qe_own, qe_sib, ge_own, ge_sib, where):
    part = jax.ShapeDtypeStruct((2, HALF, WIDE), BF)
    return pl.pallas_call(
        dkv_kernel,
        grid=(PAIRS // GROUP,),
        out_shape=(part, part),
        in_specs=[spec_half(same), spec_half(value_at)]
        + [spec_all(same)] * 4
        + [spec_all(last_at, 128)] * 4
        + MASK_SPECS,
        out_specs=(spec_half(same), spec_half(same)),
        scratch_shapes=BIAS_SCRATCH_T,
        compiler_params=PARAMS,
        cost_estimate=ATTENTION_COST,
    )(kv, kv, qe_own, qe_sib, ge_own, ge_sib, qe_own, qe_sib, ge_own, ge_sib, *where)


FWD_PIECES = ((0, 1152), (1152, 2304), (2304, 3328), (3328, FF))
BACK_PIECES = ((0, FF // 2), (FF // 2, FF))
ROWS = 2 * HALF


def normalised(v):
    mean = jnp.mean(v, axis=1, keepdims=True)
    centred = v - mean
    inv = lax.rsqrt(jnp.mean(centred * centred, axis=1, keepdims=True) + 1e-05)
    return centred * inv, inv


def weight_copies(pieces, wout, wup, wdown, wout_here, wup_here, wdown_here, sems):
    out = pltpu.make_async_copy(wout, wout_here, sems.at[0])
    ups, downs = [], []
    for k, (a, b) in enumerate(pieces):
        ups.append(pltpu.make_async_copy(wup.at[:, a:b], wup_here.at[:, a:b], sems.at[1 + 2 * k]))
        downs.append(pltpu.make_async_copy(wdown.at[a:b, :], wdown_here.at[a:b, :], sems.at[2 + 2 * k]))
    return out, ups, downs


def mlp_fwd_kernel(
    ctx, hidden, gain, gain_next, a_o, b_o, a_u, b_d, b_u, a_d, wout, wup, wdown,
    middle, n2, low_o, low_u, low_d, after, n1_next, wout_here, wup_here, wdown_here, sems
):
    out, ups, downs = weight_copies(FWD_PIECES, wout, wup, wdown, wout_here, wup_here, wdown_here, sems)
    out.start()
    for up, down in zip(ups, downs):
        up.start()
        down.start()
    x = ctx[:, :D]
    low = dot(x, a_o[...]).astype(BF)
    low_o[...] = low
    out.wait()
    mid = hidden[...] + dot(x, wout_here[...]) + dot(low, b_o[...])
    middle[...] = mid
    normed = (normalised(mid)[0] * gain[...]).astype(BF)
    n2[...] = normed
    low = dot(normed, a_u[...]).astype(BF)
    low_u[...] = low
    total, total_low = jnp.zeros((ROWS, D), F32), jnp.zeros((ROWS, RANK), F32)
    for k, (a, b) in enumerate(FWD_PIECES):
        ups[k].wait()
        up = dot(normed, wup_here[:, a:b]) + dot(low, b_u[:, a:b])
        act = (up * (0.5 * (1.0 + lax.erf(up * 0.7071067811865476)))).astype(BF)
        downs[k].wait()
        total = total + dot(act, wdown_here[a:b, :])
        total_low = total_low + dot(act, a_d[a:b, :])
    low = total_low.astype(BF)
    low_d[...] = low
    new = middle[...] + (total + dot(low, b_d[...]))
    after[...] = new
    n1_next[...] = (normalised(new)[0] * gain_next[...]).astype(BF)


def mlp_back_kernel(
    g, ctx, middle, gain, n2, low_o, low_u, low_d, a_o, b_o, a_u, b_d, spread, b_u, a_d, wout, wup, wdown,
    gh2, ge, ga_o, gb_o, ga_u, gb_d, ga_d, gb_u, wout_here, wup_here, wdown_here, sems
):
    out, ups, downs = weight_copies(BACK_PIECES, wout, wup, wdown, wout_here, wup_here, wdown_here, sems)
    for up, down in zip(ups, downs):
        up.start()
        down.start()
    out.start()
    gy = g[...].astype(BF)
    glow_d = dot_t(gy, b_d[...]).astype(BF)
    gb_d[...] = t_dot(low_d[...], gy).astype(BF)
    normed, low = n2[...], low_u[...]
    gn2, glow_u = jnp.zeros((ROWS, D), F32), jnp.zeros((ROWS, RANK), F32)
    for k, (a, b) in enumerate(BACK_PIECES):
        ups[k].wait()
        up = dot(normed, wup_here[:, a:b]) + dot(low, b_u[:, a:b])
        phi = 0.5 * (1.0 + lax.erf(up * 0.7071067811865476))
        ga_d[:, a:b] = t_dot(glow_d, (up * phi).astype(BF)).astype(BF)
        downs[k].wait()
        gact = dot_t(gy, wdown_here[a:b, :]) + dot_t(glow_d, a_d[a:b, :])
        density = jnp.exp(-0.5 * up * up) * 0.3989422804014327
        gup = (gact * (phi + up * density)).astype(BF)
        gb_u[:, a:b] = t_dot(low, gup).astype(BF)
        gn2 = gn2 + dot_t(gup, wup_here[:, a:b])
        glow_u = glow_u + dot_t(gup, b_u[:, a:b])
    glow_u = glow_u.astype(BF)
    gn2 = gn2 + dot_t(glow_u, a_u[...])
    ga_u[...] = t_dot(glow_u, normed).astype(BF)
    out.wait()
    through_norm(g, middle[...], gain, gn2, ctx[:, :D], low_o[...], a_o, b_o, wout_here, spread, gh2, ge, ga_o, gb_o)


def through_norm(g, middle, gain, gn2, x, low_o, a_o, b_o, wout, spread, gh2, ge, ga_o, gb_o):
    r, inv = normalised(middle)
    gr = gn2 * gain[...]
    grad = g[...] + inv * (
        gr - jnp.mean(gr, axis=1, keepdims=True) - r * jnp.mean(gr * r, axis=1, keepdims=True)
    )
    gh2[...] = grad
    gproj = grad.astype(BF)
    glow_o = dot_t(gproj, b_o[...]).astype(BF)
    ga_o[...] = t_dot(glow_o, x).astype(BF)
    gb_o[...] = t_dot(low_o, gproj).astype(BF)
    gctx = (dot_t(gproj, wout[...]) + dot_t(glow_o, a_o[...])).astype(BF)
    product = gctx.astype(F32) * x.astype(F32)
    first = product.astype(BF)
    second = (product - first.astype(F32)).astype(BF)
    delta = dot(first, spread[...]) + dot(second, spread[...])
    ge[:, :D] = gctx
    ge[:, D:] = row_terms(-delta)[:, HEAD_DIM:]


def qkv_back_kernel(
    gq, gk, gv, low, n1, a, b_q, b_kv, hidden, gain, gh2, wq, wkv, g, ga, gb_q, gb_kv, wq_here, wkv_here, sems
):
    first = pltpu.make_async_copy(wq, wq_here, sems.at[0])
    second = pltpu.make_async_copy(wkv, wkv_here, sems.at[1])
    first.start()
    second.start()
    q, k, v = gq[...], gk[...].reshape(ROWS, WIDE), gv[...].reshape(ROWS, WIDE)
    glow = dot_t(q, b_q[...]) + dot_t(k, b_kv[:, :WIDE]) + dot_t(v, b_kv[:, WIDE:])
    glow = glow.astype(BF)
    ga[...] = t_dot(glow, n1[...]).astype(BF)
    gb_q[...] = t_dot(low[...], q).astype(BF)
    gb_kv[:, :WIDE] = t_dot(low[...], k).astype(BF)
    gb_kv[:, WIDE:] = t_dot(low[...], v).astype(BF)
    first.wait()
    gn1 = dot_t(q, wq_here[...])
    second.wait()
    gn1 = gn1 + dot_t(k, wkv_here[:, :WIDE]) + dot_t(v, wkv_here[:, WIDE:]) + dot_t(glow, a[...])
    r, inv = normalised(hidden[...])
    gr = gn1 * gain[...]
    g[...] = gh2[...] + inv * (
        gr - jnp.mean(gr, axis=1, keepdims=True) - r * jnp.mean(gr * r, axis=1, keepdims=True)
    )


def mlp_both_kernel(
    ctx, hidden, gain, g, a_o, b_o, a_u, b_d, spread, b_u, a_d, wout, wup, wdown,
    after, gh2, ge, ga_o, gb_o, ga_u, gb_d, ga_d, gb_u, wout_here, wup_here, wdown_here, sems
):
    out, ups, downs = weight_copies(BACK_PIECES, wout, wup, wdown, wout_here, wup_here, wdown_here, sems)
    out.start()
    for up, down in zip(ups, downs):
        up.start()
        down.start()
    x = ctx[:, :D]
    low_o = dot(x, a_o[...]).astype(BF)
    out.wait()
    gh2[...] = hidden[...] + dot(x, wout_here[...]) + dot(low_o, b_o[...])
    normed = (normalised(gh2[...])[0] * gain[...]).astype(BF)
    low = dot(normed, a_u[...]).astype(BF)
    gy = g[...].astype(BF)
    glow_d = dot_t(gy, b_d[...]).astype(BF)
    total, total_low = jnp.zeros((ROWS, D), F32), jnp.zeros((ROWS, RANK), F32)
    gn2, glow_u = jnp.zeros((ROWS, D), F32), jnp.zeros((ROWS, RANK), F32)
    for k, (a, b) in enumerate(BACK_PIECES):
        ups[k].wait()
        up = dot(normed, wup_here[:, a:b]) + dot(low, b_u[:, a:b])
        phi = 0.5 * (1.0 + lax.erf(up * 0.7071067811865476))
        act = (up * phi).astype(BF)
        ga_d[:, a:b] = t_dot(glow_d, act).astype(BF)
        downs[k].wait()
        total = total + dot(act, wdown_here[a:b, :])
        total_low = total_low + dot(act, a_d[a:b, :])
        gact = dot_t(gy, wdown_here[a:b, :]) + dot_t(glow_d, a_d[a:b, :])
        density = jnp.exp(-0.5 * up * up) * 0.3989422804014327
        gup = (gact * (phi + up * density)).astype(BF)
        gb_u[:, a:b] = t_dot(low, gup).astype(BF)
        gn2 = gn2 + dot_t(gup, wup_here[:, a:b])
        glow_u = glow_u + dot_t(gup, b_u[:, a:b])
    low_d = total_low.astype(BF)
    gb_d[...] = t_dot(low_d, gy).astype(BF)
    after[...] = (gh2[...] + (total + dot(low_d, b_d[...]))).astype(BF)
    glow_u = glow_u.astype(BF)
    gn2 = gn2 + dot_t(glow_u, a_u[...])
    ga_u[...] = t_dot(glow_u, normed).astype(BF)
    through_norm(g, gh2[...], gain, gn2, x, low_o, a_o, b_o, wout_here, spread, gh2, ge, ga_o, gb_o)


HERE = pl.BlockSpec(memory_space=pltpu.VMEM)
ANYWHERE = pl.BlockSpec(memory_space=pl.ANY)


def shape_of(rows, width, kind=BF):
    return jax.ShapeDtypeStruct((rows, width), kind)


def mlp_call(kernel, pieces, args, outs, flops):
    return pl.pallas_call(
        kernel,
        out_shape=outs,
        in_specs=[HERE] * (len(args) - 3) + [ANYWHERE] * 3,
        out_specs=(HERE,) * len(outs),
        scratch_shapes=[
            pltpu.VMEM((D, D), BF),
            pltpu.VMEM((D, FF), BF),
            pltpu.VMEM((FF, D), BF),
            pltpu.SemaphoreType.DMA((1 + 2 * len(pieces),)),
        ],
        compiler_params=pltpu.CompilerParams(vmem_limit_bytes=40 * 1024 * 1024),
        cost_estimate=pl.CostEstimate(flops=flops, bytes_accessed=24 << 20, transcendentals=ROWS * FF),
    )(*args)


def mlp_fwd(*args):
    outs = (shape_of(ROWS, D, F32), shape_of(ROWS, D)) + (shape_of(ROWS, RANK),) * 3
    outs += (shape_of(ROWS, D, F32), shape_of(ROWS, D))
    return mlp_call(mlp_fwd_kernel, FWD_PIECES, args, outs, 10_000_000_000)


def mlp_both(*args):
    outs = (shape_of(ROWS, D), shape_of(ROWS, D, F32), shape_of(ROWS, WIDE)) + (shape_of(RANK, D),) * 4
    outs += (shape_of(RANK, FF),) * 2
    return mlp_call(mlp_both_kernel, BACK_PIECES, args, outs, 18_000_000_000)


def qkv_back(*args):
    return pl.pallas_call(
        qkv_back_kernel,
        out_shape=(shape_of(ROWS, D, F32), shape_of(RANK, D), shape_of(RANK, WIDE), shape_of(RANK, 2 * WIDE)),
        in_specs=[HERE] * 11 + [ANYWHERE] * 2,
        out_specs=(HERE,) * 4,
        scratch_shapes=[
            pltpu.VMEM((D, WIDE), BF),
            pltpu.VMEM((D, 2 * WIDE), BF),
            pltpu.SemaphoreType.DMA((2,)),
        ],
        compiler_params=pltpu.CompilerParams(vmem_limit_bytes=20 * 1024 * 1024),
        cost_estimate=pl.CostEstimate(flops=5_000_000_000, bytes_accessed=10 << 20, transcendentals=0),
    )(*args)


def mlp_back(*args):
    outs = (shape_of(ROWS, D, F32), shape_of(ROWS, WIDE)) + (shape_of(RANK, D),) * 4
    outs += (shape_of(RANK, FF),) * 2
    return mlp_call(mlp_back_kernel, BACK_PIECES, args, outs, 16_000_000_000)


def ring_start(block):
    return lax.ppermute(block, "seq", UP), lax.ppermute(block, "seq", DOWN)


def ring_far(block, before, after):
    far_lo = lax.ppermute(before[0], "seq", UP)
    far_hi = lax.ppermute(after[1], "seq", DOWN)
    return jnp.stack([block, before, after, jnp.stack([far_lo, far_hi])])


def other_core(own):
    return lax.ppermute(own, "seq", CORE)


def sum_sequence(parts, core, y):
    parts = parts.reshape((4, 2) + parts.shape[1:])
    mine = lax.dynamic_index_in_dim(parts, core, 1, keepdims=False)
    other = lax.dynamic_index_in_dim(parts, 1 - core, 1, keepdims=False)
    half = mine.astype(F32) + lax.ppermute(other, "seq", CORE).astype(F32)

    def of(step):
        return lax.dynamic_index_in_dim(half, (y + step) % 4, 0, keepdims=False)

    total = of(0)
    for step, route in ((1, UP), (3, DOWN), (2, FAR)):
        total = total + lax.ppermute(of(step).astype(BF), "seq", route).astype(F32)
    return total


def tie(*values):
    return lax.optimization_barrier(values)


def eighths(turned, straight):
    def cut(a, part):
        return jnp.pad(a, ((0, 0), (0, 8 * part - a.shape[1]))).reshape(RANK, 8, part)

    first = cut(jnp.concatenate(turned, axis=1), PART_A)
    return jnp.swapaxes(jnp.concatenate([first, cut(straight, PART_B)], axis=2), 0, 1)


def by_adapter_kernel(picks, *refs):
    parts, out_ref, acc = refs[:-2], refs[-2], refs[-1]
    acc[...] = jnp.zeros_like(acc)
    at = 0
    for ref in parts:
        for k in range(ref.shape[0]):
            rows = pl.ds(pl.multiple_of(picks[at] * RANK, RANK), RANK)
            acc[rows, :] = acc[rows, :] + ref[k].astype(F32)
            at += 1
    for j in range(PART // 128):
        square = acc[:, 128 * j : 128 * (j + 1)]
        square = square.T if 128 * j < PART_A else square
        out_ref[128 * j : 128 * (j + 1), :] = square.astype(BF)


def by_adapter(parts, picks):
    return pl.pallas_call(
        by_adapter_kernel,
        out_shape=jax.ShapeDtypeStruct((PART, 128), BF),
        in_specs=[pl.BlockSpec(memory_space=pltpu.SMEM)]
        + [pl.BlockSpec(memory_space=pltpu.VMEM)] * len(parts),
        out_specs=pl.BlockSpec(memory_space=pltpu.VMEM),
        scratch_shapes=[pltpu.VMEM((8 * RANK, PART), F32)],
        compiler_params=PARAMS,
        cost_estimate=pl.CostEstimate(flops=16 * RANK * PART, bytes_accessed=2 << 20, transcendentals=0),
    )(picks, *parts)


def unfold_kernel(place, own_ref, sib_ref, one_ref, *outs):
    turned, straight = outs[:-1], outs[-1]

    def rows(layer, e, at, n):
        if layer == 1:
            return one_ref[e, at : at + n, :].astype(F32)
        k = place[e]
        mine = own_ref[k % 4, at : at + n, :]
        other = sib_ref[k % 4, at : at + n, :]
        return jnp.where(k < 4, mine.astype(F32), other.astype(F32))

    for layer in range(2):
        start = 0
        for out, width in zip(turned, TURNED):
            at = start
            while at < start + width:
                n = min(start + width, (at // PART_A + 1) * PART_A) - at
                out[layer, at - start : at - start + n, :] = rows(layer, at // PART_A, at % PART_A, n)
                at += n
            start += width
        squares = PART_B // 128
        for t in range(FF // 128):
            value = rows(layer, t // squares, PART_A + 128 * (t % squares), 128)
            straight[layer, :, 128 * t : 128 * (t + 1)] = value


def unfold(own, sib, one, place):
    shapes = [(2, w, 128) for w in TURNED] + [(2, 128, FF)]
    whole = pl.BlockSpec(memory_space=pltpu.VMEM)
    return pl.pallas_call(
        unfold_kernel,
        out_shape=tuple(jax.ShapeDtypeStruct(shape, F32) for shape in shapes),
        in_specs=[pl.BlockSpec(memory_space=pltpu.SMEM), whole, whole, whole],
        out_specs=(whole,) * 8,
        compiler_params=pltpu.CompilerParams(vmem_limit_bytes=32 * 1024 * 1024),
        cost_estimate=pl.CostEstimate(flops=0, bytes_accessed=28 << 20, transcendentals=0),
    )(place, own, sib, one)


def share(w_qkv, w_out, w_up, w_down, z_lo):
    def half_row(w, front, lines):
        size = lines * 128 - w.shape[1]
        first = jnp.pad(w, ((0, 0), (0, size)))
        second = jnp.pad(w, ((0, 0), (front, size - front)))
        return jnp.where(z_lo == 0, first, second).reshape(-1, lines, 128)

    def put(a, room):
        return jnp.pad(a, ((0, 0), (0, room - a.shape[1]), (0, 0)))

    attention = [
        put(half_row(w_qkv, 32, N_QKV), AT_OUT),
        put(half_row(w_out, 32, N_OUT), LINES - AT_OUT),
    ]
    up, down = put(w_up.reshape(-1, N_UP, 128), LINES), put(w_down.reshape(-1, N_DOWN, 128), LINES)
    return jnp.concatenate(attention, axis=1), jnp.concatenate([up, down], axis=1)


def spin(a):
    return pltpu.roll(a, HEAD_DIM, 1)


def fill(ref, base, lines):
    ref[pl.ds(base, lines.shape[0], stride=2), :] = lines


def between(ref, base, n):
    now, later = ref[pl.ds(base, n, stride=2), :], ref[pl.ds(base + 2, n, stride=2), :]
    ref[pl.ds(base + 1, n, stride=2), :] = spin(jnp.where(lanes(n) < HEAD_DIM, later, now))


def columns(ref, dst, to, start, units, step=2):
    got = ref[pl.ds(start, dst.shape[0], stride=units), :].astype(BF)
    n = min(128, dst.shape[1] - to)
    dst[:, to : to + n] = got[:, :n]


def lines_of(ref, pair, zl, start, n):
    return ref[0, zl, 0, pair % 4, pair // 4, start : start + n, :].astype(F32)


def unpack_attention_kernel(g_ref, *refs):
    def lines(pair, zl):
        return lines_of(g_ref, pair, zl, 0, N_QKV), lines_of(g_ref, pair, zl, AT_OUT, N_OUT)

    unpack_attention_lines(lines, *refs)


def unpack_first_kernel(steps, own_1, sib_1, own_2, sib_2, *refs):
    def lines(pair, zl):
        x, core = pair % 4, pair // 4
        z_at, x_at = steps[4 + 2 * (pl.program_id(0) // 4) + zl], steps[8 + x]
        mine = steps[12] == core
        top = jnp.where(mine, own_1[z_at, 0, x_at], sib_1[z_at, 0, x_at])
        bottom = jnp.where(mine, own_2[0, z_at, x_at], sib_2[0, z_at, x_at])
        both = jnp.concatenate([top.astype(F32), bottom.astype(F32)], axis=0)
        return both[:N_QKV], both[AT_OUT : AT_OUT + N_OUT]

    unpack_attention_lines(lines, *refs)


def unpack_attention_lines(lines, q_ref, kv_ref, out_ref, s_qkv, s_out):
    low = lanes(1) < HEAD_DIM
    zero = jnp.zeros((1, 128), F32)
    for pair in range(8):
        (qkv0, out0), (qkv1, out1) = lines(pair, 0), lines(pair, 1)
        base, base_out = pair * 867, pair * 289
        fill(s_qkv, base, qkv0)
        fill(s_qkv, base + 433, qkv1)
        between(s_qkv, base, N_QKV - 1)
        between(s_qkv, base + 433, N_QKV)
        s_qkv[pl.ds(base + 432, 1), :] = qkv0[N_QKV - 1 :] + spin(jnp.where(low, qkv1[:1], zero))
        s_qkv[pl.ds(base + 433, 1), :] = qkv1[:1] + spin(jnp.where(low, zero, qkv0[N_QKV - 1 :]))
        fill(s_out, base_out, out0)
        fill(s_out, base_out + 144, out1)
        s_out[pl.ds(base_out + 144, 1), :] = out0[N_OUT - 1 :] + out1[:1]
        between(s_out, base_out, N_OUT - 1)
        between(s_out, base_out + 144, N_OUT - 1)
    half = lanes(BLOCK) < HEAD_DIM
    for dst, to, first in ((q_ref, 0, 0), (kv_ref, 0, 17), (kv_ref, WIDE, 34)):
        for j in range(8):
            columns(s_qkv, dst, to + 128 * j, first + 2 * j, 51)
        got = s_qkv[pl.ds(first + 16, BLOCK, stride=51), :]
        dst[:, to + D - HEAD_DIM : to + WIDE] = jnp.where(half, got, 0.0).astype(BF)
    for j in range(9):
        columns(s_out, out_ref, 128 * j, 2 * j, 17)


def unpack_mlp_kernel(g_up, g_down, up_ref, down_ref, s_up, s_down):
    for pair in range(8):
        for zl in range(2):
            at = pair * 2 + zl
            s_up[pl.ds(at * N_UP, N_UP), :] = lines_of(g_up, pair, zl, 0, N_UP)
            fill(s_down, at * 2 * N_DOWN, lines_of(g_down, pair, zl, 0, N_DOWN))
    for at in range(16):
        between(s_down, at * 2 * N_DOWN, N_DOWN)
    for j in range(34):
        columns(s_up, up_ref, 128 * j, j, 34)
    for j in range(9):
        columns(s_down, down_ref, 128 * j, 2 * j, 17)


def unpack(kernel, got, at, outs, scratch_lines):
    g = got.reshape(2, 2, 4, 4, 2, -1, 128)

    def spec(k):
        return pl.BlockSpec((1, 2, 1, 4, 2, LINES, 128), lambda i: (i // 4, 0, i % 4, 0, 0, k, 0))

    return pl.pallas_call(
        kernel,
        grid=(8,),
        out_shape=tuple(jax.ShapeDtypeStruct((8 * r, w), BF) for r, w in outs),
        in_specs=[spec(k) for k in at],
        out_specs=tuple(pl.BlockSpec((r, w), lambda i: (i, 0)) for r, w in outs),
        scratch_shapes=[pltpu.VMEM((n, 128), F32) for n in scratch_lines],
        compiler_params=pltpu.CompilerParams(vmem_limit_bytes=26 * 1024 * 1024),
        cost_estimate=pl.CostEstimate(
            flops=0, bytes_accessed=len(at) * (20 << 20), transcendentals=0
        ),
    )(*[g] * len(at))


ATTENTION_OUTS = [(BLOCK, WIDE), (BLOCK, 2 * WIDE), (BLOCK, D)]
ATTENTION_LINES = [8 * 867 + 8, 8 * 289 + 8]


def unpack_attention(got, at):
    return unpack(unpack_attention_kernel, got, [at], ATTENTION_OUTS, ATTENTION_LINES)


def along(axis, block, near):
    name, shift = SHIFTS[axis]
    before = lax.ppermute(block, name, shift(1))
    after = lax.ppermute(block, name, shift(-1))
    if near:
        far = lax.ppermute(block, name, shift(2))
    else:
        n = block.shape[0] // 2
        far = [lax.ppermute(before[:n], name, shift(1)), lax.ppermute(after[n:], name, shift(-1))]
        far = jnp.concatenate(far)
    return jnp.stack([block, before, after, far])


def unpack_first(share, steps):
    n = LINES // 2
    row = along("x", share, True)
    one, two = along("y", row[:, :n], True), along("z", row[:, n:], True)
    one, two = tie(one, two)
    one, two = along("z", one, False), along("y", two, False)
    spec_one = pl.BlockSpec((4, 1, 4, n, 128), lambda i, steps: (0, steps[i % 4], 0, 0, 0))
    spec_two = pl.BlockSpec((1, 4, 4, n, 128), lambda i, steps: (steps[i % 4], 0, 0, 0, 0))
    return pl.pallas_call(
        unpack_first_kernel,
        grid_spec=pltpu.PrefetchScalarGridSpec(
            num_scalar_prefetch=1,
            grid=(8,),
            in_specs=[spec_one, spec_one, spec_two, spec_two],
            out_specs=tuple(pl.BlockSpec((r, w), lambda i, steps: (i, 0)) for r, w in ATTENTION_OUTS),
            scratch_shapes=[pltpu.VMEM((n, 128), F32) for n in ATTENTION_LINES],
        ),
        out_shape=tuple(jax.ShapeDtypeStruct((8 * r, w), BF) for r, w in ATTENTION_OUTS),
        compiler_params=pltpu.CompilerParams(vmem_limit_bytes=26 * 1024 * 1024),
        cost_estimate=pl.CostEstimate(flops=0, bytes_accessed=30 << 20, transcendentals=0),
    )(steps, one, other_core(one), two, other_core(two))


def unpack_mlp(got, at):
    outs = [(BLOCK, FF), (4 * BLOCK, D)]
    return unpack(unpack_mlp_kernel, got, [at, at + 1], outs, [16 * N_UP, 32 * N_DOWN + 8])


def shards(
    tokens, segments, adapter_pick, norm_gain, w_qkv, w_out, w_up, w_down,
    a_qkv, b_qkv, a_out, b_out, a_up, b_up, a_down, b_down, grad_out
):
    layers = norm_gain.shape[0]
    index = lax.axis_index("seq")
    z_hi, place = index // 8, index % 8
    core, y = place % 2, place // 2

    def halves(own, other):
        return jnp.where(z_hi == 0, jnp.stack([own, other]), jnp.stack([other, own]))

    def mine(a):
        return lax.dynamic_index_in_dim(a, z_hi, 0, keepdims=False)

    def theirs(a):
        return lax.dynamic_index_in_dim(a, 1 - z_hi, 0, keepdims=False)

    attention, mlp = share(w_qkv, w_out, w_up, w_down, lax.axis_index("batch") % 2)

    def gather(a):
        return lax.all_gather(a, BOTH, axis=0, tiled=True, axis_index_groups=ALL)

    batch = lax.axis_index("batch")
    spare = jnp.concatenate([segments.reshape(1, 128), jnp.pad(adapter_pick[None], ((0, 0), (0, 126)))])
    early = lax.dynamic_update_slice(mlp[0], spare.astype(BF), (N_UP, 0))
    early = gather(jnp.concatenate([early, attention[1]], axis=0))
    spare = early.reshape(2, 2, 4, 4, 2, -1, 128)[..., N_UP : N_UP + 2, :].astype(jnp.int32)
    z_lo, x = batch % 2, batch // 2
    seg = lax.dynamic_slice(spare, (0, z_lo, 0, x, 0, 0, 0), (2, 1, 4, 1, 2, 1, 128))
    seg = mine(jnp.swapaxes(seg.reshape(16, 2, HALF), 0, 1)).reshape(2, 8, HALF)
    picks = jnp.swapaxes(spare[0, :, 0, :, 0, 1, :2], 0, 1).reshape(16)
    late = gather(mlp[1])

    sent = lax.ppermute(jnp.stack([theirs(tokens), theirs(grad_out)]), "seq", SWAP)
    hidden = halves(mine(tokens), sent[0]).reshape(2 * HALF, D).astype(F32)
    grad_hidden = halves(mine(grad_out), sent[1]).reshape(2 * HALF, D).astype(F32)
    pick = mine(adapter_pick)

    offset = jnp.arange(HALF, dtype=jnp.int32)
    start = jnp.array([0, KEYS // 2], jnp.int32)[:, None]
    lpos = (start + place * HALF + offset[None]).reshape(2 * HALF, 1)
    lseg = lax.dynamic_index_in_dim(seg, place, 1, keepdims=False).reshape(2 * HALF, 1)
    ys = (y + jnp.array([0, 3, 1, 2], jnp.int32)) % 4
    order = jnp.concatenate([2 * ys + core, 2 * ys + 1 - core])
    kpos = (start[:, :, None] + (order * HALF)[None, :, None] + offset).reshape(1, KEYS)
    kseg = jnp.take(seg, order, axis=1).reshape(1, KEYS)
    where = (lpos, lseg, kpos, kseg)

    steps = jnp.array([0, 3, 1, 2], jnp.int32)
    z = z_hi * 2 + z_lo

    def sequence(zs, xs):
        return 2 * (2 * xs + zs % 2) + zs // 2

    four = jnp.arange(4, dtype=jnp.int32)
    picks_in_order = jnp.take(picks, sequence(four[:, None], four[None, :]).reshape(16))
    zs, xs = (z + steps) % 4, (x + steps) % 4
    picks_by_step = jnp.take(picks, sequence(zs[None, :], xs[:, None]).reshape(16))
    eight = jnp.arange(8, dtype=jnp.int32)
    back = jnp.array([0, 2, 3, 1], jnp.int32)
    place_by_step = 4 * ((eight % 2) ^ core) + jnp.take(back, (eight // 2 - y) % 4)
    arrival = [jnp.take(back, (four - at) % 4) for at in (y, z, x)]
    arrival = jnp.concatenate(arrival + [core[None]]).astype(jnp.int32)

    def low_in(a, l):
        return lax.dynamic_slice_in_dim(a[l], pick * RANK, RANK, 1)

    def low_out(b, l):
        return lax.dynamic_slice_in_dim(b[l], pick * RANK, RANK, 0)

    heads_of = (jnp.arange(D, dtype=jnp.int32) // HEAD_DIM)[:, None]
    spread = (heads_of == (jnp.arange(128, dtype=jnp.int32)[None, :] - HEAD_DIM) // 3).astype(BF)

    saved, queries = [], []
    n1 = (norm_stats(hidden)[0] * norm_gain[0, 0]).astype(BF)
    first = unpack_first(attention[0], arrival)
    for l in range(layers):
        a_first = low_in(a_qkv, l)
        b_first = low_out(b_qkv, l)
        b_q = widen(b_first[:, :D])
        b_kv = jnp.concatenate([widen(b_first[:, D : 2 * D]), widen(b_first[:, 2 * D :])], axis=1)
        ad = [(low_in(a, l), low_out(b, l)) for a, b in ((a_out, b_out), (a_up, b_up), (a_down, b_down))]
        wq, wkv, wout = first
        low_qkv = dot(n1, a_first).astype(BF)
        kv = (dot(n1, wkv) + dot(low_qkv, b_kv)).astype(BF).reshape(2, HALF, 2 * WIDE)
        q = (dot(n1, wq) + dot(low_qkv, b_q)).astype(BF) * jnp.asarray(0.125, BF)
        if l > 0:
            late, kv = tie(late, kv)
        before, after = ring_start(kv)
        wup, wdown = unpack_mlp(early, 0) if l == 0 else unpack_mlp(late, 0)
        if l == 0:
            before, after, q, wup, wdown = tie(before, after, q, wup, wdown)
        else:
            before, after, q, wup, wdown, qe_own = tie(before, after, q, wup, wdown, qe_own)
            queries.append((qe_own, other_core(qe_own)))
        kv_own = ring_far(kv, before, after)
        if l == 0:
            first = unpack_attention(early, 2)
            kv_own, *first = tie(kv_own, *first)
        kv_sib = other_core(kv_own)
        ctx, qe = attend_fwd(q, kv_own, kv_sib, where)
        qe = qe.reshape(2, HALF, WIDE)
        q_before, q_after = ring_start(qe)
        gains = norm_gain[l, 1][None], norm_gain[(l + 1) % layers, 0][None]
        (a_o, b_o), (a_u, b_u), (a_d, b_d) = ad
        small, large = (a_o, b_o, a_u, b_d), (b_u, a_d, wout, wup, wdown)
        rows, hidden_next, n1_next = None, None, None
        if l < layers - 1:
            middle, n2, low_o, low_u, low_d, hidden_next, n1_next = mlp_fwd(ctx, hidden, *gains, *small, *large)
            q_before, q_after, hidden_next, n1_next = tie(q_before, q_after, hidden_next, n1_next)
            rows = (ctx, middle, gains[0], n2, low_o, low_u, low_d)
        else:
            result, *back = mlp_both(ctx, hidden, gains[0], grad_hidden, *small, spread, *large)
            q_before, q_after, *back = tie(q_before, q_after, *back)
        qe_own = ring_far(qe, q_before, q_after)
        saved.append(
            (hidden, n1, low_qkv, kv, kv_own, kv_sib, qe.reshape(2 * HALF, WIDE))
            + (rows, small, large, a_first, b_q, b_kv, wq, wkv)
        )
        hidden, n1 = hidden_next, n1_next

    behind = None
    for l in reversed(range(layers)):
        hidden_in, n1, low_qkv, kv, kv_own, kv_sib, qe, rows, small, large, a_first, b_q, b_kv, wq, wkv = saved[l]
        if l < layers - 1:
            back = mlp_back(g, *rows, *small, spread, *large)
        gh2, ge, ga_o, gb_o, ga_u, gb_d, ga_d, gb_u = back
        if l == layers - 1:
            qe_own, ge = tie(qe_own, ge)
            qe_sib = other_core(qe_own)
        else:
            qe_own, qe_sib = queries[l]
        g_block = ge.reshape(2, HALF, WIDE)
        g_before, g_after = ring_start(g_block)
        if behind is not None:
            behind, ge = tie(behind, ge)
            behind = lax.all_gather(behind, BOTH, axis=0, axis_index_groups=SAME_PLACE)
        gq = attend_dq(qe, ge, kv_own, kv_sib, where)
        g_before, g_after, gq = tie(g_before, g_after, gq)
        ge_own = ring_far(g_block, g_before, g_after)
        ge_sib = other_core(ge_own)
        gk, gv = attend_dkv(kv, qe_own, qe_sib, ge_own, ge_sib, where)
        g, ga_q, gb_q, gb_kv = qkv_back(
            gq, gk, gv, low_qkv, n1, a_first, b_q, b_kv, hidden_in, norm_gain[l, 0][None], gh2, wq, wkv
        )
        gb_q = [gb_q[:, :D], gb_kv[:, :D], gb_kv[:, WIDE : WIDE + D]]
        parts = eighths([ga_q, ga_o, ga_u, ga_d] + gb_q + [gb_o, gb_d], gb_u)
        if l > 0:
            parts, g = tie(parts, g)
            behind = sum_sequence(parts, core, y)

    got = lax.all_to_all(parts, BOTH, 0, 0, axis_index_groups=SAME_SEQUENCE)
    behind, got = tie(behind, got)
    one = by_adapter([behind], picks_in_order)
    one = lax.all_gather(one, BOTH, axis=0, axis_index_groups=SAME_SEQUENCE)
    part = jnp.sum(got.astype(F32), axis=0).astype(BF)
    along_z = [lax.ppermute(part, BOTH, z_shift(by)) for by in (1, -1, 2)]
    along_z = jnp.stack([part] + along_z)
    before = lax.ppermute(along_z, "batch", x_shift(1))
    after = lax.ppermute(along_z, "batch", x_shift(-1))
    sent_home = theirs(g.reshape(2, HALF, D)), theirs(result.reshape(2, HALF, D))
    back_home = [lax.ppermute(a, "seq", SWAP) for a in sent_home]
    before, after, *back_home = tie(before, after, *back_home)
    far = [lax.ppermute(before[:2], "batch", x_shift(1)), lax.ppermute(after[2:], "batch", x_shift(-1))]
    whole = by_adapter([along_z, before, after] + far, picks_by_step)
    whole = whole.reshape(2, -1, 128)
    own = ring_far(whole, *ring_start(whole))
    sib = other_core(own).reshape(4, PART, 128)
    ga_q, ga_o, ga_u, ga_d, gb_q, gb_o, gb_d, gb_u = unfold(
        own.reshape(4, PART, 128), sib, one, place_by_step
    )
    gb_q, gb_o, gb_d = (jnp.swapaxes(a, 1, 2) for a in (gb_q, gb_o, gb_d))
    grad_tokens = halves(mine(g.reshape(2, HALF, D)), back_home[0])
    result = halves(mine(result.reshape(2, HALF, D)), back_home[1])

    return result, grad_tokens, ga_q, gb_q, ga_o, gb_o, ga_u, gb_u, ga_d, gb_d


def solution(mesh):
    rows, flat, whole = P("batch", "seq", None), P(None, ("seq", "batch")), P()
    in_specs = (rows, P("batch", "seq"), P("batch"), whole) + (flat,) * 4 + (whole,) * 8 + (rows,)
    out_specs = (rows, rows) + (whole,) * 8
    return jax.shard_map(shards, mesh=mesh, in_specs=in_specs, out_specs=out_specs, check_vma=False)
```

```python
import jax
import jax.numpy as jnp
from jax import lax
from jax.experimental import pallas as pl
from jax.experimental.pallas import tpu as pltpu
from jax.sharding import PartitionSpec as P

D = 1088
HEADS = 17
HEAD_DIM = 64
FF = 4352
RANK = 16
WIDE = 1152
PAIRS = 9
HALF = 64
KEYS = 1024
BF = jnp.bfloat16
F32 = jnp.float32
NEG = -1e30

SWAP = [(i, i ^ 8) for i in range(16)]
CORE = [(i, i ^ 1) for i in range(16)]
UP = [(i, (i & 8) | ((i + 2) & 7)) for i in range(16)]
DOWN = [(i, (i & 8) | ((i - 2) & 7)) for i in range(16)]
FAR = [(i, (i & 8) | ((i + 4) & 7)) for i in range(16)]
def at_chip(z, y, x, core):
    return ((z // 2 * 4 + y) * 2 + core) * 8 + x * 2 + z % 2


ALL = [[at_chip(z, y, x, c) for z in range(4) for y in range(4) for x in range(4) for c in range(2)]]
SAME_SEQUENCE = [[at_chip(z, y, x, c) for y in range(4) for c in range(2)] for z in range(4) for x in range(4)]
SAME_PLACE = [[at_chip(z, y, x, c) for z in range(4) for x in range(4)] for y in range(4) for c in range(2)]


def z_shift(by):
    return [
        (at_chip(z, y, x, c), at_chip((z + by) % 4, y, x, c))
        for z in range(4) for y in range(4) for x in range(4) for c in range(2)
    ]


def x_shift(by):
    return [(i, (i + 2 * by) % 8) for i in range(8)]


def y_shift(by):
    return [(i, (i & 8) | ((i + 2 * by) & 7)) for i in range(16)]


BOTH = ("seq", "batch")
SHIFTS = {"x": ("batch", x_shift), "y": ("seq", y_shift), "z": (BOTH, z_shift)}
TURNED = (D, D, D, FF, 3 * D, D, D)
PART_A, PART_B = 1664, 640
PART = PART_A + PART_B

LINES = 304
AT_OUT = 224
N_QKV, N_OUT, N_UP, N_DOWN = 217, 73, 289, 289
BLOCK = 136


def dot(a, b):
    return jnp.dot(a, b, preferred_element_type=F32)


def dot_t(a, b):
    return lax.dot_general(a, b, (((1,), (1,)), ((), ())), preferred_element_type=F32)


def t_dot(a, b):
    return lax.dot_general(a, b, (((0,), (0,)), ((), ())), preferred_element_type=F32)


def norm_stats(v):
    mean = jnp.mean(v, axis=-1, keepdims=True)
    centred = v - mean
    inv = lax.rsqrt(jnp.mean(centred * centred, axis=-1, keepdims=True) + 1e-05)
    return centred * inv, inv


def norm_back(v, gain, grad):
    r, inv = norm_stats(v)
    gr = grad * gain
    return inv * (
        gr - jnp.mean(gr, axis=-1, keepdims=True) - r * jnp.mean(gr * r, axis=-1, keepdims=True)
    )


def widen(a):
    return jnp.pad(a, ((0, 0), (0, WIDE - D)))


def lanes(rows):
    return lax.broadcasted_iota(jnp.int32, (rows, 128), 1)


def two_heads(block, single):
    low = lanes(block.shape[0]) < HEAD_DIM
    zero = jnp.zeros_like(block)
    first = jnp.where(low, block, zero)
    return first if single else jnp.concatenate([first, jnp.where(low, zero, block)], axis=0)


def one_block(stacked, single):
    rows = stacked.shape[0] if single else stacked.shape[0] // 2
    second = jnp.zeros_like(stacked) if single else stacked[rows:]
    return jnp.where(lanes(rows) < HEAD_DIM, stacked[:rows], second)


def pick_extra(rows, pair, single):
    spot = lanes(rows) - HEAD_DIM

    def of(h):
        return ((spot >= 3 * h) & (spot < 3 * h + 3)).astype(F32)

    head = 2 * pair
    return (of(head) if single else jnp.concatenate([of(head), of(head + 1)], axis=0)).astype(BF)


def heads_of_pair(pair):
    return 128 * pair, pair == PAIRS - 1


def gathered(own_ref, sib_ref, half, at):
    return jnp.concatenate(
        [ref[:, half, :, at : at + 128].reshape(4 * HALF, 128) for ref in (own_ref, sib_ref)], axis=0
    )


def row_terms(term):
    first = term.astype(BF).astype(F32)
    rest = term - first
    second = rest.astype(BF).astype(F32)
    third = rest - second
    turn = (lanes(term.shape[0]) - HEAD_DIM) % 3
    return jnp.where(turn == 0, first, jnp.where(turn == 1, second, third)).astype(BF)


def both(a, b):
    return jnp.concatenate([a, b], axis=0)


def fwd_kernel(q_ref, kv_own, kv_sib, lpos, lseg, kpos, kseg, ctx_ref, qe_ref):
    ok = (kpos[...] <= lpos[...]) & (kseg[...] == lseg[...])
    bias = jnp.where(ok, 0.0, NEG)
    bias = (both(bias[:HALF, : KEYS // 2], bias[:HALF, : KEYS // 2]), both(bias[HALF:], bias[HALF:]))
    spot = lanes(HALF) - HEAD_DIM
    terms = [jnp.zeros((HALF, 128), F32)] * 2
    for pair in range(PAIRS):
        at, single = heads_of_pair(pair)
        k_lo, k_hi = gathered(kv_own, kv_sib, 0, at), gathered(kv_own, kv_sib, 1, at)
        v_lo, v_hi = gathered(kv_own, kv_sib, 0, WIDE + at), gathered(kv_own, kv_sib, 1, WIDE + at)
        for half, keys, values in ((0, k_lo, v_lo), (1, both(k_lo, k_hi), both(v_lo, v_hi))):
            rows = two_heads(q_ref[half * HALF : (half + 1) * HALF, at : at + 128], single)
            s = dot_t(rows, keys) + bias[half][: rows.shape[0]]
            top = jnp.max(s, axis=1, keepdims=True)
            e = jnp.exp(s - top)
            total = jnp.sum(e, axis=1, keepdims=True)
            out = one_block(dot(e.astype(BF), values) * (1.0 / total), single)
            ctx_ref[half * HALF : (half + 1) * HALF, at : at + 128] = out.astype(BF)
            lse = top + jnp.log(total)
            for n in range(rows.shape[0] // HALF):
                head = 2 * pair + n
                mine = (spot >= 3 * head) & (spot < 3 * head + 3)
                terms[half] = jnp.where(mine, -lse[n * HALF : (n + 1) * HALF], terms[half])
    qe_ref[...] = q_ref[...]
    last = q_ref[:, WIDE - 128 :]
    qe_ref[:, WIDE - 128 :] = jnp.where(lanes(2 * HALF) < HEAD_DIM, last, row_terms(both(*terms)))


def dq_kernel(qe_ref, ge_ref, kv_own, kv_sib, lpos, lseg, kpos, kseg, gq_ref):
    ok = (kpos[...] <= lpos[...]) & (kseg[...] == lseg[...])
    bias = jnp.where(ok, 0.0, NEG)
    bias = (both(bias[:HALF, : KEYS // 2], bias[:HALF, : KEYS // 2]), both(bias[HALF:], bias[HALF:]))
    for pair in range(PAIRS):
        at, single = heads_of_pair(pair)
        k_lo, k_hi = gathered(kv_own, kv_sib, 0, at), gathered(kv_own, kv_sib, 1, at)
        v_lo, v_hi = gathered(kv_own, kv_sib, 0, WIDE + at), gathered(kv_own, kv_sib, 1, WIDE + at)
        mask = pick_extra(HALF, pair, single)
        for half, keys, values in ((0, k_lo, v_lo), (1, both(k_lo, k_hi), both(v_lo, v_hi))):
            place = slice(half * HALF, (half + 1) * HALF)
            ones = jnp.ones((keys.shape[0], 128), BF)

            def with_terms(ref):
                rows, extra = two_heads(ref[place, at : at + 128], single), ref[place, WIDE - 128 :]
                extra = extra if single else both(extra, extra)
                return jnp.concatenate([rows, extra * mask], axis=1)

            s = dot_t(with_terms(qe_ref), jnp.concatenate([keys, ones], axis=1))
            dp = dot_t(with_terms(ge_ref), jnp.concatenate([values, ones], axis=1))
            ds = (jnp.exp(s + bias[half][: s.shape[0]]) * dp).astype(BF)
            gq_ref[place, at : at + 128] = (one_block(dot(ds, keys), single) * 0.125).astype(BF)


def dkv_kernel(kv, q_own, q_sib, g_own, g_sib, lpos, lseg, kpos, kseg, gk_ref, gv_ref):
    ok = (lpos[...] <= kpos[...]) & (kseg[...] == lseg[...])
    bias = jnp.where(ok, 0.0, NEG)
    bias = (both(bias[:HALF], bias[:HALF]), both(bias[HALF:, KEYS // 2 :], bias[HALF:, KEYS // 2 :]))

    def queries(own, sib, at):
        lo, hi = gathered(own, sib, 0, at), gathered(own, sib, 1, at)
        return both(lo, hi), hi

    qx, gx = queries(q_own, q_sib, WIDE - 128), queries(g_own, g_sib, WIDE - 128)
    for pair in range(PAIRS):
        at, single = heads_of_pair(pair)
        q, g = queries(q_own, q_sib, at), queries(g_own, g_sib, at)
        terms = pick_extra(HALF, pair, single)
        for half in range(2):
            k = jnp.concatenate([two_heads(kv[half, :, at : at + 128], single), terms], axis=1)
            v = two_heads(kv[half, :, WIDE + at : WIDE + at + 128], single)
            v = jnp.concatenate([v, terms], axis=1)
            s = dot_t(k, jnp.concatenate([q[half], qx[half]], axis=1))
            p = jnp.exp(s + bias[half][: s.shape[0]])
            dp = dot_t(v, jnp.concatenate([g[half], gx[half]], axis=1))
            ds = (p * dp).astype(BF)
            gk_ref[half, :, at : at + 128] = one_block(dot(ds, q[half]), single).astype(BF)
            gv_ref[half, :, at : at + 128] = one_block(dot(p.astype(BF), g[half]), single).astype(BF)


ATTENTION_COST = pl.CostEstimate(
    flops=8_000_000_000, bytes_accessed=6 << 20, transcendentals=PAIRS * 256 * KEYS
)
PARAMS = pltpu.CompilerParams(vmem_limit_bytes=24 * 1024 * 1024)
HERE = pl.BlockSpec(memory_space=pltpu.VMEM)
ANYWHERE = pl.BlockSpec(memory_space=pl.ANY)
FLAT = jax.ShapeDtypeStruct((2 * HALF, WIDE), BF)


def attention_call(kernel, outs, *args):
    return pl.pallas_call(
        kernel,
        out_shape=outs,
        in_specs=[HERE] * len(args),
        out_specs=jax.tree.map(lambda _: HERE, outs),
        compiler_params=PARAMS,
        cost_estimate=ATTENTION_COST,
    )(*args)


def attend_fwd(q, kv_own, kv_sib, where):
    return attention_call(fwd_kernel, (FLAT, FLAT), q, kv_own, kv_sib, *where)


def attend_dq(qe, ge, kv_own, kv_sib, where):
    return attention_call(dq_kernel, FLAT, qe, ge, kv_own, kv_sib, *where)


def attend_dkv(kv, qe_own, qe_sib, ge_own, ge_sib, where):
    part = jax.ShapeDtypeStruct((2, HALF, WIDE), BF)
    return attention_call(dkv_kernel, (part, part), kv, qe_own, qe_sib, ge_own, ge_sib, *where)


FWD_PIECES = ((0, 1152), (1152, 2304), (2304, 3328), (3328, FF))
BACK_PIECES = ((0, FF // 2), (FF // 2, FF))
ROWS = 2 * HALF


def normalised(v):
    mean = jnp.mean(v, axis=1, keepdims=True)
    centred = v - mean
    inv = lax.rsqrt(jnp.mean(centred * centred, axis=1, keepdims=True) + 1e-05)
    return centred * inv, inv


def weight_copies(pieces, wout, wup, wdown, wout_here, wup_here, wdown_here, sems):
    out = pltpu.make_async_copy(wout, wout_here, sems.at[0])
    ups, downs = [], []
    for k, (a, b) in enumerate(pieces):
        ups.append(pltpu.make_async_copy(wup.at[:, a:b], wup_here.at[:, a:b], sems.at[1 + 2 * k]))
        downs.append(pltpu.make_async_copy(wdown.at[a:b, :], wdown_here.at[a:b, :], sems.at[2 + 2 * k]))
    return out, ups, downs


def mlp_fwd_kernel(
    ctx, hidden, gain, gain_next, a_o, b_o, a_u, b_d, b_u, a_d, wout, wup, wdown,
    middle, n2, low_o, low_u, low_d, after, n1_next, wout_here, wup_here, wdown_here, sems
):
    out, ups, downs = weight_copies(FWD_PIECES, wout, wup, wdown, wout_here, wup_here, wdown_here, sems)
    out.start()
    for up, down in zip(ups, downs):
        up.start()
        down.start()
    x = ctx[:, :D]
    low = dot(x, a_o[...]).astype(BF)
    low_o[...] = low
    out.wait()
    mid = hidden[...] + dot(x, wout_here[...]) + dot(low, b_o[...])
    middle[...] = mid
    normed = (normalised(mid)[0] * gain[...]).astype(BF)
    n2[...] = normed
    low = dot(normed, a_u[...]).astype(BF)
    low_u[...] = low
    total, total_low = jnp.zeros((ROWS, D), F32), jnp.zeros((ROWS, RANK), F32)
    for k, (a, b) in enumerate(FWD_PIECES):
        ups[k].wait()
        up = dot(normed, wup_here[:, a:b]) + dot(low, b_u[:, a:b])
        act = (up * (0.5 * (1.0 + lax.erf(up * 0.7071067811865476)))).astype(BF)
        downs[k].wait()
        total = total + dot(act, wdown_here[a:b, :])
        total_low = total_low + dot(act, a_d[a:b, :])
    low = total_low.astype(BF)
    low_d[...] = low
    new = middle[...] + (total + dot(low, b_d[...]))
    after[...] = new
    n1_next[...] = (normalised(new)[0] * gain_next[...]).astype(BF)


def mlp_back_kernel(
    g, ctx, middle, gain, n2, low_o, low_u, low_d, a_o, b_o, a_u, b_d, spread, b_u, a_d, wout, wup, wdown,
    gh2, ge, ga_o, gb_o, ga_u, gb_d, ga_d, gb_u, wout_here, wup_here, wdown_here, sems
):
    out, ups, downs = weight_copies(BACK_PIECES, wout, wup, wdown, wout_here, wup_here, wdown_here, sems)
    for up, down in zip(ups, downs):
        up.start()
        down.start()
    out.start()
    gy = g[...].astype(BF)
    glow_d = dot_t(gy, b_d[...]).astype(BF)
    gb_d[...] = t_dot(low_d[...], gy).astype(BF)
    normed, low = n2[...], low_u[...]
    gn2, glow_u = jnp.zeros((ROWS, D), F32), jnp.zeros((ROWS, RANK), F32)
    for k, (a, b) in enumerate(BACK_PIECES):
        ups[k].wait()
        up = dot(normed, wup_here[:, a:b]) + dot(low, b_u[:, a:b])
        phi = 0.5 * (1.0 + lax.erf(up * 0.7071067811865476))
        ga_d[:, a:b] = t_dot(glow_d, (up * phi).astype(BF)).astype(BF)
        downs[k].wait()
        gact = dot_t(gy, wdown_here[a:b, :]) + dot_t(glow_d, a_d[a:b, :])
        density = jnp.exp(-0.5 * up * up) * 0.3989422804014327
        gup = (gact * (phi + up * density)).astype(BF)
        gb_u[:, a:b] = t_dot(low, gup).astype(BF)
        gn2 = gn2 + dot_t(gup, wup_here[:, a:b])
        glow_u = glow_u + dot_t(gup, b_u[:, a:b])
    glow_u = glow_u.astype(BF)
    gn2 = gn2 + dot_t(glow_u, a_u[...])
    ga_u[...] = t_dot(glow_u, normed).astype(BF)
    out.wait()
    through_norm(g, middle[...], gain, gn2, ctx[:, :D], low_o[...], a_o, b_o, wout_here, spread, gh2, ge, ga_o, gb_o)


def through_norm(g, middle, gain, gn2, x, low_o, a_o, b_o, wout, spread, gh2, ge, ga_o, gb_o):
    r, inv = normalised(middle)
    gr = gn2 * gain[...]
    grad = g[...] + inv * (
        gr - jnp.mean(gr, axis=1, keepdims=True) - r * jnp.mean(gr * r, axis=1, keepdims=True)
    )
    gh2[...] = grad
    gproj = grad.astype(BF)
    glow_o = dot_t(gproj, b_o[...]).astype(BF)
    ga_o[...] = t_dot(glow_o, x).astype(BF)
    gb_o[...] = t_dot(low_o, gproj).astype(BF)
    gctx = (dot_t(gproj, wout[...]) + dot_t(glow_o, a_o[...])).astype(BF)
    product = gctx.astype(F32) * x.astype(F32)
    first = product.astype(BF)
    second = (product - first.astype(F32)).astype(BF)
    delta = dot(first, spread[...]) + dot(second, spread[...])
    ge[:, :D] = gctx
    ge[:, D:] = row_terms(-delta)[:, HEAD_DIM:]


def qkv_back_kernel(
    gq, gk, gv, low, n1, a, b_q, b_kv, hidden, gain, gh2, wq, wkv, g, ga, gb_q, gb_kv, wq_here, wkv_here, sems
):
    first = pltpu.make_async_copy(wq, wq_here, sems.at[0])
    second = pltpu.make_async_copy(wkv, wkv_here, sems.at[1])
    first.start()
    second.start()
    q, k, v = gq[...], gk[...].reshape(ROWS, WIDE), gv[...].reshape(ROWS, WIDE)
    glow = dot_t(q, b_q[...]) + dot_t(k, b_kv[:, :WIDE]) + dot_t(v, b_kv[:, WIDE:])
    glow = glow.astype(BF)
    ga[...] = t_dot(glow, n1[...]).astype(BF)
    gb_q[...] = t_dot(low[...], q).astype(BF)
    gb_kv[:, :WIDE] = t_dot(low[...], k).astype(BF)
    gb_kv[:, WIDE:] = t_dot(low[...], v).astype(BF)
    first.wait()
    gn1 = dot_t(q, wq_here[...])
    second.wait()
    gn1 = gn1 + dot_t(k, wkv_here[:, :WIDE]) + dot_t(v, wkv_here[:, WIDE:]) + dot_t(glow, a[...])
    r, inv = normalised(hidden[...])
    gr = gn1 * gain[...]
    g[...] = gh2[...] + inv * (
        gr - jnp.mean(gr, axis=1, keepdims=True) - r * jnp.mean(gr * r, axis=1, keepdims=True)
    )


def mlp_both_kernel(
    ctx, hidden, gain, g, a_o, b_o, a_u, b_d, spread, b_u, a_d, wout, wup, wdown,
    after, gh2, ge, ga_o, gb_o, ga_u, gb_d, ga_d, gb_u, wout_here, wup_here, wdown_here, sems
):
    out, ups, downs = weight_copies(BACK_PIECES, wout, wup, wdown, wout_here, wup_here, wdown_here, sems)
    out.start()
    for up, down in zip(ups, downs):
        up.start()
        down.start()
    x = ctx[:, :D]
    low_o = dot(x, a_o[...]).astype(BF)
    out.wait()
    gh2[...] = hidden[...] + dot(x, wout_here[...]) + dot(low_o, b_o[...])
    normed = (normalised(gh2[...])[0] * gain[...]).astype(BF)
    low = dot(normed, a_u[...]).astype(BF)
    gy = g[...].astype(BF)
    glow_d = dot_t(gy, b_d[...]).astype(BF)
    total, total_low = jnp.zeros((ROWS, D), F32), jnp.zeros((ROWS, RANK), F32)
    gn2, glow_u = jnp.zeros((ROWS, D), F32), jnp.zeros((ROWS, RANK), F32)
    for k, (a, b) in enumerate(BACK_PIECES):
        ups[k].wait()
        up = dot(normed, wup_here[:, a:b]) + dot(low, b_u[:, a:b])
        phi = 0.5 * (1.0 + lax.erf(up * 0.7071067811865476))
        act = (up * phi).astype(BF)
        ga_d[:, a:b] = t_dot(glow_d, act).astype(BF)
        downs[k].wait()
        total = total + dot(act, wdown_here[a:b, :])
        total_low = total_low + dot(act, a_d[a:b, :])
        gact = dot_t(gy, wdown_here[a:b, :]) + dot_t(glow_d, a_d[a:b, :])
        density = jnp.exp(-0.5 * up * up) * 0.3989422804014327
        gup = (gact * (phi + up * density)).astype(BF)
        gb_u[:, a:b] = t_dot(low, gup).astype(BF)
        gn2 = gn2 + dot_t(gup, wup_here[:, a:b])
        glow_u = glow_u + dot_t(gup, b_u[:, a:b])
    low_d = total_low.astype(BF)
    gb_d[...] = t_dot(low_d, gy).astype(BF)
    after[...] = (gh2[...] + (total + dot(low_d, b_d[...]))).astype(BF)
    glow_u = glow_u.astype(BF)
    gn2 = gn2 + dot_t(glow_u, a_u[...])
    ga_u[...] = t_dot(glow_u, normed).astype(BF)
    through_norm(g, gh2[...], gain, gn2, x, low_o, a_o, b_o, wout_here, spread, gh2, ge, ga_o, gb_o)


def shape_of(rows, width, kind=BF):
    return jax.ShapeDtypeStruct((rows, width), kind)


def mlp_call(kernel, pieces, args, outs, flops, limit=40):
    return pl.pallas_call(
        kernel,
        out_shape=outs,
        in_specs=[HERE] * (len(args) - 3) + [ANYWHERE] * 3,
        out_specs=(HERE,) * len(outs),
        scratch_shapes=[
            pltpu.VMEM((D, D), BF),
            pltpu.VMEM((D, FF), BF),
            pltpu.VMEM((FF, D), BF),
            pltpu.SemaphoreType.DMA((1 + 2 * len(pieces),)),
        ],
        compiler_params=pltpu.CompilerParams(vmem_limit_bytes=limit * 1024 * 1024),
        cost_estimate=pl.CostEstimate(flops=flops, bytes_accessed=24 << 20, transcendentals=ROWS * FF),
    )(*args)


def mlp_fwd(*args):
    outs = (shape_of(ROWS, D, F32), shape_of(ROWS, D)) + (shape_of(ROWS, RANK),) * 3
    outs += (shape_of(ROWS, D, F32), shape_of(ROWS, D))
    return mlp_call(mlp_fwd_kernel, FWD_PIECES, args, outs, 10_000_000_000)


def mlp_both(*args):
    outs = (shape_of(ROWS, D), shape_of(ROWS, D, F32), shape_of(ROWS, WIDE)) + (shape_of(RANK, D),) * 4
    outs += (shape_of(RANK, FF),) * 2
    return mlp_call(mlp_both_kernel, BACK_PIECES, args, outs, 18_000_000_000)


def qkv_back(*args):
    return pl.pallas_call(
        qkv_back_kernel,
        out_shape=(shape_of(ROWS, D, F32), shape_of(RANK, D), shape_of(RANK, WIDE), shape_of(RANK, 2 * WIDE)),
        in_specs=[HERE] * 11 + [ANYWHERE] * 2,
        out_specs=(HERE,) * 4,
        scratch_shapes=[
            pltpu.VMEM((D, WIDE), BF),
            pltpu.VMEM((D, 2 * WIDE), BF),
            pltpu.SemaphoreType.DMA((2,)),
        ],
        compiler_params=pltpu.CompilerParams(vmem_limit_bytes=20 * 1024 * 1024),
        cost_estimate=pl.CostEstimate(flops=5_000_000_000, bytes_accessed=10 << 20, transcendentals=0),
    )(*args)


def mlp_back(*args):
    outs = (shape_of(ROWS, D, F32), shape_of(ROWS, WIDE)) + (shape_of(RANK, D),) * 4
    outs += (shape_of(RANK, FF),) * 2
    return mlp_call(mlp_back_kernel, BACK_PIECES, args, outs, 16_000_000_000, 56)


def ring_start(block):
    return lax.ppermute(block, "seq", UP), lax.ppermute(block, "seq", DOWN)


def ring_far(block, before, after):
    far_lo = lax.ppermute(before[0], "seq", UP)
    far_hi = lax.ppermute(after[1], "seq", DOWN)
    return jnp.stack([block, before, after, jnp.stack([far_lo, far_hi])])


def other_core(own):
    return lax.ppermute(own, "seq", CORE)


def sum_sequence(parts, core, y):
    parts = parts.reshape((4, 2) + parts.shape[1:])
    mine = lax.dynamic_index_in_dim(parts, core, 1, keepdims=False)
    other = lax.dynamic_index_in_dim(parts, 1 - core, 1, keepdims=False)
    half = mine.astype(F32) + lax.ppermute(other, "seq", CORE).astype(F32)

    def of(step):
        return lax.dynamic_index_in_dim(half, (y + step) % 4, 0, keepdims=False)

    total = of(0)
    for step, route in ((1, UP), (3, DOWN), (2, FAR)):
        total = total + lax.ppermute(of(step).astype(BF), "seq", route).astype(F32)
    return total


def tie(*values):
    return lax.optimization_barrier(values)


def eighths(turned, straight):
    def cut(a, part):
        return jnp.pad(a, ((0, 0), (0, 8 * part - a.shape[1]))).reshape(RANK, 8, part)

    first = cut(jnp.concatenate(turned, axis=1), PART_A)
    return jnp.swapaxes(jnp.concatenate([first, cut(straight, PART_B)], axis=2), 0, 1)


def by_adapter_kernel(picks, *refs):
    parts, out_ref, acc = refs[:-2], refs[-2], refs[-1]
    acc[...] = jnp.zeros_like(acc)
    at = 0
    for ref in parts:
        for k in range(ref.shape[0]):
            rows = pl.ds(pl.multiple_of(picks[at] * RANK, RANK), RANK)
            acc[rows, :] = acc[rows, :] + ref[k].astype(F32)
            at += 1
    for j in range(PART // 128):
        square = acc[:, 128 * j : 128 * (j + 1)]
        square = square.T if 128 * j < PART_A else square
        out_ref[128 * j : 128 * (j + 1), :] = square.astype(BF)


def by_adapter(parts, picks):
    return pl.pallas_call(
        by_adapter_kernel,
        out_shape=jax.ShapeDtypeStruct((PART, 128), BF),
        in_specs=[pl.BlockSpec(memory_space=pltpu.SMEM)]
        + [pl.BlockSpec(memory_space=pltpu.VMEM)] * len(parts),
        out_specs=pl.BlockSpec(memory_space=pltpu.VMEM),
        scratch_shapes=[pltpu.VMEM((8 * RANK, PART), F32)],
        compiler_params=PARAMS,
        cost_estimate=pl.CostEstimate(flops=16 * RANK * PART, bytes_accessed=2 << 20, transcendentals=0),
    )(picks, *parts)


def unfold_rows(layer, rows, outs):
    turned, straight = outs[:-1], outs[-1]
    start = 0
    for out, width in zip(turned, TURNED):
        at = start
        while at < start + width:
            n = min(start + width, (at // PART_A + 1) * PART_A) - at
            out[layer, at - start : at - start + n, :] = rows(at // PART_A, at % PART_A, n)
            at += n
        start += width
    squares = PART_B // 128
    for t in range(FF // 128):
        value = rows(t // squares, PART_A + 128 * (t % squares), 128)
        straight[layer, :, 128 * t : 128 * (t + 1)] = value


def unfold_late_kernel(ref, *outs):
    unfold_rows(0, lambda e, at, n: ref[e, at : at + n, :].astype(F32), outs)


def unfold_kernel(place, own_ref, sib_ref, *refs):
    half = len(refs) // 2

    def rows(e, at, n):
        k = place[e]
        mine = own_ref[k % 4, at : at + n, :]
        other = sib_ref[k % 4, at : at + n, :]
        return jnp.where(k < 4, mine.astype(F32), other.astype(F32))

    unfold_rows(0, rows, refs[half:])


def one_layer(layer, *shape):
    return pl.BlockSpec((1,) + shape, lambda i: (layer, 0, 0))


def unfold(kernel, layer, *args):
    shapes = [(w, 128) for w in TURNED] + [(128, FF)]
    whole = [jax.ShapeDtypeStruct((2,) + shape, F32) for shape in shapes]
    first, earlier = (args, ()) if layer == 1 else (args[:3], args[3])
    specs = [pl.BlockSpec(memory_space=pltpu.SMEM)] if layer == 0 else []
    specs += [fixed(*a.shape) for a in first[len(specs) :]] + [ANYWHERE] * len(earlier)
    return pl.pallas_call(
        kernel,
        grid=(1,),
        out_shape=tuple(whole),
        in_specs=specs,
        out_specs=tuple(one_layer(layer, *shape) for shape in shapes),
        input_output_aliases={3 + n: n for n in range(len(earlier))},
        compiler_params=pltpu.CompilerParams(vmem_limit_bytes=40 * 1024 * 1024),
        cost_estimate=pl.CostEstimate(flops=0, bytes_accessed=14 << 20, transcendentals=0),
    )(*first, *earlier)


def fixed(*shape):
    return pl.BlockSpec(shape, lambda i: (0,) * len(shape))


def share(w_qkv, w_out, w_up, w_down, z_lo, spare):
    def half_row(w, front, lines):
        size = lines * 128 - w.shape[1]
        first = jnp.pad(w, ((0, 0), (0, size)))
        second = jnp.pad(w, ((0, 0), (front, size - front)))
        return jnp.where(z_lo == 0, first, second).reshape(-1, lines, 128)

    def put(a, room):
        return jnp.pad(a, ((0, 0), (0, room - a.shape[1]), (0, 0)))

    extra = jnp.broadcast_to(spare[None], (2, 1, 128))
    attention = [
        put(half_row(w_qkv, 32, N_QKV), AT_OUT),
        put(half_row(w_out, 32, N_OUT), LINES - AT_OUT - 1),
        extra,
    ]
    up, down = put(w_up.reshape(-1, N_UP, 128), LINES), put(w_down.reshape(-1, N_DOWN, 128), LINES - 1)
    return jnp.concatenate(attention, axis=1), jnp.concatenate([up, down, extra], axis=1)


def spin(a):
    return pltpu.roll(a, HEAD_DIM, 1)


def fill(ref, base, lines):
    ref[pl.ds(base, lines.shape[0], stride=2), :] = lines


def between(ref, base, n):
    now, later = ref[pl.ds(base, n, stride=2), :], ref[pl.ds(base + 2, n, stride=2), :]
    ref[pl.ds(base + 1, n, stride=2), :] = spin(jnp.where(lanes(n) < HEAD_DIM, later, now))


def columns(ref, dst, to, start, units, step=2):
    got = ref[pl.ds(start, dst.shape[0], stride=units), :].astype(BF)
    n = min(128, dst.shape[1] - to)
    dst[:, to : to + n] = got[:, :n]


def lines_of(ref, pair, zl, start, n):
    return ref[0, zl, 0, pair % 4, pair // 4, start : start + n, :].astype(F32)


def unpack_attention_kernel(g_ref, *refs):
    def lines(pair, zl):
        return lines_of(g_ref, pair, zl, 0, N_QKV), lines_of(g_ref, pair, zl, AT_OUT, N_OUT)

    unpack_attention_lines(lines, *refs)


def unpack_first_kernel(steps, own_1, sib_1, own_2, sib_2, *refs):
    def lines(pair, zl):
        x, core = pair % 4, pair // 4
        z_at, x_at = steps[4 + 2 * (pl.program_id(0) // 4) + zl], steps[8 + x]
        mine = steps[12] == core
        top = jnp.where(mine, own_1[z_at, 0, x_at], sib_1[z_at, 0, x_at])
        bottom = jnp.where(mine, own_2[0, z_at, x_at], sib_2[0, z_at, x_at])
        both = jnp.concatenate([top.astype(F32), bottom.astype(F32)], axis=0)
        return both[:N_QKV], both[AT_OUT : AT_OUT + N_OUT]

    unpack_attention_lines(lines, *refs)


def unpack_attention_lines(lines, q_ref, kv_ref, out_ref, s_qkv, s_out):
    low = lanes(1) < HEAD_DIM
    zero = jnp.zeros((1, 128), F32)
    for pair in range(8):
        (qkv0, out0), (qkv1, out1) = lines(pair, 0), lines(pair, 1)
        base, base_out = pair * 867, pair * 289
        fill(s_qkv, base, qkv0)
        fill(s_qkv, base + 433, qkv1)
        between(s_qkv, base, N_QKV - 1)
        between(s_qkv, base + 433, N_QKV)
        s_qkv[pl.ds(base + 432, 1), :] = qkv0[N_QKV - 1 :] + spin(jnp.where(low, qkv1[:1], zero))
        s_qkv[pl.ds(base + 433, 1), :] = qkv1[:1] + spin(jnp.where(low, zero, qkv0[N_QKV - 1 :]))
        fill(s_out, base_out, out0)
        fill(s_out, base_out + 144, out1)
        s_out[pl.ds(base_out + 144, 1), :] = out0[N_OUT - 1 :] + out1[:1]
        between(s_out, base_out, N_OUT - 1)
        between(s_out, base_out + 144, N_OUT - 1)
    half = lanes(BLOCK) < HEAD_DIM
    for dst, to, first in ((q_ref, 0, 0), (kv_ref, 0, 17), (kv_ref, WIDE, 34)):
        for j in range(8):
            columns(s_qkv, dst, to + 128 * j, first + 2 * j, 51)
        got = s_qkv[pl.ds(first + 16, BLOCK, stride=51), :]
        dst[:, to + D - HEAD_DIM : to + WIDE] = jnp.where(half, got, 0.0).astype(BF)
    for j in range(9):
        columns(s_out, out_ref, 128 * j, 2 * j, 17)


def unpack_mlp_kernel(g_up, g_down, up_ref, down_ref, s_up, s_down):
    for pair in range(8):
        for zl in range(2):
            at = pair * 2 + zl
            s_up[pl.ds(at * N_UP, N_UP), :] = lines_of(g_up, pair, zl, 0, N_UP)
            fill(s_down, at * 2 * N_DOWN, lines_of(g_down, pair, zl, 0, N_DOWN))
    for at in range(16):
        between(s_down, at * 2 * N_DOWN, N_DOWN)
    for j in range(34):
        columns(s_up, up_ref, 128 * j, j, 34)
    for j in range(9):
        columns(s_down, down_ref, 128 * j, 2 * j, 17)


def unpack(kernel, got, at, outs, scratch_lines):
    g = got.reshape(2, 2, 4, 4, 2, -1, 128)

    def spec(k):
        return pl.BlockSpec((1, 2, 1, 4, 2, LINES, 128), lambda i: (i // 4, 0, i % 4, 0, 0, k, 0))

    return pl.pallas_call(
        kernel,
        grid=(8,),
        out_shape=tuple(jax.ShapeDtypeStruct((8 * r, w), BF) for r, w in outs),
        in_specs=[spec(k) for k in at],
        out_specs=tuple(pl.BlockSpec((r, w), lambda i: (i, 0)) for r, w in outs),
        scratch_shapes=[pltpu.VMEM((n, 128), F32) for n in scratch_lines],
        compiler_params=pltpu.CompilerParams(vmem_limit_bytes=26 * 1024 * 1024),
        cost_estimate=pl.CostEstimate(
            flops=0, bytes_accessed=len(at) * (20 << 20), transcendentals=0
        ),
    )(*[g] * len(at))


ATTENTION_OUTS = [(BLOCK, WIDE), (BLOCK, 2 * WIDE), (BLOCK, D)]
ATTENTION_LINES = [8 * 867 + 8, 8 * 289 + 8]


def unpack_attention(got, at):
    return unpack(unpack_attention_kernel, got, [at], ATTENTION_OUTS, ATTENTION_LINES)


def along(axis, block, near):
    name, shift = SHIFTS[axis]
    before = lax.ppermute(block, name, shift(1))
    after = lax.ppermute(block, name, shift(-1))
    if near:
        far = lax.ppermute(block, name, shift(2))
    else:
        n = block.shape[0] // 2
        far = [lax.ppermute(before[:n], name, shift(1)), lax.ppermute(after[n:], name, shift(-1))]
        far = jnp.concatenate(far)
    return jnp.stack([block, before, after, far])


def gather_first(share, later):
    n = LINES // 2
    row = along("x", share, True)
    one, two = along("y", row[:, :n], True), along("z", row[:, n:], True)
    one, two, later = tie(one, two, later)
    one, two = along("z", one, False), along("y", two, False)
    return (one, other_core(one), two, other_core(two)), later


def unpack_first(one, sib_one, two, sib_two, steps):
    n = LINES // 2
    spec_one = pl.BlockSpec((4, 1, 4, n, 128), lambda i, steps: (0, steps[i % 4], 0, 0, 0))
    spec_two = pl.BlockSpec((1, 4, 4, n, 128), lambda i, steps: (steps[i % 4], 0, 0, 0, 0))
    return pl.pallas_call(
        unpack_first_kernel,
        grid_spec=pltpu.PrefetchScalarGridSpec(
            num_scalar_prefetch=1,
            grid=(8,),
            in_specs=[spec_one, spec_one, spec_two, spec_two],
            out_specs=tuple(pl.BlockSpec((r, w), lambda i, steps: (i, 0)) for r, w in ATTENTION_OUTS),
            scratch_shapes=[pltpu.VMEM((n, 128), F32) for n in ATTENTION_LINES],
        ),
        out_shape=tuple(jax.ShapeDtypeStruct((8 * r, w), BF) for r, w in ATTENTION_OUTS),
        compiler_params=pltpu.CompilerParams(vmem_limit_bytes=26 * 1024 * 1024),
        cost_estimate=pl.CostEstimate(flops=0, bytes_accessed=30 << 20, transcendentals=0),
    )(steps, one, sib_one, two, sib_two)


def unpack_mlp(got, at):
    outs = [(BLOCK, FF), (4 * BLOCK, D)]
    return unpack(unpack_mlp_kernel, got, [at, at + 1], outs, [16 * N_UP, 32 * N_DOWN + 8])


def shards(
    tokens, segments, adapter_pick, norm_gain, w_qkv, w_out, w_up, w_down,
    a_qkv, b_qkv, a_out, b_out, a_up, b_up, a_down, b_down, grad_out
):
    layers = norm_gain.shape[0]
    index = lax.axis_index("seq")
    z_hi, place = index // 8, index % 8
    core, y = place % 2, place // 2

    def halves(own, other):
        return jnp.where(z_hi == 0, jnp.stack([own, other]), jnp.stack([other, own]))

    def mine(a):
        return lax.dynamic_index_in_dim(a, z_hi, 0, keepdims=False)

    def theirs(a):
        return lax.dynamic_index_in_dim(a, 1 - z_hi, 0, keepdims=False)

    batch = lax.axis_index("batch")
    spare = (segments.reshape(1, 128), jnp.pad(adapter_pick[None], ((0, 0), (0, 126))))
    attention, _ = share(w_qkv, w_out, w_up, w_down, batch % 2, spare[0].astype(BF))
    _, mlp = share(w_qkv, w_out, w_up, w_down, batch % 2, spare[1].astype(BF))

    def gather(a):
        return lax.all_gather(a, BOTH, axis=0, tiled=True, axis_index_groups=ALL)

    early = gather(jnp.concatenate([mlp[0], attention[1]], axis=0))
    late = gather(mlp[1])
    raw = (a_qkv, b_qkv, a_out, b_out, a_up, b_up, a_down, b_down, norm_gain)
    (one, sib_one, two, sib_two), raw = gather_first(attention[0], raw)
    a_qkv, b_qkv, a_out, b_out, a_up, b_up, a_down, b_down, norm_gain = raw

    sent = lax.ppermute(jnp.stack([theirs(tokens), theirs(grad_out)]), "seq", SWAP)
    hidden = halves(mine(tokens), sent[0]).reshape(2 * HALF, D).astype(F32)
    grad_hidden = halves(mine(grad_out), sent[1]).reshape(2 * HALF, D).astype(F32)
    pick = mine(adapter_pick)

    def segments_of(two):
        lines = two[:, :, 0, -1]
        lines = jnp.stack([lines[:, 0], lines[:, 3]])
        return lax.dynamic_slice(lines, (0, 0, z_hi * HALF), (2, 4, HALF))

    seg = jnp.stack([segments_of(two), segments_of(sib_two)], axis=1)
    seg = jnp.where(z_hi == 0, seg, seg[::-1]).astype(jnp.int32)
    offset = jnp.arange(HALF, dtype=jnp.int32)
    start = jnp.array([0, KEYS // 2], jnp.int32)[:, None]
    lpos = (start + place * HALF + offset[None]).reshape(2 * HALF, 1)
    lseg = seg[:, 0, 0].reshape(2 * HALF, 1)
    ys = (y + jnp.array([0, 3, 1, 2], jnp.int32)) % 4
    order = jnp.concatenate([2 * ys + core, 2 * ys + 1 - core])
    kpos = (start[:, :, None] + (order * HALF)[None, :, None] + offset).reshape(1, KEYS)
    where = (lpos, lseg, kpos, seg.reshape(1, KEYS))

    z_lo, x = batch % 2, batch // 2
    z = z_hi * 2 + z_lo
    picks = early.reshape(2, 2, 4, 4, 2, -1, 128)[0, :, 0, :, 0, 2 * LINES - 1, :2].astype(jnp.int32)
    picks = jnp.swapaxes(picks, 0, 1).reshape(16)
    steps = jnp.array([0, 3, 1, 2], jnp.int32)

    def sequence(zs, xs):
        return 2 * (2 * xs + zs % 2) + zs // 2

    four = jnp.arange(4, dtype=jnp.int32)
    picks_in_order = jnp.take(picks, sequence(four[:, None], four[None, :]).reshape(16))
    zs, xs = (z + steps) % 4, (x + steps) % 4
    picks_by_step = jnp.take(picks, sequence(zs[None, :], xs[:, None]).reshape(16))
    eight = jnp.arange(8, dtype=jnp.int32)
    back = jnp.array([0, 2, 3, 1], jnp.int32)
    place_by_step = 4 * ((eight % 2) ^ core) + jnp.take(back, (eight // 2 - y) % 4)
    arrival = [jnp.take(back, (four - at) % 4) for at in (y, z, x)]
    arrival = jnp.concatenate(arrival + [core[None]]).astype(jnp.int32)

    def low_in(a, l):
        return lax.dynamic_slice_in_dim(a[l], pick * RANK, RANK, 1)

    def low_out(b, l):
        return lax.dynamic_slice_in_dim(b[l], pick * RANK, RANK, 0)

    heads_of = (jnp.arange(D, dtype=jnp.int32) // HEAD_DIM)[:, None]
    spread = (heads_of == (jnp.arange(128, dtype=jnp.int32)[None, :] - HEAD_DIM) // 3).astype(BF)

    def adapters(l):
        b_first = low_out(b_qkv, l)
        b_kv = jnp.concatenate([widen(b_first[:, D : 2 * D]), widen(b_first[:, 2 * D :])], axis=1)
        rest = [f(a, l) for pair in ((a_out, b_out), (a_up, b_up), (a_down, b_down)) for f, a in zip((low_in, low_out), pair)]
        return [low_in(a_qkv, l), widen(b_first[:, :D]), b_kv] + rest

    n1 = (norm_stats(hidden)[0] * norm_gain[0, 0]).astype(BF)
    ahead = (where, spread, n1, grad_hidden, [adapters(l) for l in range(layers)])
    sib_one, (where, spread, n1, grad_hidden, adapter_parts) = tie(sib_one, ahead)
    first = unpack_first(one, sib_one, two, sib_two, arrival)
    saved, queries = [], []
    for l in range(layers):
        a_first, b_q, b_kv, a_o, b_o, a_u, b_u, a_d, b_d = adapter_parts[l]
        wq, wkv, wout = first
        low_qkv = dot(n1, a_first).astype(BF)
        kv = (dot(n1, wkv) + dot(low_qkv, b_kv)).astype(BF).reshape(2, HALF, 2 * WIDE)
        q = (dot(n1, wq) + dot(low_qkv, b_q)).astype(BF) * jnp.asarray(0.125, BF)
        before, after = ring_start(kv)
        if l == 0:
            wup, wdown = unpack_mlp(early, 0)
            before, after, q, wup, wdown = tie(before, after, q, wup, wdown)
        else:
            before, after, q, qe_own = tie(before, after, q, qe_own)
            queries.append((qe_own, other_core(qe_own)))
        kv_own = ring_far(kv, before, after)
        if l > 0:
            late, kv_own = tie(late, kv_own)
            wup, wdown = unpack_mlp(late, 0)
        if l == 0:
            first = unpack_attention(early, 2)
            kv_own, *first = tie(kv_own, *first)
        kv_sib = other_core(kv_own)
        ctx, qe = attend_fwd(q, kv_own, kv_sib, where)
        qe = qe.reshape(2, HALF, WIDE)
        q_before, q_after = ring_start(qe)
        gains = norm_gain[l, 1][None], norm_gain[(l + 1) % layers, 0][None]
        small, large = (a_o, b_o, a_u, b_d), (b_u, a_d, wout, wup, wdown)
        rows, hidden_next, n1_next = None, None, None
        if l < layers - 1:
            middle, n2, low_o, low_u, low_d, hidden_next, n1_next = mlp_fwd(ctx, hidden, *gains, *small, *large)
            q_before, q_after, hidden_next, n1_next = tie(q_before, q_after, hidden_next, n1_next)
            rows = (ctx, middle, gains[0], n2, low_o, low_u, low_d)
        else:
            result, *back = mlp_both(ctx, hidden, gains[0], grad_hidden, *small, spread, *large)
            q_before, q_after, *back = tie(q_before, q_after, *back)
        qe_own = ring_far(qe, q_before, q_after)
        saved.append(
            (hidden, n1, low_qkv, kv, kv_own, kv_sib, qe.reshape(2 * HALF, WIDE))
            + (rows, small, large, a_first, b_q, b_kv, wq, wkv)
        )
        hidden, n1 = hidden_next, n1_next

    behind = None
    for l in reversed(range(layers)):
        hidden_in, n1, low_qkv, kv, kv_own, kv_sib, qe, rows, small, large, a_first, b_q, b_kv, wq, wkv = saved[l]
        if l < layers - 1:
            back = mlp_back(g, *rows, *small, spread, *large)
        gh2, ge, ga_o, gb_o, ga_u, gb_d, ga_d, gb_u = back
        if l == layers - 1:
            qe_own, ge = tie(qe_own, ge)
            qe_sib = other_core(qe_own)
        else:
            qe_own, qe_sib = queries[l]
        g_block = ge.reshape(2, HALF, WIDE)
        g_before, g_after = ring_start(g_block)
        if behind is not None:
            behind, ge = tie(behind, ge)
            behind = lax.all_gather(behind, BOTH, axis=0, axis_index_groups=SAME_PLACE)
        gq = attend_dq(qe, ge, kv_own, kv_sib, where)
        g_before, g_after, gq = tie(g_before, g_after, gq)
        ge_own = ring_far(g_block, g_before, g_after)
        ge_sib = other_core(ge_own)
        gk, gv = attend_dkv(kv, qe_own, qe_sib, ge_own, ge_sib, where)
        g, ga_q, gb_q, gb_kv = qkv_back(
            gq, gk, gv, low_qkv, n1, a_first, b_q, b_kv, hidden_in, norm_gain[l, 0][None], gh2, wq, wkv
        )
        gb_q = [gb_q[:, :D], gb_kv[:, :D], gb_kv[:, WIDE : WIDE + D]]
        parts = eighths([ga_q, ga_o, ga_u, ga_d] + gb_q + [gb_o, gb_d], gb_u)
        if l > 0:
            parts, g = tie(parts, g)
            behind = sum_sequence(parts, core, y)

    got = lax.all_to_all(parts, BOTH, 0, 0, axis_index_groups=SAME_SEQUENCE)
    part = jnp.sum(got.astype(F32), axis=0).astype(BF)
    along_z = [lax.ppermute(part, BOTH, z_shift(by)) for by in (1, -1, 2)]
    behind, part = tie(behind, part)
    one = by_adapter([behind], picks_in_order)
    one, *along_z = tie(one, *along_z)
    one = lax.all_gather(one, BOTH, axis=0, axis_index_groups=SAME_SEQUENCE)
    along_z = jnp.stack([part] + along_z)
    before = lax.ppermute(along_z, "batch", x_shift(1))
    after = lax.ppermute(along_z, "batch", x_shift(-1))
    sent_home = theirs(g.reshape(2, HALF, D)), theirs(result.reshape(2, HALF, D))
    back_home = [lax.ppermute(a, "seq", SWAP) for a in sent_home]
    before, after, *back_home = tie(before, after, *back_home)
    far = [lax.ppermute(before[:2], "batch", x_shift(1)), lax.ppermute(after[2:], "batch", x_shift(-1))]
    whole = by_adapter([along_z, before, after] + far, picks_by_step)
    whole = whole.reshape(2, -1, 128)
    own = ring_far(whole, *ring_start(whole))
    one = unfold(unfold_late_kernel, 1, one)
    grad_tokens = halves(mine(g.reshape(2, HALF, D)), back_home[0])
    result = halves(mine(result.reshape(2, HALF, D)), back_home[1])
    own, grad_tokens, result, *one = tie(own, grad_tokens, result, *one)
    sib = other_core(own).reshape(4, PART, 128)
    ga_q, ga_o, ga_u, ga_d, gb_q, gb_o, gb_d, gb_u = unfold(
        unfold_kernel, 0, place_by_step, own.reshape(4, PART, 128), sib, one
    )
    gb_q, gb_o, gb_d = (jnp.swapaxes(a, 1, 2) for a in (gb_q, gb_o, gb_d))

    return result, grad_tokens, ga_q, gb_q, ga_o, gb_o, ga_u, gb_u, ga_d, gb_d


def solution(mesh):
    rows, flat, whole = P("batch", "seq", None), P(None, ("seq", "batch")), P()
    in_specs = (rows, P("batch", "seq"), P("batch"), whole) + (flat,) * 4 + (whole,) * 8 + (rows,)
    out_specs = (rows, rows) + (whole,) * 8
    return jax.shard_map(shards, mesh=mesh, in_specs=in_specs, out_specs=out_specs, check_vma=False)
```

```python
import jax
import jax.numpy as jnp
from jax import lax
from jax.experimental import pallas as pl
from jax.experimental.pallas import tpu as pltpu
from jax.sharding import PartitionSpec as P

D = 1088
HEADS = 17
HEAD_DIM = 64
FF = 4352
RANK = 16
WIDE = 1152
PAIRS = 9
HALF = 64
KEYS = 1024
BF = jnp.bfloat16
F32 = jnp.float32
NEG = -1e30

SWAP = [(i, i ^ 8) for i in range(16)]
CORE = [(i, i ^ 1) for i in range(16)]
UP = [(i, (i & 8) | ((i + 2) & 7)) for i in range(16)]
DOWN = [(i, (i & 8) | ((i - 2) & 7)) for i in range(16)]
FAR = [(i, (i & 8) | ((i + 4) & 7)) for i in range(16)]
def at_chip(z, y, x, core):
    return ((z // 2 * 4 + y) * 2 + core) * 8 + x * 2 + z % 2


ALL = [[at_chip(z, y, x, c) for z in range(4) for y in range(4) for x in range(4) for c in range(2)]]
SAME_SEQUENCE = [[at_chip(z, y, x, c) for y in range(4) for c in range(2)] for z in range(4) for x in range(4)]
SAME_PLACE = [[at_chip(z, y, x, c) for z in range(4) for x in range(4)] for y in range(4) for c in range(2)]


def z_shift(by):
    return [
        (at_chip(z, y, x, c), at_chip((z + by) % 4, y, x, c))
        for z in range(4) for y in range(4) for x in range(4) for c in range(2)
    ]


def x_shift(by):
    return [(i, (i + 2 * by) % 8) for i in range(8)]


def y_shift(by):
    return [(i, (i & 8) | ((i + 2 * by) & 7)) for i in range(16)]


BOTH = ("seq", "batch")
SHIFTS = {"x": ("batch", x_shift), "y": ("seq", y_shift), "z": (BOTH, z_shift)}
TURNED = (D, D, D, FF, 3 * D, D, D)
PART_A, PART_B = 1664, 640
PART = PART_A + PART_B

LINES = 304
AT_OUT = 224
N_QKV, N_OUT, N_UP, N_DOWN = 217, 73, 289, 289
BLOCK = 136


def dot(a, b):
    return jnp.dot(a, b, preferred_element_type=F32)


def dot_t(a, b):
    return lax.dot_general(a, b, (((1,), (1,)), ((), ())), preferred_element_type=F32)


def t_dot(a, b):
    return lax.dot_general(a, b, (((0,), (0,)), ((), ())), preferred_element_type=F32)


def norm_stats(v):
    mean = jnp.mean(v, axis=-1, keepdims=True)
    centred = v - mean
    inv = lax.rsqrt(jnp.mean(centred * centred, axis=-1, keepdims=True) + 1e-05)
    return centred * inv, inv


def norm_back(v, gain, grad):
    r, inv = norm_stats(v)
    gr = grad * gain
    return inv * (
        gr - jnp.mean(gr, axis=-1, keepdims=True) - r * jnp.mean(gr * r, axis=-1, keepdims=True)
    )


def widen(a):
    return jnp.pad(a, ((0, 0), (0, WIDE - D)))


def lanes(rows):
    return lax.broadcasted_iota(jnp.int32, (rows, 128), 1)


def two_heads(block, single):
    low = lanes(block.shape[0]) < HEAD_DIM
    zero = jnp.zeros_like(block)
    first = jnp.where(low, block, zero)
    return first if single else jnp.concatenate([first, jnp.where(low, zero, block)], axis=0)


def one_block(stacked, single):
    rows = stacked.shape[0] if single else stacked.shape[0] // 2
    second = jnp.zeros_like(stacked) if single else stacked[rows:]
    return jnp.where(lanes(rows) < HEAD_DIM, stacked[:rows], second)


def pick_extra(rows, pair, single):
    spot = lanes(rows) - HEAD_DIM

    def of(h):
        return ((spot >= 3 * h) & (spot < 3 * h + 3)).astype(F32)

    head = 2 * pair
    return (of(head) if single else jnp.concatenate([of(head), of(head + 1)], axis=0)).astype(BF)


def heads_of_pair(pair):
    return 128 * pair, pair == PAIRS - 1


def gathered(own_ref, sib_ref, half, at):
    return jnp.concatenate(
        [ref[:, half, :, at : at + 128].reshape(4 * HALF, 128) for ref in (own_ref, sib_ref)], axis=0
    )


def row_terms(term):
    first = term.astype(BF).astype(F32)
    rest = term - first
    second = rest.astype(BF).astype(F32)
    third = rest - second
    turn = (lanes(term.shape[0]) - HEAD_DIM) % 3
    return jnp.where(turn == 0, first, jnp.where(turn == 1, second, third)).astype(BF)


def both(a, b):
    return jnp.concatenate([a, b], axis=0)


def fwd_kernel(q_ref, kv_own, kv_sib, lpos, lseg, kpos, kseg, ctx_ref, qe_ref):
    ok = (kpos[...] <= lpos[...]) & (kseg[...] == lseg[...])
    bias = jnp.where(ok, 0.0, NEG)
    bias = (both(bias[:HALF, : KEYS // 2], bias[:HALF, : KEYS // 2]), both(bias[HALF:], bias[HALF:]))
    spot = lanes(HALF) - HEAD_DIM
    terms = [jnp.zeros((HALF, 128), F32)] * 2
    for pair in range(PAIRS):
        at, single = heads_of_pair(pair)
        k_lo, k_hi = gathered(kv_own, kv_sib, 0, at), gathered(kv_own, kv_sib, 1, at)
        v_lo, v_hi = gathered(kv_own, kv_sib, 0, WIDE + at), gathered(kv_own, kv_sib, 1, WIDE + at)
        for half, keys, values in ((0, k_lo, v_lo), (1, both(k_lo, k_hi), both(v_lo, v_hi))):
            rows = two_heads(q_ref[half * HALF : (half + 1) * HALF, at : at + 128], single)
            s = dot_t(rows, keys) + bias[half][: rows.shape[0]]
            top = jnp.max(s, axis=1, keepdims=True)
            e = jnp.exp(s - top)
            total = jnp.sum(e, axis=1, keepdims=True)
            out = one_block(dot(e.astype(BF), values) * (1.0 / total), single)
            ctx_ref[half * HALF : (half + 1) * HALF, at : at + 128] = out.astype(BF)
            lse = top + jnp.log(total)
            for n in range(rows.shape[0] // HALF):
                head = 2 * pair + n
                mine = (spot >= 3 * head) & (spot < 3 * head + 3)
                terms[half] = jnp.where(mine, -lse[n * HALF : (n + 1) * HALF], terms[half])
    qe_ref[...] = q_ref[...]
    last = q_ref[:, WIDE - 128 :]
    qe_ref[:, WIDE - 128 :] = jnp.where(lanes(2 * HALF) < HEAD_DIM, last, row_terms(both(*terms)))


def dq_kernel(qe_ref, ge_ref, kv_own, kv_sib, lpos, lseg, kpos, kseg, gq_ref):
    ok = (kpos[...] <= lpos[...]) & (kseg[...] == lseg[...])
    bias = jnp.where(ok, 0.0, NEG)
    bias = (both(bias[:HALF, : KEYS // 2], bias[:HALF, : KEYS // 2]), both(bias[HALF:], bias[HALF:]))
    for pair in range(PAIRS):
        at, single = heads_of_pair(pair)
        k_lo, k_hi = gathered(kv_own, kv_sib, 0, at), gathered(kv_own, kv_sib, 1, at)
        v_lo, v_hi = gathered(kv_own, kv_sib, 0, WIDE + at), gathered(kv_own, kv_sib, 1, WIDE + at)
        mask = pick_extra(HALF, pair, single)
        for half, keys, values in ((0, k_lo, v_lo), (1, both(k_lo, k_hi), both(v_lo, v_hi))):
            place = slice(half * HALF, (half + 1) * HALF)
            ones = jnp.ones((keys.shape[0], 128), BF)

            def with_terms(ref):
                rows, extra = two_heads(ref[place, at : at + 128], single), ref[place, WIDE - 128 :]
                extra = extra if single else both(extra, extra)
                return jnp.concatenate([rows, extra * mask], axis=1)

            s = dot_t(with_terms(qe_ref), jnp.concatenate([keys, ones], axis=1))
            dp = dot_t(with_terms(ge_ref), jnp.concatenate([values, ones], axis=1))
            ds = (jnp.exp(s + bias[half][: s.shape[0]]) * dp).astype(BF)
            gq_ref[place, at : at + 128] = (one_block(dot(ds, keys), single) * 0.125).astype(BF)


def dkv_kernel(kv, q_own, q_sib, g_own, g_sib, lpos, lseg, kpos, kseg, gk_ref, gv_ref):
    ok = (lpos[...] <= kpos[...]) & (kseg[...] == lseg[...])
    bias = jnp.where(ok, 0.0, NEG)
    bias = (both(bias[:HALF], bias[:HALF]), both(bias[HALF:, KEYS // 2 :], bias[HALF:, KEYS // 2 :]))

    def queries(own, sib, at):
        lo, hi = gathered(own, sib, 0, at), gathered(own, sib, 1, at)
        return both(lo, hi), hi

    qx, gx = queries(q_own, q_sib, WIDE - 128), queries(g_own, g_sib, WIDE - 128)
    for pair in range(PAIRS):
        at, single = heads_of_pair(pair)
        q, g = queries(q_own, q_sib, at), queries(g_own, g_sib, at)
        terms = pick_extra(HALF, pair, single)
        for half in range(2):
            k = jnp.concatenate([two_heads(kv[half, :, at : at + 128], single), terms], axis=1)
            v = two_heads(kv[half, :, WIDE + at : WIDE + at + 128], single)
            v = jnp.concatenate([v, terms], axis=1)
            s = dot_t(k, jnp.concatenate([q[half], qx[half]], axis=1))
            p = jnp.exp(s + bias[half][: s.shape[0]])
            dp = dot_t(v, jnp.concatenate([g[half], gx[half]], axis=1))
            ds = (p * dp).astype(BF)
            gk_ref[half, :, at : at + 128] = one_block(dot(ds, q[half]), single).astype(BF)
            gv_ref[half, :, at : at + 128] = one_block(dot(p.astype(BF), g[half]), single).astype(BF)


ATTENTION_COST = pl.CostEstimate(
    flops=8_000_000_000, bytes_accessed=6 << 20, transcendentals=PAIRS * 256 * KEYS
)
PARAMS = pltpu.CompilerParams(vmem_limit_bytes=17 * 1024 * 1024)
HERE = pl.BlockSpec(memory_space=pltpu.VMEM)
ANYWHERE = pl.BlockSpec(memory_space=pl.ANY)
FLAT = jax.ShapeDtypeStruct((2 * HALF, WIDE), BF)


def attention_call(kernel, outs, *args):
    return pl.pallas_call(
        kernel,
        out_shape=outs,
        in_specs=[HERE] * len(args),
        out_specs=jax.tree.map(lambda _: HERE, outs),
        compiler_params=PARAMS,
        cost_estimate=ATTENTION_COST,
    )(*args)


def attend_fwd(q, kv_own, kv_sib, where):
    return attention_call(fwd_kernel, (FLAT, FLAT), q, kv_own, kv_sib, *where)


def attend_dq(qe, ge, kv_own, kv_sib, where):
    return attention_call(dq_kernel, FLAT, qe, ge, kv_own, kv_sib, *where)


def attend_dkv(kv, qe_own, qe_sib, ge_own, ge_sib, where):
    part = jax.ShapeDtypeStruct((2, HALF, WIDE), BF)
    return attention_call(dkv_kernel, (part, part), kv, qe_own, qe_sib, ge_own, ge_sib, *where)


FWD_PIECES = ((0, 1152), (1152, 2304), (2304, 3328), (3328, FF))
BACK_PIECES = ((0, FF // 2), (FF // 2, FF))
ROWS = 2 * HALF


def normalised(v):
    mean = jnp.mean(v, axis=1, keepdims=True)
    centred = v - mean
    inv = lax.rsqrt(jnp.mean(centred * centred, axis=1, keepdims=True) + 1e-05)
    return centred * inv, inv


def weight_copies(pieces, wout, wup, wdown, wout_here, wup_here, wdown_here, sems):
    out = pltpu.make_async_copy(wout, wout_here, sems.at[0])
    ups, downs = [], []
    for k, (a, b) in enumerate(pieces):
        ups.append(pltpu.make_async_copy(wup.at[:, a:b], wup_here.at[:, a:b], sems.at[1 + 2 * k]))
        downs.append(pltpu.make_async_copy(wdown.at[a:b, :], wdown_here.at[a:b, :], sems.at[2 + 2 * k]))
    return out, ups, downs


def mlp_fwd_kernel(
    ctx, hidden, gain, gain_next, a_o, b_o, a_u, b_d, b_u, a_d, wout, wup, wdown,
    middle, n2, low_o, low_u, low_d, after, n1_next
):
    x = ctx[:, :D]
    low = dot(x, a_o[...]).astype(BF)
    low_o[...] = low
    mid = hidden[...] + dot(x, wout[...]) + dot(low, b_o[...])
    middle[...] = mid
    normed = (normalised(mid)[0] * gain[...]).astype(BF)
    n2[...] = normed
    low = dot(normed, a_u[...]).astype(BF)
    low_u[...] = low
    total, total_low = jnp.zeros((ROWS, D), F32), jnp.zeros((ROWS, RANK), F32)
    for a, b in FWD_PIECES:
        up = dot(normed, wup[:, a:b]) + dot(low, b_u[:, a:b])
        act = (up * (0.5 * (1.0 + lax.erf(up * 0.7071067811865476)))).astype(BF)
        total = total + dot(act, wdown[a:b, :])
        total_low = total_low + dot(act, a_d[a:b, :])
    low = total_low.astype(BF)
    low_d[...] = low
    new = middle[...] + (total + dot(low, b_d[...]))
    after[...] = new
    n1_next[...] = (normalised(new)[0] * gain_next[...]).astype(BF)


def mlp_back_kernel(
    g, ctx, middle, gain, n2, low_o, low_u, low_d, a_o, b_o, a_u, b_d, spread, b_u, a_d, wout, wup, wdown,
    gh2, ge, ga_o, gb_o, ga_u, gb_d, ga_d, gb_u, wout_here, wup_here, wdown_here, sems
):
    out, ups, downs = weight_copies(BACK_PIECES, wout, wup, wdown, wout_here, wup_here, wdown_here, sems)
    for up, down in zip(ups, downs):
        up.start()
        down.start()
    out.start()
    gy = g[...].astype(BF)
    glow_d = dot_t(gy, b_d[...]).astype(BF)
    gb_d[...] = t_dot(low_d[...], gy).astype(BF)
    normed, low = n2[...], low_u[...]
    gn2, glow_u = jnp.zeros((ROWS, D), F32), jnp.zeros((ROWS, RANK), F32)
    for k, (a, b) in enumerate(BACK_PIECES):
        ups[k].wait()
        up = dot(normed, wup_here[:, a:b]) + dot(low, b_u[:, a:b])
        phi = 0.5 * (1.0 + lax.erf(up * 0.7071067811865476))
        ga_d[:, a:b] = t_dot(glow_d, (up * phi).astype(BF)).astype(BF)
        downs[k].wait()
        gact = dot_t(gy, wdown_here[a:b, :]) + dot_t(glow_d, a_d[a:b, :])
        density = jnp.exp(-0.5 * up * up) * 0.3989422804014327
        gup = (gact * (phi + up * density)).astype(BF)
        gb_u[:, a:b] = t_dot(low, gup).astype(BF)
        gn2 = gn2 + dot_t(gup, wup_here[:, a:b])
        glow_u = glow_u + dot_t(gup, b_u[:, a:b])
    glow_u = glow_u.astype(BF)
    gn2 = gn2 + dot_t(glow_u, a_u[...])
    ga_u[...] = t_dot(glow_u, normed).astype(BF)
    out.wait()
    through_norm(g, middle[...], gain, gn2, ctx[:, :D], low_o[...], a_o, b_o, wout_here, spread, gh2, ge, ga_o, gb_o)


def through_norm(g, middle, gain, gn2, x, low_o, a_o, b_o, wout, spread, gh2, ge, ga_o, gb_o):
    r, inv = normalised(middle)
    gr = gn2 * gain[...]
    grad = g[...] + inv * (
        gr - jnp.mean(gr, axis=1, keepdims=True) - r * jnp.mean(gr * r, axis=1, keepdims=True)
    )
    gh2[...] = grad
    gproj = grad.astype(BF)
    glow_o = dot_t(gproj, b_o[...]).astype(BF)
    ga_o[...] = t_dot(glow_o, x).astype(BF)
    gb_o[...] = t_dot(low_o, gproj).astype(BF)
    gctx = (dot_t(gproj, wout[...]) + dot_t(glow_o, a_o[...])).astype(BF)
    product = gctx.astype(F32) * x.astype(F32)
    first = product.astype(BF)
    second = (product - first.astype(F32)).astype(BF)
    delta = dot(first, spread[...]) + dot(second, spread[...])
    ge[:, :D] = gctx
    ge[:, D:] = row_terms(-delta)[:, HEAD_DIM:]


def qkv_back_kernel(
    gq, gk, gv, low, n1, a, b_q, b_kv, hidden, gain, gh2, wq, wkv, g, ga, gb_q, gb_kv, wq_here, wkv_here, sems
):
    first = pltpu.make_async_copy(wq, wq_here, sems.at[0])
    second = pltpu.make_async_copy(wkv, wkv_here, sems.at[1])
    first.start()
    second.start()
    q, k, v = gq[...], gk[...].reshape(ROWS, WIDE), gv[...].reshape(ROWS, WIDE)
    glow = dot_t(q, b_q[...]) + dot_t(k, b_kv[:, :WIDE]) + dot_t(v, b_kv[:, WIDE:])
    glow = glow.astype(BF)
    ga[...] = t_dot(glow, n1[...]).astype(BF)
    gb_q[...] = t_dot(low[...], q).astype(BF)
    gb_kv[:, :WIDE] = t_dot(low[...], k).astype(BF)
    gb_kv[:, WIDE:] = t_dot(low[...], v).astype(BF)
    first.wait()
    gn1 = dot_t(q, wq_here[...])
    second.wait()
    gn1 = gn1 + dot_t(k, wkv_here[:, :WIDE]) + dot_t(v, wkv_here[:, WIDE:]) + dot_t(glow, a[...])
    r, inv = normalised(hidden[...])
    gr = gn1 * gain[...]
    g[...] = gh2[...] + inv * (
        gr - jnp.mean(gr, axis=1, keepdims=True) - r * jnp.mean(gr * r, axis=1, keepdims=True)
    )


def mlp_both_kernel(
    ctx, hidden, gain, g, a_o, b_o, a_u, b_d, spread, b_u, a_d, wout, wup, wdown,
    after, gh2, ge, ga_o, gb_o, ga_u, gb_d, ga_d, gb_u
):
    x = ctx[:, :D]
    low_o = dot(x, a_o[...]).astype(BF)
    gh2[...] = hidden[...] + dot(x, wout[...]) + dot(low_o, b_o[...])
    normed = (normalised(gh2[...])[0] * gain[...]).astype(BF)
    low = dot(normed, a_u[...]).astype(BF)
    gy = g[...].astype(BF)
    glow_d = dot_t(gy, b_d[...]).astype(BF)
    total, total_low = jnp.zeros((ROWS, D), F32), jnp.zeros((ROWS, RANK), F32)
    gn2, glow_u = jnp.zeros((ROWS, D), F32), jnp.zeros((ROWS, RANK), F32)
    for a, b in BACK_PIECES:
        up = dot(normed, wup[:, a:b]) + dot(low, b_u[:, a:b])
        phi = 0.5 * (1.0 + lax.erf(up * 0.7071067811865476))
        act = (up * phi).astype(BF)
        ga_d[:, a:b] = t_dot(glow_d, act).astype(BF)
        total = total + dot(act, wdown[a:b, :])
        total_low = total_low + dot(act, a_d[a:b, :])
        gact = dot_t(gy, wdown[a:b, :]) + dot_t(glow_d, a_d[a:b, :])
        density = jnp.exp(-0.5 * up * up) * 0.3989422804014327
        gup = (gact * (phi + up * density)).astype(BF)
        gb_u[:, a:b] = t_dot(low, gup).astype(BF)
        gn2 = gn2 + dot_t(gup, wup[:, a:b])
        glow_u = glow_u + dot_t(gup, b_u[:, a:b])
    low_d = total_low.astype(BF)
    gb_d[...] = t_dot(low_d, gy).astype(BF)
    after[...] = (gh2[...] + (total + dot(low_d, b_d[...]))).astype(BF)
    glow_u = glow_u.astype(BF)
    gn2 = gn2 + dot_t(glow_u, a_u[...])
    ga_u[...] = t_dot(glow_u, normed).astype(BF)
    through_norm(g, gh2[...], gain, gn2, x, low_o, a_o, b_o, wout, spread, gh2, ge, ga_o, gb_o)


def shape_of(rows, width, kind=BF):
    return jax.ShapeDtypeStruct((rows, width), kind)


def mlp_call(kernel, args, outs, flops, weights=0, limit=24):
    scratch = [
        pltpu.VMEM((D, D), BF),
        pltpu.VMEM((D, FF), BF),
        pltpu.VMEM((FF, D), BF),
        pltpu.SemaphoreType.DMA((1 + 2 * len(BACK_PIECES),)),
    ]
    return pl.pallas_call(
        kernel,
        out_shape=outs,
        in_specs=[HERE] * (len(args) - weights) + [ANYWHERE] * weights,
        out_specs=(HERE,) * len(outs),
        scratch_shapes=scratch if weights else (),
        compiler_params=pltpu.CompilerParams(vmem_limit_bytes=limit * 1024 * 1024),
        cost_estimate=pl.CostEstimate(flops=flops, bytes_accessed=24 << 20, transcendentals=ROWS * FF),
    )(*args)


def mlp_fwd(*args):
    outs = (shape_of(ROWS, D, F32), shape_of(ROWS, D)) + (shape_of(ROWS, RANK),) * 3
    outs += (shape_of(ROWS, D, F32), shape_of(ROWS, D))
    return mlp_call(mlp_fwd_kernel, args, outs, 10_000_000_000, limit=12)


def mlp_both(*args):
    outs = (shape_of(ROWS, D), shape_of(ROWS, D, F32), shape_of(ROWS, WIDE)) + (shape_of(RANK, D),) * 4
    outs += (shape_of(RANK, FF),) * 2
    return mlp_call(mlp_both_kernel, args, outs, 18_000_000_000, limit=20)


def mlp_back(*args):
    outs = (shape_of(ROWS, D, F32), shape_of(ROWS, WIDE)) + (shape_of(RANK, D),) * 4
    outs += (shape_of(RANK, FF),) * 2
    return mlp_call(mlp_back_kernel, args, outs, 16_000_000_000, 3, 56)


def qkv_back(*args):
    return pl.pallas_call(
        qkv_back_kernel,
        out_shape=(shape_of(ROWS, D, F32), shape_of(RANK, D), shape_of(RANK, WIDE), shape_of(RANK, 2 * WIDE)),
        in_specs=[HERE] * 11 + [ANYWHERE] * 2,
        out_specs=(HERE,) * 4,
        scratch_shapes=[
            pltpu.VMEM((D, WIDE), BF),
            pltpu.VMEM((D, 2 * WIDE), BF),
            pltpu.SemaphoreType.DMA((2,)),
        ],
        compiler_params=pltpu.CompilerParams(vmem_limit_bytes=20 * 1024 * 1024),
        cost_estimate=pl.CostEstimate(flops=5_000_000_000, bytes_accessed=10 << 20, transcendentals=0),
    )(*args)


def ring_start(block):
    return lax.ppermute(block, "seq", UP), lax.ppermute(block, "seq", DOWN)


def ring_far(block, before, after, beside=()):
    far_lo = lax.ppermute(before[0], "seq", UP)
    far_hi = lax.ppermute(after[1], "seq", DOWN)
    far_lo, far_hi, *beside = tie(far_lo, far_hi, *beside)
    own = jnp.stack([block, before, after, jnp.stack([far_lo, far_hi])])
    return (own, *beside) if beside else own


def other_core(own):
    return lax.ppermute(own, "seq", CORE)


def sum_sequence(parts, core, y):
    parts = parts.reshape((4, 2) + parts.shape[1:])
    mine = lax.dynamic_index_in_dim(parts, core, 1, keepdims=False)
    other = lax.dynamic_index_in_dim(parts, 1 - core, 1, keepdims=False)
    half = mine.astype(F32) + lax.ppermute(other, "seq", CORE).astype(F32)

    def of(step):
        return lax.dynamic_index_in_dim(half, (y + step) % 4, 0, keepdims=False)

    total = of(0)
    for step, route in ((1, UP), (3, DOWN), (2, FAR)):
        total = total + lax.ppermute(of(step).astype(BF), "seq", route).astype(F32)
    return total


def tie(*values):
    return lax.optimization_barrier(values)


def eighths(turned, straight):
    def cut(a, part):
        return jnp.pad(a, ((0, 0), (0, 8 * part - a.shape[1]))).reshape(RANK, 8, part)

    first = cut(jnp.concatenate(turned, axis=1), PART_A)
    return jnp.swapaxes(jnp.concatenate([first, cut(straight, PART_B)], axis=2), 0, 1)


def by_adapter_kernel(picks, *refs):
    parts, out_ref, acc = refs[:-2], refs[-2], refs[-1]
    acc[...] = jnp.zeros_like(acc)
    at = 0
    for ref in parts:
        for k in range(ref.shape[0]):
            rows = pl.ds(pl.multiple_of(picks[at] * RANK, RANK), RANK)
            acc[rows, :] = acc[rows, :] + ref[k].astype(F32)
            at += 1
    for j in range(PART // 128):
        square = acc[:, 128 * j : 128 * (j + 1)]
        square = square.T if 128 * j < PART_A else square
        out_ref[128 * j : 128 * (j + 1), :] = square.astype(BF)


def by_adapter(parts, picks):
    return pl.pallas_call(
        by_adapter_kernel,
        out_shape=jax.ShapeDtypeStruct((PART, 128), BF),
        in_specs=[pl.BlockSpec(memory_space=pltpu.SMEM)]
        + [pl.BlockSpec(memory_space=pltpu.VMEM)] * len(parts),
        out_specs=pl.BlockSpec(memory_space=pltpu.VMEM),
        scratch_shapes=[pltpu.VMEM((8 * RANK, PART), F32)],
        compiler_params=PARAMS,
        cost_estimate=pl.CostEstimate(flops=16 * RANK * PART, bytes_accessed=2 << 20, transcendentals=0),
    )(picks, *parts)


def unfold_rows(layer, rows, outs):
    turned, straight = outs[:-1], outs[-1]
    start = 0
    for out, width in zip(turned, TURNED):
        at = start
        while at < start + width:
            n = min(start + width, (at // PART_A + 1) * PART_A) - at
            out[layer, at - start : at - start + n, :] = rows(at // PART_A, at % PART_A, n)
            at += n
        start += width
    squares = PART_B // 128
    for t in range(FF // 128):
        value = rows(t // squares, PART_A + 128 * (t % squares), 128)
        straight[layer, :, 128 * t : 128 * (t + 1)] = value


def unfold_late_kernel(ref, *outs):
    unfold_rows(0, lambda e, at, n: ref[e, at : at + n, :].astype(F32), outs)


def unfold_kernel(place, own_ref, sib_ref, *refs):
    half = len(refs) // 2

    def rows(e, at, n):
        k = place[e]
        mine = own_ref[k % 4, at : at + n, :]
        other = sib_ref[k % 4, at : at + n, :]
        return jnp.where(k < 4, mine.astype(F32), other.astype(F32))

    unfold_rows(0, rows, refs[half:])


def one_layer(layer, *shape):
    return pl.BlockSpec((1,) + shape, lambda i: (layer, 0, 0))


def unfold(kernel, layer, *args):
    shapes = [(w, 128) for w in TURNED] + [(128, FF)]
    whole = [jax.ShapeDtypeStruct((2,) + shape, F32) for shape in shapes]
    first, earlier = (args, ()) if layer == 1 else (args[:3], args[3])
    specs = [pl.BlockSpec(memory_space=pltpu.SMEM)] if layer == 0 else []
    specs += [fixed(*a.shape) for a in first[len(specs) :]] + [ANYWHERE] * len(earlier)
    return pl.pallas_call(
        kernel,
        grid=(1,),
        out_shape=tuple(whole),
        in_specs=specs,
        out_specs=tuple(one_layer(layer, *shape) for shape in shapes),
        input_output_aliases={3 + n: n for n in range(len(earlier))},
        compiler_params=pltpu.CompilerParams(vmem_limit_bytes=40 * 1024 * 1024),
        cost_estimate=pl.CostEstimate(flops=0, bytes_accessed=14 << 20, transcendentals=0),
    )(*first, *earlier)


def fixed(*shape):
    return pl.BlockSpec(shape, lambda i: (0,) * len(shape))


def share(w_qkv, w_out, w_up, w_down, z_lo, spare):
    def half_row(w, front, lines):
        size = lines * 128 - w.shape[1]
        first = jnp.pad(w, ((0, 0), (0, size)))
        second = jnp.pad(w, ((0, 0), (front, size - front)))
        return jnp.where(z_lo == 0, first, second).reshape(-1, lines, 128)

    def put(a, room):
        return jnp.pad(a, ((0, 0), (0, room - a.shape[1]), (0, 0)))

    extra = jnp.broadcast_to(spare[None], (2, 1, 128))
    attention = [
        put(half_row(w_qkv, 32, N_QKV), AT_OUT),
        put(half_row(w_out, 32, N_OUT), LINES - AT_OUT - 1),
        extra,
    ]
    up, down = put(w_up.reshape(-1, N_UP, 128), LINES), put(w_down.reshape(-1, N_DOWN, 128), LINES - 1)
    return jnp.concatenate(attention, axis=1), jnp.concatenate([up, down, extra], axis=1)


def spin(a):
    return pltpu.roll(a, HEAD_DIM, 1)


def fill(ref, base, lines):
    ref[pl.ds(base, lines.shape[0], stride=2), :] = lines


def between(ref, base, n):
    now, later = ref[pl.ds(base, n, stride=2), :], ref[pl.ds(base + 2, n, stride=2), :]
    ref[pl.ds(base + 1, n, stride=2), :] = spin(jnp.where(lanes(n) < HEAD_DIM, later, now))


def columns(ref, dst, to, start, units, step=2):
    got = ref[pl.ds(start, dst.shape[0], stride=units), :].astype(BF)
    n = min(128, dst.shape[1] - to)
    dst[:, to : to + n] = got[:, :n]


def lines_of(ref, pair, zl, start, n):
    return ref[0, zl, 0, pair % 4, pair // 4, start : start + n, :].astype(F32)


def unpack_attention_kernel(g_ref, *refs):
    def lines(pair, zl):
        return lines_of(g_ref, pair, zl, 0, N_QKV), lines_of(g_ref, pair, zl, AT_OUT, N_OUT)

    unpack_attention_lines(lines, *refs)


def unpack_first_kernel(steps, own_1, sib_1, own_2, sib_2, *refs):
    def lines(pair, zl):
        x, core = pair % 4, pair // 4
        z_at, x_at = steps[4 + 2 * (pl.program_id(0) // 4) + zl], steps[8 + x]
        mine = steps[12] == core
        top = jnp.where(mine, own_1[z_at, 0, x_at], sib_1[z_at, 0, x_at])
        bottom = jnp.where(mine, own_2[0, z_at, x_at], sib_2[0, z_at, x_at])
        both = jnp.concatenate([top.astype(F32), bottom.astype(F32)], axis=0)
        return both[:N_QKV], both[AT_OUT : AT_OUT + N_OUT]

    unpack_attention_lines(lines, *refs)


def unpack_attention_lines(lines, q_ref, kv_ref, out_ref, s_qkv, s_out):
    low = lanes(1) < HEAD_DIM
    zero = jnp.zeros((1, 128), F32)
    for pair in range(8):
        (qkv0, out0), (qkv1, out1) = lines(pair, 0), lines(pair, 1)
        base, base_out = pair * 867, pair * 289
        fill(s_qkv, base, qkv0)
        fill(s_qkv, base + 433, qkv1)
        between(s_qkv, base, N_QKV - 1)
        between(s_qkv, base + 433, N_QKV)
        s_qkv[pl.ds(base + 432, 1), :] = qkv0[N_QKV - 1 :] + spin(jnp.where(low, qkv1[:1], zero))
        s_qkv[pl.ds(base + 433, 1), :] = qkv1[:1] + spin(jnp.where(low, zero, qkv0[N_QKV - 1 :]))
        fill(s_out, base_out, out0)
        fill(s_out, base_out + 144, out1)
        s_out[pl.ds(base_out + 144, 1), :] = out0[N_OUT - 1 :] + out1[:1]
        between(s_out, base_out, N_OUT - 1)
        between(s_out, base_out + 144, N_OUT - 1)
    half = lanes(BLOCK) < HEAD_DIM
    for dst, to, first in ((q_ref, 0, 0), (kv_ref, 0, 17), (kv_ref, WIDE, 34)):
        for j in range(8):
            columns(s_qkv, dst, to + 128 * j, first + 2 * j, 51)
        got = s_qkv[pl.ds(first + 16, BLOCK, stride=51), :]
        dst[:, to + D - HEAD_DIM : to + WIDE] = jnp.where(half, got, 0.0).astype(BF)
    for j in range(9):
        columns(s_out, out_ref, 128 * j, 2 * j, 17)


def unpack_mlp_kernel(g_up, g_down, up_ref, down_ref, s_up, s_down):
    for pair in range(8):
        for zl in range(2):
            at = pair * 2 + zl
            s_up[pl.ds(at * N_UP, N_UP), :] = lines_of(g_up, pair, zl, 0, N_UP)
            fill(s_down, at * 2 * N_DOWN, lines_of(g_down, pair, zl, 0, N_DOWN))
    for at in range(16):
        between(s_down, at * 2 * N_DOWN, N_DOWN)
    for j in range(34):
        columns(s_up, up_ref, 128 * j, j, 34)
    for j in range(9):
        columns(s_down, down_ref, 128 * j, 2 * j, 17)


def unpack(kernel, got, at, outs, scratch_lines, limit):
    g = got.reshape(2, 2, 4, 4, 2, -1, 128)

    def spec(k):
        return pl.BlockSpec((1, 2, 1, 4, 2, LINES, 128), lambda i: (i // 4, 0, i % 4, 0, 0, k, 0))

    return pl.pallas_call(
        kernel,
        grid=(8,),
        out_shape=tuple(jax.ShapeDtypeStruct((8 * r, w), BF) for r, w in outs),
        in_specs=[spec(k) for k in at],
        out_specs=tuple(pl.BlockSpec((r, w), lambda i: (i, 0)) for r, w in outs),
        scratch_shapes=[pltpu.VMEM((n, 128), F32) for n in scratch_lines],
        compiler_params=pltpu.CompilerParams(vmem_limit_bytes=limit * 1024 * 1024),
        cost_estimate=pl.CostEstimate(
            flops=0, bytes_accessed=len(at) * (20 << 20), transcendentals=0
        ),
    )(*[g] * len(at))


ATTENTION_OUTS = [(BLOCK, WIDE), (BLOCK, 2 * WIDE), (BLOCK, D)]
ATTENTION_LINES = [8 * 867 + 8, 8 * 289 + 8]


def unpack_attention(got, at):
    return unpack(unpack_attention_kernel, got, [at], ATTENTION_OUTS, ATTENTION_LINES, 36)


def along(axis, block, near):
    name, shift = SHIFTS[axis]
    before = lax.ppermute(block, name, shift(1))
    after = lax.ppermute(block, name, shift(-1))
    if near:
        far = lax.ppermute(block, name, shift(2))
    else:
        n = block.shape[0] // 2
        far = [lax.ppermute(before[:n], name, shift(1)), lax.ppermute(after[n:], name, shift(-1))]
        far = jnp.concatenate(far)
    return jnp.stack([block, before, after, far])


def gather_first(share, later):
    n = LINES // 2
    row = along("x", share, True)
    one, two = along("y", row[:, :n], True), along("z", row[:, n:], True)
    one, two, later = tie(one, two, later)
    one, two = along("z", one, False), along("y", two, False)
    return (one, other_core(one), two, other_core(two)), later


def unpack_first(one, sib_one, two, sib_two, steps):
    n = LINES // 2
    spec_one = pl.BlockSpec((4, 1, 4, n, 128), lambda i, steps: (0, steps[i % 4], 0, 0, 0))
    spec_two = pl.BlockSpec((1, 4, 4, n, 128), lambda i, steps: (steps[i % 4], 0, 0, 0, 0))
    return pl.pallas_call(
        unpack_first_kernel,
        grid_spec=pltpu.PrefetchScalarGridSpec(
            num_scalar_prefetch=1,
            grid=(8,),
            in_specs=[spec_one, spec_one, spec_two, spec_two],
            out_specs=tuple(pl.BlockSpec((r, w), lambda i, steps: (i, 0)) for r, w in ATTENTION_OUTS),
            scratch_shapes=[pltpu.VMEM((n, 128), F32) for n in ATTENTION_LINES],
        ),
        out_shape=tuple(jax.ShapeDtypeStruct((8 * r, w), BF) for r, w in ATTENTION_OUTS),
        compiler_params=pltpu.CompilerParams(vmem_limit_bytes=26 * 1024 * 1024),
        cost_estimate=pl.CostEstimate(flops=0, bytes_accessed=30 << 20, transcendentals=0),
    )(steps, one, sib_one, two, sib_two)


def unpack_mlp(got, at):
    outs = [(BLOCK, FF), (4 * BLOCK, D)]
    return unpack(unpack_mlp_kernel, got, [at, at + 1], outs, [16 * N_UP, 32 * N_DOWN + 8], 20)


def shards(
    tokens, segments, adapter_pick, norm_gain, w_qkv, w_out, w_up, w_down,
    a_qkv, b_qkv, a_out, b_out, a_up, b_up, a_down, b_down, grad_out
):
    layers = norm_gain.shape[0]
    index = lax.axis_index("seq")
    z_hi, place = index // 8, index % 8
    core, y = place % 2, place // 2

    def halves(own, other):
        return jnp.where(z_hi == 0, jnp.stack([own, other]), jnp.stack([other, own]))

    def mine(a):
        return lax.dynamic_index_in_dim(a, z_hi, 0, keepdims=False)

    def theirs(a):
        return lax.dynamic_index_in_dim(a, 1 - z_hi, 0, keepdims=False)

    batch = lax.axis_index("batch")
    spare = (segments.reshape(1, 128), jnp.pad(adapter_pick[None], ((0, 0), (0, 126))))
    attention, _ = share(w_qkv, w_out, w_up, w_down, batch % 2, spare[0].astype(BF))
    _, mlp = share(w_qkv, w_out, w_up, w_down, batch % 2, spare[1].astype(BF))

    def gather(a):
        return lax.all_gather(a, BOTH, axis=0, tiled=True, axis_index_groups=ALL)

    early = gather(jnp.concatenate([mlp[0], attention[1]], axis=0))
    late = gather(mlp[1])
    raw = (a_qkv, b_qkv, a_out, b_out, a_up, b_up, a_down, b_down, norm_gain)
    (one, sib_one, two, sib_two), raw = gather_first(attention[0], raw)
    a_qkv, b_qkv, a_out, b_out, a_up, b_up, a_down, b_down, norm_gain = raw

    sent = lax.ppermute(jnp.stack([theirs(tokens), theirs(grad_out)]), "seq", SWAP)
    hidden = halves(mine(tokens), sent[0]).reshape(2 * HALF, D).astype(F32)
    grad_hidden = halves(mine(grad_out), sent[1]).reshape(2 * HALF, D).astype(F32)
    pick = mine(adapter_pick)

    def segments_of(two):
        lines = two[:, :, 0, -1]
        lines = jnp.stack([lines[:, 0], lines[:, 3]])
        return lax.dynamic_slice(lines, (0, 0, z_hi * HALF), (2, 4, HALF))

    seg = jnp.stack([segments_of(two), segments_of(sib_two)], axis=1)
    seg = jnp.where(z_hi == 0, seg, seg[::-1]).astype(jnp.int32)
    offset = jnp.arange(HALF, dtype=jnp.int32)
    start = jnp.array([0, KEYS // 2], jnp.int32)[:, None]
    lpos = (start + place * HALF + offset[None]).reshape(2 * HALF, 1)
    lseg = seg[:, 0, 0].reshape(2 * HALF, 1)
    ys = (y + jnp.array([0, 3, 1, 2], jnp.int32)) % 4
    order = jnp.concatenate([2 * ys + core, 2 * ys + 1 - core])
    kpos = (start[:, :, None] + (order * HALF)[None, :, None] + offset).reshape(1, KEYS)
    where = (lpos, lseg, kpos, seg.reshape(1, KEYS))

    z_lo, x = batch % 2, batch // 2
    z = z_hi * 2 + z_lo
    picks = early.reshape(2, 2, 4, 4, 2, -1, 128)[0, :, 0, :, 0, 2 * LINES - 1, :2].astype(jnp.int32)
    picks = jnp.swapaxes(picks, 0, 1).reshape(16)
    steps = jnp.array([0, 3, 1, 2], jnp.int32)

    def sequence(zs, xs):
        return 2 * (2 * xs + zs % 2) + zs // 2

    four = jnp.arange(4, dtype=jnp.int32)
    picks_in_order = jnp.take(picks, sequence(four[:, None], four[None, :]).reshape(16))
    zs, xs = (z + steps) % 4, (x + steps) % 4
    picks_by_step = jnp.take(picks, sequence(zs[None, :], xs[:, None]).reshape(16))
    eight = jnp.arange(8, dtype=jnp.int32)
    back = jnp.array([0, 2, 3, 1], jnp.int32)
    place_by_step = 4 * ((eight % 2) ^ core) + jnp.take(back, (eight // 2 - y) % 4)
    arrival = [jnp.take(back, (four - at) % 4) for at in (y, z, x)]
    arrival = jnp.concatenate(arrival + [core[None]]).astype(jnp.int32)

    def low_in(a, l):
        return lax.dynamic_slice_in_dim(a[l], pick * RANK, RANK, 1)

    def low_out(b, l):
        return lax.dynamic_slice_in_dim(b[l], pick * RANK, RANK, 0)

    heads_of = (jnp.arange(D, dtype=jnp.int32) // HEAD_DIM)[:, None]
    spread = (heads_of == (jnp.arange(128, dtype=jnp.int32)[None, :] - HEAD_DIM) // 3).astype(BF)

    def adapters(l):
        b_first = low_out(b_qkv, l)
        b_kv = jnp.concatenate([widen(b_first[:, D : 2 * D]), widen(b_first[:, 2 * D :])], axis=1)
        rest = [f(a, l) for pair in ((a_out, b_out), (a_up, b_up), (a_down, b_down)) for f, a in zip((low_in, low_out), pair)]
        return [low_in(a_qkv, l), widen(b_first[:, :D]), b_kv] + rest

    n1 = (norm_stats(hidden)[0] * norm_gain[0, 0]).astype(BF)
    ahead = (where, spread, n1, grad_hidden, [adapters(l) for l in range(layers)])
    sib_one, (where, spread, n1, grad_hidden, adapter_parts) = tie(sib_one, ahead)
    first = unpack_first(one, sib_one, two, sib_two, arrival)
    saved, queries = [], []
    for l in range(layers):
        a_first, b_q, b_kv, a_o, b_o, a_u, b_u, a_d, b_d = adapter_parts[l]
        wq, wkv, wout = first
        low_qkv = dot(n1, a_first).astype(BF)
        kv = (dot(n1, wkv) + dot(low_qkv, b_kv)).astype(BF).reshape(2, HALF, 2 * WIDE)
        q = (dot(n1, wq) + dot(low_qkv, b_q)).astype(BF) * jnp.asarray(0.125, BF)
        before, after = ring_start(kv)
        if l == 0:
            before, after, q, wup, wdown = tie(before, after, q, *unpack_mlp(early, 0))
        else:
            before, after, q, late = tie(before, after, q, late)
        if l == 0:
            kv_own, *first = ring_far(kv, before, after, unpack_attention(early, 2))
        else:
            kv_own, wup, wdown = ring_far(kv, before, after, unpack_mlp(late, 0))
        kv_sib = other_core(kv_own)
        ctx, qe = attend_fwd(q, kv_own, kv_sib, where)
        queries.append(qe.reshape(2, HALF, WIDE))
        gains = norm_gain[l, 1][None], norm_gain[(l + 1) % layers, 0][None]
        small, large = (a_o, b_o, a_u, b_d), (b_u, a_d, wout, wup, wdown)
        rows, hidden_next, n1_next = None, None, None
        if l < layers - 1:
            middle, n2, low_o, low_u, low_d, hidden_next, n1_next = mlp_fwd(ctx, hidden, *gains, *small, *large)
            rows = (ctx, middle, gains[0], n2, low_o, low_u, low_d)
        else:
            starts = [ring_start(a) for a in queries]
            result, *back = mlp_both(ctx, hidden, gains[0], grad_hidden, *small, spread, *large)
            starts, back = tie(starts, back)
            queries = [ring_far(a, *start) for a, start in zip(queries, starts)]
        saved.append(
            (hidden, n1, low_qkv, kv, kv_own, kv_sib, qe)
            + (rows, small, large, a_first, b_q, b_kv, wq, wkv)
        )
        hidden, n1 = hidden_next, n1_next

    behind = None
    for l in reversed(range(layers)):
        hidden_in, n1, low_qkv, kv, kv_own, kv_sib, qe, rows, small, large, a_first, b_q, b_kv, wq, wkv = saved[l]
        if l < layers - 1:
            back = mlp_back(g, *rows, *small, spread, *large)
        gh2, ge, ga_o, gb_o, ga_u, gb_d, ga_d, gb_u = back
        if l == layers - 1:
            queries, ge = tie(queries, ge)
        qe_own, qe_sib = queries[l], other_core(queries[l])
        g_block = ge.reshape(2, HALF, WIDE)
        g_before, g_after = ring_start(g_block)
        if behind is not None:
            behind, ge = tie(behind, ge)
            behind = lax.all_gather(behind, BOTH, axis=0, axis_index_groups=SAME_PLACE)
        gq = attend_dq(qe, ge, kv_own, kv_sib, where)
        g_before, g_after, gq = tie(g_before, g_after, gq)
        ge_own = ring_far(g_block, g_before, g_after)
        ge_sib = other_core(ge_own)
        gk, gv = attend_dkv(kv, qe_own, qe_sib, ge_own, ge_sib, where)
        g, ga_q, gb_q, gb_kv = qkv_back(
            gq, gk, gv, low_qkv, n1, a_first, b_q, b_kv, hidden_in, norm_gain[l, 0][None], gh2, wq, wkv
        )
        gb_q = [gb_q[:, :D], gb_kv[:, :D], gb_kv[:, WIDE : WIDE + D]]
        parts = eighths([ga_q, ga_o, ga_u, ga_d] + gb_q + [gb_o, gb_d], gb_u)
        if l > 0:
            parts, g = tie(parts, g)
            behind = sum_sequence(parts, core, y)

    got = lax.all_to_all(parts, BOTH, 0, 0, axis_index_groups=SAME_SEQUENCE)
    part = jnp.sum(got.astype(F32), axis=0).astype(BF)
    along_z = [lax.ppermute(part, BOTH, z_shift(by)) for by in (1, -1, 2)]
    behind, part = tie(behind, part)
    one = by_adapter([behind], picks_in_order)
    one, *along_z = tie(one, *along_z)
    one = lax.all_gather(one, BOTH, axis=0, axis_index_groups=SAME_SEQUENCE)
    along_z = jnp.stack([part] + along_z)
    before = lax.ppermute(along_z, "batch", x_shift(1))
    after = lax.ppermute(along_z, "batch", x_shift(-1))
    sent_home = theirs(g.reshape(2, HALF, D)), theirs(result.reshape(2, HALF, D))
    back_home = [lax.ppermute(a, "seq", SWAP) for a in sent_home]
    far = [lax.ppermute(before[:2], "batch", x_shift(1)), lax.ppermute(after[2:], "batch", x_shift(-1))]
    whole = by_adapter([along_z, before, after] + far, picks_by_step)
    whole = whole.reshape(2, -1, 128)
    own = ring_far(whole, *ring_start(whole))
    one = unfold(unfold_late_kernel, 1, one)
    grad_tokens = halves(mine(g.reshape(2, HALF, D)), back_home[0])
    result = halves(mine(result.reshape(2, HALF, D)), back_home[1])
    own, grad_tokens, result, *one = tie(own, grad_tokens, result, *one)
    sib = other_core(own).reshape(4, PART, 128)
    ga_q, ga_o, ga_u, ga_d, gb_q, gb_o, gb_d, gb_u = unfold(
        unfold_kernel, 0, place_by_step, own.reshape(4, PART, 128), sib, one
    )
    gb_q, gb_o, gb_d = (jnp.swapaxes(a, 1, 2) for a in (gb_q, gb_o, gb_d))

    return result, grad_tokens, ga_q, gb_q, ga_o, gb_o, ga_u, gb_u, ga_d, gb_d


def solution(mesh):
    rows, flat, whole = P("batch", "seq", None), P(None, ("seq", "batch")), P()
    in_specs = (rows, P("batch", "seq"), P("batch"), whole) + (flat,) * 4 + (whole,) * 8 + (rows,)
    out_specs = (rows, rows) + (whole,) * 8
    return jax.shard_map(shards, mesh=mesh, in_specs=in_specs, out_specs=out_specs, check_vma=False)
```

```python
import jax
import jax.numpy as jnp
from jax import lax
from jax.experimental import pallas as pl
from jax.experimental.pallas import tpu as pltpu
from jax.sharding import PartitionSpec as P

D = 1088
HEADS = 17
HEAD_DIM = 64
FF = 4352
RANK = 16
WIDE = 1152
PAIRS = 9
HALF = 64
KEYS = 1024
BF = jnp.bfloat16
F32 = jnp.float32
NEG = -1e30

SWAP = [(i, i ^ 8) for i in range(16)]
CORE = [(i, i ^ 1) for i in range(16)]
UP = [(i, (i & 8) | ((i + 2) & 7)) for i in range(16)]
DOWN = [(i, (i & 8) | ((i - 2) & 7)) for i in range(16)]
FAR = [(i, (i & 8) | ((i + 4) & 7)) for i in range(16)]
def at_chip(z, y, x, core):
    return ((z // 2 * 4 + y) * 2 + core) * 8 + x * 2 + z % 2


ALL = [[at_chip(z, y, x, c) for z in range(4) for y in range(4) for x in range(4) for c in range(2)]]
SAME_SEQUENCE = [[at_chip(z, y, x, c) for y in range(4) for c in range(2)] for z in range(4) for x in range(4)]
SAME_PLACE = [[at_chip(z, y, x, c) for z in range(4) for x in range(4)] for y in range(4) for c in range(2)]


def z_shift(by):
    return [
        (at_chip(z, y, x, c), at_chip((z + by) % 4, y, x, c))
        for z in range(4) for y in range(4) for x in range(4) for c in range(2)
    ]


def x_shift(by):
    return [(i, (i + 2 * by) % 8) for i in range(8)]


def y_shift(by):
    return [(i, (i & 8) | ((i + 2 * by) & 7)) for i in range(16)]


BOTH = ("seq", "batch")
SHIFTS = {"x": ("batch", x_shift), "y": ("seq", y_shift), "z": (BOTH, z_shift)}
TURNED = (D, D, D, FF, 3 * D, D, D)
PART_A, PART_B = 1664, 640
PART = PART_A + PART_B

LINES = 304
AT_OUT = 224
N_QKV, N_OUT, N_UP, N_DOWN = 217, 73, 289, 289
BLOCK = 136


def dot(a, b):
    return jnp.dot(a, b, preferred_element_type=F32)


def dot_t(a, b):
    return lax.dot_general(a, b, (((1,), (1,)), ((), ())), preferred_element_type=F32)


def t_dot(a, b):
    return lax.dot_general(a, b, (((0,), (0,)), ((), ())), preferred_element_type=F32)


def norm_stats(v):
    mean = jnp.mean(v, axis=-1, keepdims=True)
    centred = v - mean
    inv = lax.rsqrt(jnp.mean(centred * centred, axis=-1, keepdims=True) + 1e-05)
    return centred * inv, inv


def norm_back(v, gain, grad):
    r, inv = norm_stats(v)
    gr = grad * gain
    return inv * (
        gr - jnp.mean(gr, axis=-1, keepdims=True) - r * jnp.mean(gr * r, axis=-1, keepdims=True)
    )


def widen(a):
    return jnp.pad(a, ((0, 0), (0, WIDE - D)))


def lanes(rows):
    return lax.broadcasted_iota(jnp.int32, (rows, 128), 1)


def two_heads(block, single):
    low = lanes(block.shape[0]) < HEAD_DIM
    zero = jnp.zeros_like(block)
    first = jnp.where(low, block, zero)
    return first if single else jnp.concatenate([first, jnp.where(low, zero, block)], axis=0)


def one_block(stacked, single):
    rows = stacked.shape[0] if single else stacked.shape[0] // 2
    second = jnp.zeros_like(stacked) if single else stacked[rows:]
    return jnp.where(lanes(rows) < HEAD_DIM, stacked[:rows], second)


def pick_extra(rows, pair, single):
    spot = lanes(rows) - HEAD_DIM

    def of(h):
        return ((spot >= 3 * h) & (spot < 3 * h + 3)).astype(F32)

    head = 2 * pair
    return (of(head) if single else jnp.concatenate([of(head), of(head + 1)], axis=0)).astype(BF)


def heads_of_pair(pair):
    return 128 * pair, pair == PAIRS - 1


def gathered(own_ref, sib_ref, half, at):
    return jnp.concatenate(
        [ref[:, half, :, at : at + 128].reshape(4 * HALF, 128) for ref in (own_ref, sib_ref)], axis=0
    )


def row_terms(term):
    first = term.astype(BF).astype(F32)
    rest = term - first
    second = rest.astype(BF).astype(F32)
    third = rest - second
    turn = (lanes(term.shape[0]) - HEAD_DIM) % 3
    return jnp.where(turn == 0, first, jnp.where(turn == 1, second, third)).astype(BF)


def both(a, b):
    return jnp.concatenate([a, b], axis=0)


def fwd_kernel(q_ref, kv_own, kv_sib, lpos, lseg, kpos, kseg, ctx_ref, qe_ref):
    ok = (kpos[...] <= lpos[...]) & (kseg[...] == lseg[...])
    bias = jnp.where(ok, 0.0, NEG)
    bias = (both(bias[:HALF, : KEYS // 2], bias[:HALF, : KEYS // 2]), both(bias[HALF:], bias[HALF:]))
    spot = lanes(HALF) - HEAD_DIM
    terms = [jnp.zeros((HALF, 128), F32)] * 2
    for pair in range(PAIRS):
        at, single = heads_of_pair(pair)
        k_lo, k_hi = gathered(kv_own, kv_sib, 0, at), gathered(kv_own, kv_sib, 1, at)
        v_lo, v_hi = gathered(kv_own, kv_sib, 0, WIDE + at), gathered(kv_own, kv_sib, 1, WIDE + at)
        for half, keys, values in ((0, k_lo, v_lo), (1, both(k_lo, k_hi), both(v_lo, v_hi))):
            rows = two_heads(q_ref[half * HALF : (half + 1) * HALF, at : at + 128], single)
            s = dot_t(rows, keys) + bias[half][: rows.shape[0]]
            top = jnp.max(s, axis=1, keepdims=True)
            e = jnp.exp(s - top)
            total = jnp.sum(e, axis=1, keepdims=True)
            out = one_block(dot(e.astype(BF), values) * (1.0 / total), single)
            ctx_ref[half * HALF : (half + 1) * HALF, at : at + 128] = out.astype(BF)
            lse = top + jnp.log(total)
            for n in range(rows.shape[0] // HALF):
                head = 2 * pair + n
                mine = (spot >= 3 * head) & (spot < 3 * head + 3)
                terms[half] = jnp.where(mine, -lse[n * HALF : (n + 1) * HALF], terms[half])
    qe_ref[...] = q_ref[...]
    last = q_ref[:, WIDE - 128 :]
    qe_ref[:, WIDE - 128 :] = jnp.where(lanes(2 * HALF) < HEAD_DIM, last, row_terms(both(*terms)))


def dq_kernel(qe_ref, ge_ref, kv_own, kv_sib, lpos, lseg, kpos, kseg, gq_ref):
    ok = (kpos[...] <= lpos[...]) & (kseg[...] == lseg[...])
    bias = jnp.where(ok, 0.0, NEG)
    bias = (both(bias[:HALF, : KEYS // 2], bias[:HALF, : KEYS // 2]), both(bias[HALF:], bias[HALF:]))
    for pair in range(PAIRS):
        at, single = heads_of_pair(pair)
        k_lo, k_hi = gathered(kv_own, kv_sib, 0, at), gathered(kv_own, kv_sib, 1, at)
        v_lo, v_hi = gathered(kv_own, kv_sib, 0, WIDE + at), gathered(kv_own, kv_sib, 1, WIDE + at)
        mask = pick_extra(HALF, pair, single)
        for half, keys, values in ((0, k_lo, v_lo), (1, both(k_lo, k_hi), both(v_lo, v_hi))):
            place = slice(half * HALF, (half + 1) * HALF)
            ones = jnp.ones((keys.shape[0], 128), BF)

            def with_terms(ref):
                rows, extra = two_heads(ref[place, at : at + 128], single), ref[place, WIDE - 128 :]
                extra = extra if single else both(extra, extra)
                return jnp.concatenate([rows, extra * mask], axis=1)

            s = dot_t(with_terms(qe_ref), jnp.concatenate([keys, ones], axis=1))
            dp = dot_t(with_terms(ge_ref), jnp.concatenate([values, ones], axis=1))
            ds = (jnp.exp(s + bias[half][: s.shape[0]]) * dp).astype(BF)
            gq_ref[place, at : at + 128] = (one_block(dot(ds, keys), single) * 0.125).astype(BF)


def dkv_kernel(kv, q_own, q_sib, g_own, g_sib, lpos, lseg, kpos, kseg, gk_ref, gv_ref):
    ok = (lpos[...] <= kpos[...]) & (kseg[...] == lseg[...])
    bias = jnp.where(ok, 0.0, NEG)
    bias = (both(bias[:HALF], bias[:HALF]), both(bias[HALF:, KEYS // 2 :], bias[HALF:, KEYS // 2 :]))

    def queries(own, sib, at):
        lo, hi = gathered(own, sib, 0, at), gathered(own, sib, 1, at)
        return both(lo, hi), hi

    qx, gx = queries(q_own, q_sib, WIDE - 128), queries(g_own, g_sib, WIDE - 128)
    for pair in range(PAIRS):
        at, single = heads_of_pair(pair)
        q, g = queries(q_own, q_sib, at), queries(g_own, g_sib, at)
        terms = pick_extra(HALF, pair, single)
        for half in range(2):
            k = jnp.concatenate([two_heads(kv[half, :, at : at + 128], single), terms], axis=1)
            v = two_heads(kv[half, :, WIDE + at : WIDE + at + 128], single)
            v = jnp.concatenate([v, terms], axis=1)
            s = dot_t(k, jnp.concatenate([q[half], qx[half]], axis=1))
            p = jnp.exp(s + bias[half][: s.shape[0]])
            dp = dot_t(v, jnp.concatenate([g[half], gx[half]], axis=1))
            ds = (p * dp).astype(BF)
            gk_ref[half, :, at : at + 128] = one_block(dot(ds, q[half]), single).astype(BF)
            gv_ref[half, :, at : at + 128] = one_block(dot(p.astype(BF), g[half]), single).astype(BF)


ATTENTION_COST = pl.CostEstimate(
    flops=8_000_000_000, bytes_accessed=6 << 20, transcendentals=PAIRS * 256 * KEYS
)
PARAMS = pltpu.CompilerParams(vmem_limit_bytes=17 * 1024 * 1024)
HERE = pl.BlockSpec(memory_space=pltpu.VMEM)
ANYWHERE = pl.BlockSpec(memory_space=pl.ANY)
FLAT = jax.ShapeDtypeStruct((2 * HALF, WIDE), BF)


def attention_call(kernel, outs, *args):
    return pl.pallas_call(
        kernel,
        out_shape=outs,
        in_specs=[HERE] * len(args),
        out_specs=jax.tree.map(lambda _: HERE, outs),
        compiler_params=PARAMS,
        cost_estimate=ATTENTION_COST,
    )(*args)


def attend_fwd(q, kv_own, kv_sib, where):
    return attention_call(fwd_kernel, (FLAT, FLAT), q, kv_own, kv_sib, *where)


def attend_dq(qe, ge, kv_own, kv_sib, where):
    return attention_call(dq_kernel, FLAT, qe, ge, kv_own, kv_sib, *where)


def attend_dkv(kv, qe_own, qe_sib, ge_own, ge_sib, where):
    part = jax.ShapeDtypeStruct((2, HALF, WIDE), BF)
    return attention_call(dkv_kernel, (part, part), kv, qe_own, qe_sib, ge_own, ge_sib, *where)


FWD_PIECES = ((0, 1152), (1152, 2304), (2304, 3328), (3328, FF))
BACK_PIECES = ((0, FF // 2), (FF // 2, FF))
ROWS = 2 * HALF


def normalised(v):
    mean = jnp.mean(v, axis=1, keepdims=True)
    centred = v - mean
    inv = lax.rsqrt(jnp.mean(centred * centred, axis=1, keepdims=True) + 1e-05)
    return centred * inv, inv


def weight_copies(pieces, wout, wup, wdown, wout_here, wup_here, wdown_here, sems):
    out = pltpu.make_async_copy(wout, wout_here, sems.at[0])
    ups, downs = [], []
    for k, (a, b) in enumerate(pieces):
        ups.append(pltpu.make_async_copy(wup.at[:, a:b], wup_here.at[:, a:b], sems.at[1 + 2 * k]))
        downs.append(pltpu.make_async_copy(wdown.at[a:b, :], wdown_here.at[a:b, :], sems.at[2 + 2 * k]))
    return out, ups, downs


def mlp_fwd_kernel(
    ctx, hidden, gain, gain_next, a_o, b_o, a_u, b_d, b_u, a_d, wout, wup, wdown,
    middle, n2, low_o, low_u, low_d, after, n1_next
):
    x = ctx[:, :D]
    low = dot(x, a_o[...]).astype(BF)
    low_o[...] = low
    mid = hidden[...] + dot(x, wout[...]) + dot(low, b_o[...])
    middle[...] = mid
    normed = (normalised(mid)[0] * gain[...]).astype(BF)
    n2[...] = normed
    low = dot(normed, a_u[...]).astype(BF)
    low_u[...] = low
    total, total_low = jnp.zeros((ROWS, D), F32), jnp.zeros((ROWS, RANK), F32)
    for a, b in FWD_PIECES:
        up = dot(normed, wup[:, a:b]) + dot(low, b_u[:, a:b])
        act = (up * (0.5 * (1.0 + lax.erf(up * 0.7071067811865476)))).astype(BF)
        total = total + dot(act, wdown[a:b, :])
        total_low = total_low + dot(act, a_d[a:b, :])
    low = total_low.astype(BF)
    low_d[...] = low
    new = middle[...] + (total + dot(low, b_d[...]))
    after[...] = new
    n1_next[...] = (normalised(new)[0] * gain_next[...]).astype(BF)


def mlp_back_kernel(
    g, ctx, middle, gain, n2, low_o, low_u, low_d, a_o, b_o, a_u, b_d, spread, b_u, a_d, wout, wup, wdown,
    gh2, ge, ga_o, gb_o, ga_u, gb_d, ga_d, gb_u, wout_here, wup_here, wdown_here, sems
):
    out, ups, downs = weight_copies(BACK_PIECES, wout, wup, wdown, wout_here, wup_here, wdown_here, sems)
    for up, down in zip(ups, downs):
        up.start()
        down.start()
    out.start()
    gy = g[...].astype(BF)
    glow_d = dot_t(gy, b_d[...]).astype(BF)
    gb_d[...] = t_dot(low_d[...], gy).astype(BF)
    normed, low = n2[...], low_u[...]
    gn2, glow_u = jnp.zeros((ROWS, D), F32), jnp.zeros((ROWS, RANK), F32)
    for k, (a, b) in enumerate(BACK_PIECES):
        ups[k].wait()
        up = dot(normed, wup_here[:, a:b]) + dot(low, b_u[:, a:b])
        phi = 0.5 * (1.0 + lax.erf(up * 0.7071067811865476))
        ga_d[:, a:b] = t_dot(glow_d, (up * phi).astype(BF)).astype(BF)
        downs[k].wait()
        gact = dot_t(gy, wdown_here[a:b, :]) + dot_t(glow_d, a_d[a:b, :])
        density = jnp.exp(-0.5 * up * up) * 0.3989422804014327
        gup = (gact * (phi + up * density)).astype(BF)
        gb_u[:, a:b] = t_dot(low, gup).astype(BF)
        gn2 = gn2 + dot_t(gup, wup_here[:, a:b])
        glow_u = glow_u + dot_t(gup, b_u[:, a:b])
    glow_u = glow_u.astype(BF)
    gn2 = gn2 + dot_t(glow_u, a_u[...])
    ga_u[...] = t_dot(glow_u, normed).astype(BF)
    out.wait()
    through_norm(g, middle[...], gain, gn2, ctx[:, :D], low_o[...], a_o, b_o, wout_here, spread, gh2, ge, ga_o, gb_o)


def through_norm(g, middle, gain, gn2, x, low_o, a_o, b_o, wout, spread, gh2, ge, ga_o, gb_o):
    r, inv = normalised(middle)
    gr = gn2 * gain[...]
    grad = g[...] + inv * (
        gr - jnp.mean(gr, axis=1, keepdims=True) - r * jnp.mean(gr * r, axis=1, keepdims=True)
    )
    gh2[...] = grad
    gproj = grad.astype(BF)
    glow_o = dot_t(gproj, b_o[...]).astype(BF)
    ga_o[...] = t_dot(glow_o, x).astype(BF)
    gb_o[...] = t_dot(low_o, gproj).astype(BF)
    gctx = (dot_t(gproj, wout[...]) + dot_t(glow_o, a_o[...])).astype(BF)
    product = gctx.astype(F32) * x.astype(F32)
    first = product.astype(BF)
    second = (product - first.astype(F32)).astype(BF)
    delta = dot(first, spread[...]) + dot(second, spread[...])
    ge[:, :D] = gctx
    ge[:, D:] = row_terms(-delta)[:, HEAD_DIM:]


def qkv_back_kernel(
    gq, gk, gv, low, n1, a, b_q, b_kv, hidden, gain, gh2, wq, wkv, g, ga, gb_q, gb_kv, wq_here, wkv_here, sems
):
    first = pltpu.make_async_copy(wq, wq_here, sems.at[0])
    second = pltpu.make_async_copy(wkv, wkv_here, sems.at[1])
    first.start()
    second.start()
    q, k, v = gq[...], gk[...].reshape(ROWS, WIDE), gv[...].reshape(ROWS, WIDE)
    glow = dot_t(q, b_q[...]) + dot_t(k, b_kv[:, :WIDE]) + dot_t(v, b_kv[:, WIDE:])
    glow = glow.astype(BF)
    ga[...] = t_dot(glow, n1[...]).astype(BF)
    gb_q[...] = t_dot(low[...], q).astype(BF)
    gb_kv[:, :WIDE] = t_dot(low[...], k).astype(BF)
    gb_kv[:, WIDE:] = t_dot(low[...], v).astype(BF)
    first.wait()
    gn1 = dot_t(q, wq_here[...])
    second.wait()
    gn1 = gn1 + dot_t(k, wkv_here[:, :WIDE]) + dot_t(v, wkv_here[:, WIDE:]) + dot_t(glow, a[...])
    r, inv = normalised(hidden[...])
    gr = gn1 * gain[...]
    g[...] = gh2[...] + inv * (
        gr - jnp.mean(gr, axis=1, keepdims=True) - r * jnp.mean(gr * r, axis=1, keepdims=True)
    )


def mlp_both_kernel(
    ctx, hidden, gain, g, a_o, b_o, a_u, b_d, spread, b_u, a_d, wout, wup, wdown,
    after, gh2, ge, ga_o, gb_o, ga_u, gb_d, ga_d, gb_u
):
    x = ctx[:, :D]
    low_o = dot(x, a_o[...]).astype(BF)
    gh2[...] = hidden[...] + dot(x, wout[...]) + dot(low_o, b_o[...])
    normed = (normalised(gh2[...])[0] * gain[...]).astype(BF)
    low = dot(normed, a_u[...]).astype(BF)
    gy = g[...].astype(BF)
    glow_d = dot_t(gy, b_d[...]).astype(BF)
    total, total_low = jnp.zeros((ROWS, D), F32), jnp.zeros((ROWS, RANK), F32)
    gn2, glow_u = jnp.zeros((ROWS, D), F32), jnp.zeros((ROWS, RANK), F32)
    for a, b in BACK_PIECES:
        up = dot(normed, wup[:, a:b]) + dot(low, b_u[:, a:b])
        phi = 0.5 * (1.0 + lax.erf(up * 0.7071067811865476))
        act = (up * phi).astype(BF)
        ga_d[:, a:b] = t_dot(glow_d, act).astype(BF)
        total = total + dot(act, wdown[a:b, :])
        total_low = total_low + dot(act, a_d[a:b, :])
        gact = dot_t(gy, wdown[a:b, :]) + dot_t(glow_d, a_d[a:b, :])
        density = jnp.exp(-0.5 * up * up) * 0.3989422804014327
        gup = (gact * (phi + up * density)).astype(BF)
        gb_u[:, a:b] = t_dot(low, gup).astype(BF)
        gn2 = gn2 + dot_t(gup, wup[:, a:b])
        glow_u = glow_u + dot_t(gup, b_u[:, a:b])
    low_d = total_low.astype(BF)
    gb_d[...] = t_dot(low_d, gy).astype(BF)
    after[...] = (gh2[...] + (total + dot(low_d, b_d[...]))).astype(BF)
    glow_u = glow_u.astype(BF)
    gn2 = gn2 + dot_t(glow_u, a_u[...])
    ga_u[...] = t_dot(glow_u, normed).astype(BF)
    through_norm(g, gh2[...], gain, gn2, x, low_o, a_o, b_o, wout, spread, gh2, ge, ga_o, gb_o)


def shape_of(rows, width, kind=BF):
    return jax.ShapeDtypeStruct((rows, width), kind)


def mlp_call(kernel, args, outs, flops, weights=0, limit=24):
    scratch = [
        pltpu.VMEM((D, D), BF),
        pltpu.VMEM((D, FF), BF),
        pltpu.VMEM((FF, D), BF),
        pltpu.SemaphoreType.DMA((1 + 2 * len(BACK_PIECES),)),
    ]
    return pl.pallas_call(
        kernel,
        out_shape=outs,
        in_specs=[HERE] * (len(args) - weights) + [ANYWHERE] * weights,
        out_specs=(HERE,) * len(outs),
        scratch_shapes=scratch if weights else (),
        compiler_params=pltpu.CompilerParams(vmem_limit_bytes=limit * 1024 * 1024),
        cost_estimate=pl.CostEstimate(flops=flops, bytes_accessed=24 << 20, transcendentals=ROWS * FF),
    )(*args)


def mlp_fwd(*args):
    outs = (shape_of(ROWS, D, F32), shape_of(ROWS, D)) + (shape_of(ROWS, RANK),) * 3
    outs += (shape_of(ROWS, D, F32), shape_of(ROWS, D))
    return mlp_call(mlp_fwd_kernel, args, outs, 10_000_000_000, limit=12)


def mlp_both(*args):
    outs = (shape_of(ROWS, D), shape_of(ROWS, D, F32), shape_of(ROWS, WIDE)) + (shape_of(RANK, D),) * 4
    outs += (shape_of(RANK, FF),) * 2
    return mlp_call(mlp_both_kernel, args, outs, 18_000_000_000, limit=20)


def mlp_back(*args):
    outs = (shape_of(ROWS, D, F32), shape_of(ROWS, WIDE)) + (shape_of(RANK, D),) * 4
    outs += (shape_of(RANK, FF),) * 2
    return mlp_call(mlp_back_kernel, args, outs, 16_000_000_000, 3, 56)


def qkv_back(*args):
    return pl.pallas_call(
        qkv_back_kernel,
        out_shape=(shape_of(ROWS, D, F32), shape_of(RANK, D), shape_of(RANK, WIDE), shape_of(RANK, 2 * WIDE)),
        in_specs=[HERE] * 11 + [ANYWHERE] * 2,
        out_specs=(HERE,) * 4,
        scratch_shapes=[
            pltpu.VMEM((D, WIDE), BF),
            pltpu.VMEM((D, 2 * WIDE), BF),
            pltpu.SemaphoreType.DMA((2,)),
        ],
        compiler_params=pltpu.CompilerParams(vmem_limit_bytes=20 * 1024 * 1024),
        cost_estimate=pl.CostEstimate(flops=5_000_000_000, bytes_accessed=10 << 20, transcendentals=0),
    )(*args)


def ring_start(block):
    return lax.ppermute(block, "seq", UP), lax.ppermute(block, "seq", DOWN)


def ring_far(block, before, after, beside=()):
    far_lo = lax.ppermute(before[0], "seq", UP)
    far_hi = lax.ppermute(after[1], "seq", DOWN)
    far_lo, far_hi, *beside = tie(far_lo, far_hi, *beside)
    own = jnp.stack([block, before, after, jnp.stack([far_lo, far_hi])])
    return (own, *beside) if beside else own


def other_core(own):
    return lax.ppermute(own, "seq", CORE)


def sum_sequence(parts, core, y):
    parts = parts.reshape((4, 2) + parts.shape[1:])
    mine = lax.dynamic_index_in_dim(parts, core, 1, keepdims=False)
    other = lax.dynamic_index_in_dim(parts, 1 - core, 1, keepdims=False)
    half = mine.astype(F32) + lax.ppermute(other, "seq", CORE).astype(F32)

    def of(step):
        return lax.dynamic_index_in_dim(half, (y + step) % 4, 0, keepdims=False)

    total = of(0)
    for step, route in ((1, UP), (3, DOWN), (2, FAR)):
        total = total + lax.ppermute(of(step).astype(BF), "seq", route).astype(F32)
    return total


def tie(*values):
    return lax.optimization_barrier(values)


def eighths(turned, straight):
    def cut(a, part):
        return jnp.pad(a, ((0, 0), (0, 8 * part - a.shape[1]))).reshape(RANK, 8, part)

    first = cut(jnp.concatenate(turned, axis=1), PART_A)
    return jnp.swapaxes(jnp.concatenate([first, cut(straight, PART_B)], axis=2), 0, 1)


def by_adapter_kernel(picks, *refs):
    parts, out_ref, acc = refs[:-2], refs[-2], refs[-1]
    acc[...] = jnp.zeros_like(acc)
    at = 0
    for ref in parts:
        for k in range(ref.shape[0]):
            rows = pl.ds(pl.multiple_of(picks[at] * RANK, RANK), RANK)
            acc[rows, :] = acc[rows, :] + ref[k].astype(F32)
            at += 1
    for j in range(PART // 128):
        square = acc[:, 128 * j : 128 * (j + 1)]
        square = square.T if 128 * j < PART_A else square
        out_ref[128 * j : 128 * (j + 1), :] = square.astype(BF)


def by_adapter(parts, picks):
    return pl.pallas_call(
        by_adapter_kernel,
        out_shape=jax.ShapeDtypeStruct((PART, 128), BF),
        in_specs=[pl.BlockSpec(memory_space=pltpu.SMEM)]
        + [pl.BlockSpec(memory_space=pltpu.VMEM)] * len(parts),
        out_specs=pl.BlockSpec(memory_space=pltpu.VMEM),
        scratch_shapes=[pltpu.VMEM((8 * RANK, PART), F32)],
        compiler_params=PARAMS,
        cost_estimate=pl.CostEstimate(flops=16 * RANK * PART, bytes_accessed=2 << 20, transcendentals=0),
    )(picks, *parts)


def unfold_rows(layer, rows, outs):
    turned, straight = outs[:-1], outs[-1]
    start = 0
    for out, width in zip(turned, TURNED):
        at = start
        while at < start + width:
            n = min(start + width, (at // PART_A + 1) * PART_A) - at
            out[layer, at - start : at - start + n, :] = rows(at // PART_A, at % PART_A, n)
            at += n
        start += width
    squares = PART_B // 128
    for t in range(FF // 128):
        value = rows(t // squares, PART_A + 128 * (t % squares), 128)
        straight[layer, :, 128 * t : 128 * (t + 1)] = value


def unfold_late_kernel(ref, *outs):
    unfold_rows(0, lambda e, at, n: ref[e, at : at + n, :].astype(F32), outs)


def unfold_kernel(place, own_ref, sib_ref, *refs):
    half = len(refs) // 2

    def rows(e, at, n):
        k = place[e]
        mine = own_ref[k % 4, at : at + n, :]
        other = sib_ref[k % 4, at : at + n, :]
        return jnp.where(k < 4, mine.astype(F32), other.astype(F32))

    unfold_rows(0, rows, refs[half:])


def one_layer(layer, *shape):
    return pl.BlockSpec((1,) + shape, lambda i: (layer, 0, 0))


def unfold(kernel, layer, *args):
    shapes = [(w, 128) for w in TURNED] + [(128, FF)]
    whole = [jax.ShapeDtypeStruct((2,) + shape, F32) for shape in shapes]
    first, earlier = (args, ()) if layer == 1 else (args[:3], args[3])
    specs = [pl.BlockSpec(memory_space=pltpu.SMEM)] if layer == 0 else []
    specs += [fixed(*a.shape) for a in first[len(specs) :]] + [ANYWHERE] * len(earlier)
    return pl.pallas_call(
        kernel,
        grid=(1,),
        out_shape=tuple(whole),
        in_specs=specs,
        out_specs=tuple(one_layer(layer, *shape) for shape in shapes),
        input_output_aliases={3 + n: n for n in range(len(earlier))},
        compiler_params=pltpu.CompilerParams(vmem_limit_bytes=40 * 1024 * 1024),
        cost_estimate=pl.CostEstimate(flops=0, bytes_accessed=14 << 20, transcendentals=0),
    )(*first, *earlier)


def fixed(*shape):
    return pl.BlockSpec(shape, lambda i: (0,) * len(shape))


def share(w_qkv, w_out, w_up, w_down, z_lo, spare):
    def half_row(w, front, lines):
        size = lines * 128 - w.shape[1]
        first = jnp.pad(w, ((0, 0), (0, size)))
        second = jnp.pad(w, ((0, 0), (front, size - front)))
        return jnp.where(z_lo == 0, first, second).reshape(-1, lines, 128)

    def put(a, room):
        return jnp.pad(a, ((0, 0), (0, room - a.shape[1]), (0, 0)))

    extra = jnp.broadcast_to(spare[None], (2, 1, 128))
    attention = [
        put(half_row(w_qkv, 32, N_QKV), AT_OUT),
        put(half_row(w_out, 32, N_OUT), LINES - AT_OUT - 1),
        extra,
    ]
    up, down = put(w_up.reshape(-1, N_UP, 128), LINES), put(w_down.reshape(-1, N_DOWN, 128), LINES - 1)
    return jnp.concatenate(attention, axis=1), jnp.concatenate([up, down, extra], axis=1)


def spin(a):
    return pltpu.roll(a, HEAD_DIM, 1)


def fill(ref, base, lines):
    ref[pl.ds(base, lines.shape[0], stride=2), :] = lines


def between(ref, base, n):
    now, later = ref[pl.ds(base, n, stride=2), :], ref[pl.ds(base + 2, n, stride=2), :]
    ref[pl.ds(base + 1, n, stride=2), :] = spin(jnp.where(lanes(n) < HEAD_DIM, later, now))


def columns(ref, dst, to, start, units, step=2):
    got = ref[pl.ds(start, dst.shape[0], stride=units), :].astype(BF)
    n = min(128, dst.shape[1] - to)
    dst[:, to : to + n] = got[:, :n]


def lines_of(ref, pair, zl, start, n):
    return ref[0, zl, 0, pair % 4, pair // 4, start : start + n, :].astype(F32)


def unpack_attention_kernel(g_ref, *refs):
    def lines(pair, zl):
        return lines_of(g_ref, pair, zl, 0, N_QKV), lines_of(g_ref, pair, zl, AT_OUT, N_OUT)

    unpack_attention_lines(lines, *refs)


def unpack_first_kernel(steps, own_1, sib_1, own_2, sib_2, *refs):
    def lines(pair, zl):
        x, core = pair % 4, pair // 4
        z_at, x_at = steps[4 + 2 * (pl.program_id(0) // 4) + zl], steps[8 + x]
        mine = steps[12] == core
        top = jnp.where(mine, own_1[z_at, 0, x_at], sib_1[z_at, 0, x_at])
        bottom = jnp.where(mine, own_2[0, z_at, x_at], sib_2[0, z_at, x_at])
        both = jnp.concatenate([top.astype(F32), bottom.astype(F32)], axis=0)
        return both[:N_QKV], both[AT_OUT : AT_OUT + N_OUT]

    unpack_attention_lines(lines, *refs)


def unpack_attention_lines(lines, q_ref, kv_ref, out_ref, s_qkv, s_out):
    low = lanes(1) < HEAD_DIM
    zero = jnp.zeros((1, 128), F32)
    for pair in range(8):
        (qkv0, out0), (qkv1, out1) = lines(pair, 0), lines(pair, 1)
        base, base_out = pair * 867, pair * 289
        fill(s_qkv, base, qkv0)
        fill(s_qkv, base + 433, qkv1)
        between(s_qkv, base, N_QKV - 1)
        between(s_qkv, base + 433, N_QKV)
        s_qkv[pl.ds(base + 432, 1), :] = qkv0[N_QKV - 1 :] + spin(jnp.where(low, qkv1[:1], zero))
        s_qkv[pl.ds(base + 433, 1), :] = qkv1[:1] + spin(jnp.where(low, zero, qkv0[N_QKV - 1 :]))
        fill(s_out, base_out, out0)
        fill(s_out, base_out + 144, out1)
        s_out[pl.ds(base_out + 144, 1), :] = out0[N_OUT - 1 :] + out1[:1]
        between(s_out, base_out, N_OUT - 1)
        between(s_out, base_out + 144, N_OUT - 1)
    half = lanes(BLOCK) < HEAD_DIM
    for dst, to, first in ((q_ref, 0, 0), (kv_ref, 0, 17), (kv_ref, WIDE, 34)):
        for j in range(8):
            columns(s_qkv, dst, to + 128 * j, first + 2 * j, 51)
        got = s_qkv[pl.ds(first + 16, BLOCK, stride=51), :]
        dst[:, to + D - HEAD_DIM : to + WIDE] = jnp.where(half, got, 0.0).astype(BF)
    for j in range(9):
        columns(s_out, out_ref, 128 * j, 2 * j, 17)


def unpack_mlp_kernel(g_up, g_down, up_ref, down_ref, s_up, s_down):
    for pair in range(8):
        for zl in range(2):
            at = pair * 2 + zl
            s_up[pl.ds(at * N_UP, N_UP), :] = lines_of(g_up, pair, zl, 0, N_UP)
            fill(s_down, at * 2 * N_DOWN, lines_of(g_down, pair, zl, 0, N_DOWN))
    for at in range(16):
        between(s_down, at * 2 * N_DOWN, N_DOWN)
    for j in range(34):
        columns(s_up, up_ref, 128 * j, j, 34)
    for j in range(9):
        columns(s_down, down_ref, 128 * j, 2 * j, 17)


def unpack(kernel, got, at, outs, scratch_lines, limit):
    g = got.reshape(2, 2, 4, 4, 2, -1, 128)

    def spec(k):
        return pl.BlockSpec((1, 2, 1, 4, 2, LINES, 128), lambda i: (i // 4, 0, i % 4, 0, 0, k, 0))

    return pl.pallas_call(
        kernel,
        grid=(8,),
        out_shape=tuple(jax.ShapeDtypeStruct((8 * r, w), BF) for r, w in outs),
        in_specs=[spec(k) for k in at],
        out_specs=tuple(pl.BlockSpec((r, w), lambda i: (i, 0)) for r, w in outs),
        scratch_shapes=[pltpu.VMEM((n, 128), F32) for n in scratch_lines],
        compiler_params=pltpu.CompilerParams(vmem_limit_bytes=limit * 1024 * 1024),
        cost_estimate=pl.CostEstimate(
            flops=0, bytes_accessed=len(at) * (20 << 20), transcendentals=0
        ),
    )(*[g] * len(at))


ATTENTION_OUTS = [(BLOCK, WIDE), (BLOCK, 2 * WIDE), (BLOCK, D)]
ATTENTION_LINES = [8 * 867 + 8, 8 * 289 + 8]


def unpack_attention(got, at):
    return unpack(unpack_attention_kernel, got, [at], ATTENTION_OUTS, ATTENTION_LINES, 36)


def along(axis, block, near):
    name, shift = SHIFTS[axis]
    before = lax.ppermute(block, name, shift(1))
    after = lax.ppermute(block, name, shift(-1))
    if near:
        far = lax.ppermute(block, name, shift(2))
    else:
        n = block.shape[0] // 2
        far = [lax.ppermute(before[:n], name, shift(1)), lax.ppermute(after[n:], name, shift(-1))]
        far = jnp.concatenate(far)
    return jnp.stack([block, before, after, far])


def gather_first(share, later):
    n = LINES // 2
    row = along("x", share, True)
    one, two = along("y", row[:, :n], True), along("z", row[:, n:], True)
    one, two, later = tie(one, two, later)
    one, two = along("z", one, False), along("y", two, False)
    return (one, other_core(one), two, other_core(two)), later


def unpack_first(one, sib_one, two, sib_two, steps):
    n = LINES // 2
    spec_one = pl.BlockSpec((4, 1, 4, n, 128), lambda i, steps: (0, steps[i % 4], 0, 0, 0))
    spec_two = pl.BlockSpec((1, 4, 4, n, 128), lambda i, steps: (steps[i % 4], 0, 0, 0, 0))
    return pl.pallas_call(
        unpack_first_kernel,
        grid_spec=pltpu.PrefetchScalarGridSpec(
            num_scalar_prefetch=1,
            grid=(8,),
            in_specs=[spec_one, spec_one, spec_two, spec_two],
            out_specs=tuple(pl.BlockSpec((r, w), lambda i, steps: (i, 0)) for r, w in ATTENTION_OUTS),
            scratch_shapes=[pltpu.VMEM((n, 128), F32) for n in ATTENTION_LINES],
        ),
        out_shape=tuple(jax.ShapeDtypeStruct((8 * r, w), BF) for r, w in ATTENTION_OUTS),
        compiler_params=pltpu.CompilerParams(vmem_limit_bytes=26 * 1024 * 1024),
        cost_estimate=pl.CostEstimate(flops=0, bytes_accessed=30 << 20, transcendentals=0),
    )(steps, one, sib_one, two, sib_two)


def unpack_mlp(got, at):
    outs = [(BLOCK, FF), (4 * BLOCK, D)]
    return unpack(unpack_mlp_kernel, got, [at, at + 1], outs, [16 * N_UP, 32 * N_DOWN + 8], 20)


def shards(
    tokens, segments, adapter_pick, norm_gain, w_qkv, w_out, w_up, w_down,
    a_qkv, b_qkv, a_out, b_out, a_up, b_up, a_down, b_down, grad_out
):
    layers = norm_gain.shape[0]
    index = lax.axis_index("seq")
    z_hi, place = index // 8, index % 8
    core, y = place % 2, place // 2

    def halves(own, other):
        return jnp.where(z_hi == 0, jnp.stack([own, other]), jnp.stack([other, own]))

    def mine(a):
        return lax.dynamic_index_in_dim(a, z_hi, 0, keepdims=False)

    def theirs(a):
        return lax.dynamic_index_in_dim(a, 1 - z_hi, 0, keepdims=False)

    batch = lax.axis_index("batch")
    spare = (segments.reshape(1, 128), jnp.pad(adapter_pick[None], ((0, 0), (0, 126))))
    attention, _ = share(w_qkv, w_out, w_up, w_down, batch % 2, spare[0].astype(BF))
    _, mlp = share(w_qkv, w_out, w_up, w_down, batch % 2, spare[1].astype(BF))

    def gather(a):
        return lax.all_gather(a, BOTH, axis=0, tiled=True, axis_index_groups=ALL)

    early = gather(jnp.concatenate([mlp[0], attention[1]], axis=0))
    late = gather(mlp[1])
    raw = (a_qkv, b_qkv, a_out, b_out, a_up, b_up, a_down, b_down, norm_gain)
    (one, sib_one, two, sib_two), raw = gather_first(attention[0], raw)
    a_qkv, b_qkv, a_out, b_out, a_up, b_up, a_down, b_down, norm_gain = raw

    sent = lax.ppermute(jnp.stack([theirs(tokens), theirs(grad_out)]), "seq", SWAP)
    hidden = halves(mine(tokens), sent[0]).reshape(2 * HALF, D).astype(F32)
    grad_hidden = halves(mine(grad_out), sent[1]).reshape(2 * HALF, D).astype(F32)
    pick = mine(adapter_pick)

    def segments_of(two):
        lines = two[:, :, 0, -1]
        lines = jnp.stack([lines[:, 0], lines[:, 3]])
        return lax.dynamic_slice(lines, (0, 0, z_hi * HALF), (2, 4, HALF))

    seg = jnp.stack([segments_of(two), segments_of(sib_two)], axis=1)
    seg = jnp.where(z_hi == 0, seg, seg[::-1]).astype(jnp.int32)
    offset = jnp.arange(HALF, dtype=jnp.int32)
    start = jnp.array([0, KEYS // 2], jnp.int32)[:, None]
    lpos = (start + place * HALF + offset[None]).reshape(2 * HALF, 1)
    lseg = seg[:, 0, 0].reshape(2 * HALF, 1)
    ys = (y + jnp.array([0, 3, 1, 2], jnp.int32)) % 4
    order = jnp.concatenate([2 * ys + core, 2 * ys + 1 - core])
    kpos = (start[:, :, None] + (order * HALF)[None, :, None] + offset).reshape(1, KEYS)
    where = (lpos, lseg, kpos, seg.reshape(1, KEYS))

    z_lo, x = batch % 2, batch // 2
    z = z_hi * 2 + z_lo
    picks = early.reshape(2, 2, 4, 4, 2, -1, 128)[0, :, 0, :, 0, 2 * LINES - 1, :2].astype(jnp.int32)
    picks = jnp.swapaxes(picks, 0, 1).reshape(16)
    steps = jnp.array([0, 3, 1, 2], jnp.int32)

    def sequence(zs, xs):
        return 2 * (2 * xs + zs % 2) + zs // 2

    four = jnp.arange(4, dtype=jnp.int32)
    picks_in_order = jnp.take(picks, sequence(four[:, None], four[None, :]).reshape(16))
    zs, xs = (z + steps) % 4, (x + steps) % 4
    picks_by_step = jnp.take(picks, sequence(zs[None, :], xs[:, None]).reshape(16))
    eight = jnp.arange(8, dtype=jnp.int32)
    back = jnp.array([0, 2, 3, 1], jnp.int32)
    place_by_step = 4 * ((eight % 2) ^ core) + jnp.take(back, (eight // 2 - y) % 4)
    arrival = [jnp.take(back, (four - at) % 4) for at in (y, z, x)]
    arrival = jnp.concatenate(arrival + [core[None]]).astype(jnp.int32)

    def low_in(a, l):
        return lax.dynamic_slice_in_dim(a[l], pick * RANK, RANK, 1)

    def low_out(b, l):
        return lax.dynamic_slice_in_dim(b[l], pick * RANK, RANK, 0)

    heads_of = (jnp.arange(D, dtype=jnp.int32) // HEAD_DIM)[:, None]
    spread = (heads_of == (jnp.arange(128, dtype=jnp.int32)[None, :] - HEAD_DIM) // 3).astype(BF)

    def adapters(l):
        b_first = low_out(b_qkv, l)
        b_kv = jnp.concatenate([widen(b_first[:, D : 2 * D]), widen(b_first[:, 2 * D :])], axis=1)
        rest = [f(a, l) for pair in ((a_out, b_out), (a_up, b_up), (a_down, b_down)) for f, a in zip((low_in, low_out), pair)]
        return [low_in(a_qkv, l), widen(b_first[:, :D]), b_kv] + rest

    n1 = (norm_stats(hidden)[0] * norm_gain[0, 0]).astype(BF)
    ahead = (where, spread, n1, grad_hidden, [adapters(l) for l in range(layers)])
    sib_one, (where, spread, n1, grad_hidden, adapter_parts) = tie(sib_one, ahead)
    first = unpack_first(one, sib_one, two, sib_two, arrival)
    saved, queries = [], []
    for l in range(layers):
        a_first, b_q, b_kv, a_o, b_o, a_u, b_u, a_d, b_d = adapter_parts[l]
        wq, wkv, wout = first
        low_qkv = dot(n1, a_first).astype(BF)
        kv = (dot(n1, wkv) + dot(low_qkv, b_kv)).astype(BF).reshape(2, HALF, 2 * WIDE)
        q = (dot(n1, wq) + dot(low_qkv, b_q)).astype(BF) * jnp.asarray(0.125, BF)
        before, after = ring_start(kv)
        if l == 0:
            before, after, q, wup, wdown = tie(before, after, q, *unpack_mlp(early, 0))
        else:
            before, after, q, late = tie(before, after, q, late)
        if l == 0:
            kv_own, *first = ring_far(kv, before, after, unpack_attention(early, 2))
        else:
            kv_own, wup, wdown = ring_far(kv, before, after, unpack_mlp(late, 0))
        kv_sib = other_core(kv_own)
        ctx, qe = attend_fwd(q, kv_own, kv_sib, where)
        queries.append(qe.reshape(2, HALF, WIDE))
        gains = norm_gain[l, 1][None], norm_gain[(l + 1) % layers, 0][None]
        small, large = (a_o, b_o, a_u, b_d), (b_u, a_d, wout, wup, wdown)
        rows, hidden_next, n1_next = None, None, None
        if l < layers - 1:
            middle, n2, low_o, low_u, low_d, hidden_next, n1_next = mlp_fwd(ctx, hidden, *gains, *small, *large)
            rows = (ctx, middle, gains[0], n2, low_o, low_u, low_d)
        else:
            starts = [ring_start(a) for a in queries]
            result, *back = mlp_both(ctx, hidden, gains[0], grad_hidden, *small, spread, *large)
            starts, back = tie(starts, back)
            queries = [ring_far(a, *start) for a, start in zip(queries, starts)]
        saved.append(
            (hidden, n1, low_qkv, kv, kv_own, kv_sib, qe)
            + (rows, small, large, a_first, b_q, b_kv, wq, wkv)
        )
        hidden, n1 = hidden_next, n1_next

    behind = None
    for l in reversed(range(layers)):
        hidden_in, n1, low_qkv, kv, kv_own, kv_sib, qe, rows, small, large, a_first, b_q, b_kv, wq, wkv = saved[l]
        if l < layers - 1:
            back = mlp_back(g, *rows, *small, spread, *large)
        gh2, ge, ga_o, gb_o, ga_u, gb_d, ga_d, gb_u = back
        if l == layers - 1:
            queries, ge = tie(queries, ge)
        qe_own, qe_sib = queries[l], other_core(queries[l])
        g_block = ge.reshape(2, HALF, WIDE)
        g_before, g_after = ring_start(g_block)
        if behind is not None:
            behind, ge = tie(behind, ge)
            behind = lax.all_gather(behind, BOTH, axis=0, axis_index_groups=SAME_PLACE)
        gq = attend_dq(qe, ge, kv_own, kv_sib, where)
        g_before, g_after, gq = tie(g_before, g_after, gq)
        ge_own = ring_far(g_block, g_before, g_after)
        ge_sib = other_core(ge_own)
        gk, gv = attend_dkv(kv, qe_own, qe_sib, ge_own, ge_sib, where)
        g, ga_q, gb_q, gb_kv = qkv_back(
            gq, gk, gv, low_qkv, n1, a_first, b_q, b_kv, hidden_in, norm_gain[l, 0][None], gh2, wq, wkv
        )
        gb_q = [gb_q[:, :D], gb_kv[:, :D], gb_kv[:, WIDE : WIDE + D]]
        parts = eighths([ga_q, ga_o, ga_u, ga_d] + gb_q + [gb_o, gb_d], gb_u)
        if l > 0:
            parts, g = tie(parts, g)
            behind = sum_sequence(parts, core, y)

    got = lax.all_to_all(parts, BOTH, 0, 0, axis_index_groups=SAME_SEQUENCE)
    part = jnp.sum(got.astype(F32), axis=0).astype(BF)
    along_z = [lax.ppermute(part, BOTH, z_shift(by)) for by in (1, -1, 2)]
    behind, part = tie(behind, part)
    one = by_adapter([behind], picks_in_order)
    one, *along_z = tie(one, *along_z)
    one = lax.all_gather(one, BOTH, axis=0, axis_index_groups=SAME_SEQUENCE)
    along_z = jnp.stack([part] + along_z)
    before = lax.ppermute(along_z, "batch", x_shift(1))
    after = lax.ppermute(along_z, "batch", x_shift(-1))
    sent_home = theirs(g.reshape(2, HALF, D)), theirs(result.reshape(2, HALF, D))
    back_home = [lax.ppermute(a, "seq", SWAP) for a in sent_home]
    far = [lax.ppermute(before[:2], "batch", x_shift(1)), lax.ppermute(after[2:], "batch", x_shift(-1))]
    whole = by_adapter([along_z, before, after] + far, picks_by_step)
    whole = whole.reshape(2, -1, 128)
    own = ring_far(whole, *ring_start(whole))
    one = unfold(unfold_late_kernel, 1, one)
    grad_tokens = halves(mine(g.reshape(2, HALF, D)), back_home[0])
    result = halves(mine(result.reshape(2, HALF, D)), back_home[1])
    sib = other_core(own)
    sib, grad_tokens, result, *one = tie(sib, grad_tokens, result, *one)
    sib = sib.reshape(4, PART, 128)
    ga_q, ga_o, ga_u, ga_d, gb_q, gb_o, gb_d, gb_u = unfold(
        unfold_kernel, 0, place_by_step, own.reshape(4, PART, 128), sib, one
    )
    gb_q, gb_o, gb_d = (jnp.swapaxes(a, 1, 2) for a in (gb_q, gb_o, gb_d))

    return result, grad_tokens, ga_q, gb_q, ga_o, gb_o, ga_u, gb_u, ga_d, gb_d


def solution(mesh):
    rows, flat, whole = P("batch", "seq", None), P(None, ("seq", "batch")), P()
    in_specs = (rows, P("batch", "seq"), P("batch"), whole) + (flat,) * 4 + (whole,) * 8 + (rows,)
    out_specs = (rows, rows) + (whole,) * 8
    return jax.shard_map(shards, mesh=mesh, in_specs=in_specs, out_specs=out_specs, check_vma=False)
```

```python
import jax
import jax.numpy as jnp
from jax import lax
from jax.experimental import pallas as pl
from jax.experimental.pallas import tpu as pltpu
from jax.sharding import PartitionSpec as P

D = 1088
HEADS = 17
HEAD_DIM = 64
FF = 4352
RANK = 16
WIDE = 1152
PAIRS = 9
HALF = 64
KEYS = 1024
BF = jnp.bfloat16
F32 = jnp.float32
NEG = -1e30

SWAP = [(i, i ^ 8) for i in range(16)]
CORE = [(i, i ^ 1) for i in range(16)]
UP = [(i, (i & 8) | ((i + 2) & 7)) for i in range(16)]
DOWN = [(i, (i & 8) | ((i - 2) & 7)) for i in range(16)]
FAR = [(i, (i & 8) | ((i + 4) & 7)) for i in range(16)]
def at_chip(z, y, x, core):
    return ((z // 2 * 4 + y) * 2 + core) * 8 + x * 2 + z % 2


ALL = [[at_chip(z, y, x, c) for z in range(4) for y in range(4) for x in range(4) for c in range(2)]]
SAME_SEQUENCE = [[at_chip(z, y, x, c) for y in range(4) for c in range(2)] for z in range(4) for x in range(4)]
SAME_PLACE = [[at_chip(z, y, x, c) for z in range(4) for x in range(4)] for y in range(4) for c in range(2)]


def z_shift(by):
    return [
        (at_chip(z, y, x, c), at_chip((z + by) % 4, y, x, c))
        for z in range(4) for y in range(4) for x in range(4) for c in range(2)
    ]


def x_shift(by):
    return [(i, (i + 2 * by) % 8) for i in range(8)]


def y_shift(by):
    return [(i, (i & 8) | ((i + 2 * by) & 7)) for i in range(16)]


BOTH = ("seq", "batch")
SHIFTS = {"x": ("batch", x_shift), "y": ("seq", y_shift), "z": (BOTH, z_shift)}
TURNED = (D, D, D, FF, 3 * D, D, D)
PART_A, PART_B = 1664, 640
PART = PART_A + PART_B

LINES = 304
AT_OUT = 224
N_QKV, N_OUT, N_UP, N_DOWN = 217, 73, 289, 289
BLOCK = 136


def dot(a, b):
    return jnp.dot(a, b, preferred_element_type=F32)


def dot_t(a, b):
    return lax.dot_general(a, b, (((1,), (1,)), ((), ())), preferred_element_type=F32)


def t_dot(a, b):
    return lax.dot_general(a, b, (((0,), (0,)), ((), ())), preferred_element_type=F32)


def norm_stats(v):
    mean = jnp.mean(v, axis=-1, keepdims=True)
    centred = v - mean
    inv = lax.rsqrt(jnp.mean(centred * centred, axis=-1, keepdims=True) + 1e-05)
    return centred * inv, inv


def norm_back(v, gain, grad):
    r, inv = norm_stats(v)
    gr = grad * gain
    return inv * (
        gr - jnp.mean(gr, axis=-1, keepdims=True) - r * jnp.mean(gr * r, axis=-1, keepdims=True)
    )


def widen(a):
    return jnp.pad(a, ((0, 0), (0, WIDE - D)))


def lanes(rows):
    return lax.broadcasted_iota(jnp.int32, (rows, 128), 1)


def two_heads(block, single):
    low = lanes(block.shape[0]) < HEAD_DIM
    zero = jnp.zeros_like(block)
    first = jnp.where(low, block, zero)
    return first if single else jnp.concatenate([first, jnp.where(low, zero, block)], axis=0)


def one_block(stacked, single):
    rows = stacked.shape[0] if single else stacked.shape[0] // 2
    second = jnp.zeros_like(stacked) if single else stacked[rows:]
    return jnp.where(lanes(rows) < HEAD_DIM, stacked[:rows], second)


def pick_extra(rows, pair, single):
    spot = lanes(rows) - HEAD_DIM

    def of(h):
        return ((spot >= 3 * h) & (spot < 3 * h + 3)).astype(F32)

    head = 2 * pair
    return (of(head) if single else jnp.concatenate([of(head), of(head + 1)], axis=0)).astype(BF)


def heads_of_pair(pair):
    return 128 * pair, pair == PAIRS - 1


def gathered(own_ref, sib_ref, half, at):
    return jnp.concatenate(
        [ref[:, half, :, at : at + 128].reshape(4 * HALF, 128) for ref in (own_ref, sib_ref)], axis=0
    )


def row_terms(term):
    first = term.astype(BF).astype(F32)
    rest = term - first
    second = rest.astype(BF).astype(F32)
    third = rest - second
    turn = (lanes(term.shape[0]) - HEAD_DIM) % 3
    return jnp.where(turn == 0, first, jnp.where(turn == 1, second, third)).astype(BF)


def both(a, b):
    return jnp.concatenate([a, b], axis=0)


def fwd_kernel(q_ref, kv_own, kv_sib, lpos, lseg, kpos, kseg, ctx_ref, qe_ref):
    ok = (kpos[...] <= lpos[...]) & (kseg[...] == lseg[...])
    bias = jnp.where(ok, 0.0, NEG)
    bias = (both(bias[:HALF, : KEYS // 2], bias[:HALF, : KEYS // 2]), both(bias[HALF:], bias[HALF:]))
    spot = lanes(HALF) - HEAD_DIM
    terms = [jnp.zeros((HALF, 128), F32)] * 2
    for pair in range(PAIRS):
        at, single = heads_of_pair(pair)
        k_lo, k_hi = gathered(kv_own, kv_sib, 0, at), gathered(kv_own, kv_sib, 1, at)
        v_lo, v_hi = gathered(kv_own, kv_sib, 0, WIDE + at), gathered(kv_own, kv_sib, 1, WIDE + at)
        for half, keys, values in ((0, k_lo, v_lo), (1, both(k_lo, k_hi), both(v_lo, v_hi))):
            rows = two_heads(q_ref[half * HALF : (half + 1) * HALF, at : at + 128], single)
            s = dot_t(rows, keys) + bias[half][: rows.shape[0]]
            top = jnp.max(s, axis=1, keepdims=True)
            e = jnp.exp(s - top)
            total = jnp.sum(e, axis=1, keepdims=True)
            out = one_block(dot(e.astype(BF), values) * (1.0 / total), single)
            ctx_ref[half * HALF : (half + 1) * HALF, at : at + 128] = out.astype(BF)
            lse = top + jnp.log(total)
            for n in range(rows.shape[0] // HALF):
                head = 2 * pair + n
                mine = (spot >= 3 * head) & (spot < 3 * head + 3)
                terms[half] = jnp.where(mine, -lse[n * HALF : (n + 1) * HALF], terms[half])
    qe_ref[...] = q_ref[...]
    last = q_ref[:, WIDE - 128 :]
    qe_ref[:, WIDE - 128 :] = jnp.where(lanes(2 * HALF) < HEAD_DIM, last, row_terms(both(*terms)))


def dq_kernel(qe_ref, ge_ref, kv_own, kv_sib, lpos, lseg, kpos, kseg, gq_ref):
    ok = (kpos[...] <= lpos[...]) & (kseg[...] == lseg[...])
    bias = jnp.where(ok, 0.0, NEG)
    bias = (both(bias[:HALF, : KEYS // 2], bias[:HALF, : KEYS // 2]), both(bias[HALF:], bias[HALF:]))
    for pair in range(PAIRS):
        at, single = heads_of_pair(pair)
        k_lo, k_hi = gathered(kv_own, kv_sib, 0, at), gathered(kv_own, kv_sib, 1, at)
        v_lo, v_hi = gathered(kv_own, kv_sib, 0, WIDE + at), gathered(kv_own, kv_sib, 1, WIDE + at)
        mask = pick_extra(HALF, pair, single)
        for half, keys, values in ((0, k_lo, v_lo), (1, both(k_lo, k_hi), both(v_lo, v_hi))):
            place = slice(half * HALF, (half + 1) * HALF)
            ones = jnp.ones((keys.shape[0], 128), BF)

            def with_terms(ref):
                rows, extra = two_heads(ref[place, at : at + 128], single), ref[place, WIDE - 128 :]
                extra = extra if single else both(extra, extra)
                return jnp.concatenate([rows, extra * mask], axis=1)

            s = dot_t(with_terms(qe_ref), jnp.concatenate([keys, ones], axis=1))
            dp = dot_t(with_terms(ge_ref), jnp.concatenate([values, ones], axis=1))
            ds = (jnp.exp(s + bias[half][: s.shape[0]]) * dp).astype(BF)
            gq_ref[place, at : at + 128] = (one_block(dot(ds, keys), single) * 0.125).astype(BF)


def dkv_kernel(kv, q_own, q_sib, g_own, g_sib, lpos, lseg, kpos, kseg, gk_ref, gv_ref):
    ok = (lpos[...] <= kpos[...]) & (kseg[...] == lseg[...])
    bias = jnp.where(ok, 0.0, NEG)
    bias = (both(bias[:HALF], bias[:HALF]), both(bias[HALF:, KEYS // 2 :], bias[HALF:, KEYS // 2 :]))

    def queries(own, sib, at):
        lo, hi = gathered(own, sib, 0, at), gathered(own, sib, 1, at)
        return both(lo, hi), hi

    qx, gx = queries(q_own, q_sib, WIDE - 128), queries(g_own, g_sib, WIDE - 128)
    for pair in range(PAIRS):
        at, single = heads_of_pair(pair)
        q, g = queries(q_own, q_sib, at), queries(g_own, g_sib, at)
        terms = pick_extra(HALF, pair, single)
        for half in range(2):
            k = jnp.concatenate([two_heads(kv[half, :, at : at + 128], single), terms], axis=1)
            v = two_heads(kv[half, :, WIDE + at : WIDE + at + 128], single)
            v = jnp.concatenate([v, terms], axis=1)
            s = dot_t(k, jnp.concatenate([q[half], qx[half]], axis=1))
            p = jnp.exp(s + bias[half][: s.shape[0]])
            dp = dot_t(v, jnp.concatenate([g[half], gx[half]], axis=1))
            ds = (p * dp).astype(BF)
            gk_ref[half, :, at : at + 128] = one_block(dot(ds, q[half]), single).astype(BF)
            gv_ref[half, :, at : at + 128] = one_block(dot(p.astype(BF), g[half]), single).astype(BF)


ATTENTION_COST = pl.CostEstimate(
    flops=8_000_000_000, bytes_accessed=6 << 20, transcendentals=PAIRS * 256 * KEYS
)
PARAMS = pltpu.CompilerParams(vmem_limit_bytes=17 * 1024 * 1024)
HERE = pl.BlockSpec(memory_space=pltpu.VMEM)
ANYWHERE = pl.BlockSpec(memory_space=pl.ANY)
FLAT = jax.ShapeDtypeStruct((2 * HALF, WIDE), BF)


def attention_call(kernel, outs, *args):
    return pl.pallas_call(
        kernel,
        out_shape=outs,
        in_specs=[HERE] * len(args),
        out_specs=jax.tree.map(lambda _: HERE, outs),
        compiler_params=PARAMS,
        cost_estimate=ATTENTION_COST,
    )(*args)


def attend_fwd(q, kv_own, kv_sib, where):
    return attention_call(fwd_kernel, (FLAT, FLAT), q, kv_own, kv_sib, *where)


def attend_dq(qe, ge, kv_own, kv_sib, where):
    return attention_call(dq_kernel, FLAT, qe, ge, kv_own, kv_sib, *where)


def attend_dkv(kv, qe_own, qe_sib, ge_own, ge_sib, where):
    part = jax.ShapeDtypeStruct((2, HALF, WIDE), BF)
    return attention_call(dkv_kernel, (part, part), kv, qe_own, qe_sib, ge_own, ge_sib, *where)


FWD_PIECES = ((0, 1152), (1152, 2304), (2304, 3328), (3328, FF))
BACK_PIECES = ((0, FF // 2), (FF // 2, FF))
ROWS = 2 * HALF


def normalised(v):
    mean = jnp.mean(v, axis=1, keepdims=True)
    centred = v - mean
    inv = lax.rsqrt(jnp.mean(centred * centred, axis=1, keepdims=True) + 1e-05)
    return centred * inv, inv


def weight_copies(pieces, wout, wup, wdown, wout_here, wup_here, wdown_here, sems):
    out = pltpu.make_async_copy(wout, wout_here, sems.at[0])
    ups, downs = [], []
    for k, (a, b) in enumerate(pieces):
        ups.append(pltpu.make_async_copy(wup.at[:, a:b], wup_here.at[:, a:b], sems.at[1 + 2 * k]))
        downs.append(pltpu.make_async_copy(wdown.at[a:b, :], wdown_here.at[a:b, :], sems.at[2 + 2 * k]))
    return out, ups, downs


def mlp_fwd_kernel(
    ctx, hidden, gain, gain_next, a_o, b_o, a_u, b_d, b_u, a_d, wout, wup, wdown,
    middle, n2, low_o, low_u, low_d, after, n1_next
):
    x = ctx[:, :D]
    low = dot(x, a_o[...]).astype(BF)
    low_o[...] = low
    mid = hidden[...] + dot(x, wout[...]) + dot(low, b_o[...])
    middle[...] = mid
    normed = (normalised(mid)[0] * gain[...]).astype(BF)
    n2[...] = normed
    low = dot(normed, a_u[...]).astype(BF)
    low_u[...] = low
    total, total_low = jnp.zeros((ROWS, D), F32), jnp.zeros((ROWS, RANK), F32)
    for a, b in FWD_PIECES:
        up = dot(normed, wup[:, a:b]) + dot(low, b_u[:, a:b])
        act = (up * (0.5 * (1.0 + lax.erf(up * 0.7071067811865476)))).astype(BF)
        total = total + dot(act, wdown[a:b, :])
        total_low = total_low + dot(act, a_d[a:b, :])
    low = total_low.astype(BF)
    low_d[...] = low
    new = middle[...] + (total + dot(low, b_d[...]))
    after[...] = new
    n1_next[...] = (normalised(new)[0] * gain_next[...]).astype(BF)


def mlp_back_kernel(
    g, ctx, middle, gain, n2, low_o, low_u, low_d, a_o, b_o, a_u, b_d, spread, b_u, a_d, wout, wup, wdown,
    gh2, ge, ga_o, gb_o, ga_u, gb_d, ga_d, gb_u, wout_here, wup_here, wdown_here, sems
):
    out, ups, downs = weight_copies(BACK_PIECES, wout, wup, wdown, wout_here, wup_here, wdown_here, sems)
    for up, down in zip(ups, downs):
        up.start()
        down.start()
    out.start()
    gy = g[...].astype(BF)
    glow_d = dot_t(gy, b_d[...]).astype(BF)
    gb_d[...] = t_dot(low_d[...], gy).astype(BF)
    normed, low = n2[...], low_u[...]
    gn2, glow_u = jnp.zeros((ROWS, D), F32), jnp.zeros((ROWS, RANK), F32)
    for k, (a, b) in enumerate(BACK_PIECES):
        ups[k].wait()
        up = dot(normed, wup_here[:, a:b]) + dot(low, b_u[:, a:b])
        phi = 0.5 * (1.0 + lax.erf(up * 0.7071067811865476))
        ga_d[:, a:b] = t_dot(glow_d, (up * phi).astype(BF)).astype(BF)
        downs[k].wait()
        gact = dot_t(gy, wdown_here[a:b, :]) + dot_t(glow_d, a_d[a:b, :])
        density = jnp.exp(-0.5 * up * up) * 0.3989422804014327
        gup = (gact * (phi + up * density)).astype(BF)
        gb_u[:, a:b] = t_dot(low, gup).astype(BF)
        gn2 = gn2 + dot_t(gup, wup_here[:, a:b])
        glow_u = glow_u + dot_t(gup, b_u[:, a:b])
    glow_u = glow_u.astype(BF)
    gn2 = gn2 + dot_t(glow_u, a_u[...])
    ga_u[...] = t_dot(glow_u, normed).astype(BF)
    out.wait()
    through_norm(g, middle[...], gain, gn2, ctx[:, :D], low_o[...], a_o, b_o, wout_here, spread, gh2, ge, ga_o, gb_o)


def through_norm(g, middle, gain, gn2, x, low_o, a_o, b_o, wout, spread, gh2, ge, ga_o, gb_o):
    r, inv = normalised(middle)
    gr = gn2 * gain[...]
    grad = g[...] + inv * (
        gr - jnp.mean(gr, axis=1, keepdims=True) - r * jnp.mean(gr * r, axis=1, keepdims=True)
    )
    gh2[...] = grad
    gproj = grad.astype(BF)
    glow_o = dot_t(gproj, b_o[...]).astype(BF)
    ga_o[...] = t_dot(glow_o, x).astype(BF)
    gb_o[...] = t_dot(low_o, gproj).astype(BF)
    gctx = (dot_t(gproj, wout[...]) + dot_t(glow_o, a_o[...])).astype(BF)
    product = gctx.astype(F32) * x.astype(F32)
    first = product.astype(BF)
    second = (product - first.astype(F32)).astype(BF)
    delta = dot(first, spread[...]) + dot(second, spread[...])
    ge[:, :D] = gctx
    ge[:, D:] = row_terms(-delta)[:, HEAD_DIM:]


def qkv_back_kernel(
    gq, gk, gv, low, n1, a, b_q, b_kv, hidden, gain, gh2, wq, wkv, g, ga, gb_q, gb_kv, wq_here, wkv_here, sems
):
    first = pltpu.make_async_copy(wq, wq_here, sems.at[0])
    second = pltpu.make_async_copy(wkv, wkv_here, sems.at[1])
    first.start()
    second.start()
    q, k, v = gq[...], gk[...].reshape(ROWS, WIDE), gv[...].reshape(ROWS, WIDE)
    glow = dot_t(q, b_q[...]) + dot_t(k, b_kv[:, :WIDE]) + dot_t(v, b_kv[:, WIDE:])
    glow = glow.astype(BF)
    ga[...] = t_dot(glow, n1[...]).astype(BF)
    gb_q[...] = t_dot(low[...], q).astype(BF)
    gb_kv[:, :WIDE] = t_dot(low[...], k).astype(BF)
    gb_kv[:, WIDE:] = t_dot(low[...], v).astype(BF)
    first.wait()
    gn1 = dot_t(q, wq_here[...])
    second.wait()
    gn1 = gn1 + dot_t(k, wkv_here[:, :WIDE]) + dot_t(v, wkv_here[:, WIDE:]) + dot_t(glow, a[...])
    r, inv = normalised(hidden[...])
    gr = gn1 * gain[...]
    g[...] = gh2[...] + inv * (
        gr - jnp.mean(gr, axis=1, keepdims=True) - r * jnp.mean(gr * r, axis=1, keepdims=True)
    )


def mlp_both_kernel(
    ctx, hidden, gain, g, a_o, b_o, a_u, b_d, spread, b_u, a_d, wout, wup, wdown,
    after, gh2, ge, ga_o, gb_o, ga_u, gb_d, ga_d, gb_u
):
    x = ctx[:, :D]
    low_o = dot(x, a_o[...]).astype(BF)
    gh2[...] = hidden[...] + dot(x, wout[...]) + dot(low_o, b_o[...])
    normed = (normalised(gh2[...])[0] * gain[...]).astype(BF)
    low = dot(normed, a_u[...]).astype(BF)
    gy = g[...].astype(BF)
    glow_d = dot_t(gy, b_d[...]).astype(BF)
    total, total_low = jnp.zeros((ROWS, D), F32), jnp.zeros((ROWS, RANK), F32)
    gn2, glow_u = jnp.zeros((ROWS, D), F32), jnp.zeros((ROWS, RANK), F32)
    for a, b in BACK_PIECES:
        up = dot(normed, wup[:, a:b]) + dot(low, b_u[:, a:b])
        phi = 0.5 * (1.0 + lax.erf(up * 0.7071067811865476))
        act = (up * phi).astype(BF)
        ga_d[:, a:b] = t_dot(glow_d, act).astype(BF)
        total = total + dot(act, wdown[a:b, :])
        total_low = total_low + dot(act, a_d[a:b, :])
        gact = dot_t(gy, wdown[a:b, :]) + dot_t(glow_d, a_d[a:b, :])
        density = jnp.exp(-0.5 * up * up) * 0.3989422804014327
        gup = (gact * (phi + up * density)).astype(BF)
        gb_u[:, a:b] = t_dot(low, gup).astype(BF)
        gn2 = gn2 + dot_t(gup, wup[:, a:b])
        glow_u = glow_u + dot_t(gup, b_u[:, a:b])
    low_d = total_low.astype(BF)
    gb_d[...] = t_dot(low_d, gy).astype(BF)
    after[...] = (gh2[...] + (total + dot(low_d, b_d[...]))).astype(BF)
    glow_u = glow_u.astype(BF)
    gn2 = gn2 + dot_t(glow_u, a_u[...])
    ga_u[...] = t_dot(glow_u, normed).astype(BF)
    through_norm(g, gh2[...], gain, gn2, x, low_o, a_o, b_o, wout, spread, gh2, ge, ga_o, gb_o)


def shape_of(rows, width, kind=BF):
    return jax.ShapeDtypeStruct((rows, width), kind)


def mlp_call(kernel, args, outs, flops, weights=0, limit=24):
    scratch = [
        pltpu.VMEM((D, D), BF),
        pltpu.VMEM((D, FF), BF),
        pltpu.VMEM((FF, D), BF),
        pltpu.SemaphoreType.DMA((1 + 2 * len(BACK_PIECES),)),
    ]
    return pl.pallas_call(
        kernel,
        out_shape=outs,
        in_specs=[HERE] * (len(args) - weights) + [ANYWHERE] * weights,
        out_specs=(HERE,) * len(outs),
        scratch_shapes=scratch if weights else (),
        compiler_params=pltpu.CompilerParams(vmem_limit_bytes=limit * 1024 * 1024),
        cost_estimate=pl.CostEstimate(flops=flops, bytes_accessed=24 << 20, transcendentals=ROWS * FF),
    )(*args)


def mlp_fwd(*args):
    outs = (shape_of(ROWS, D, F32), shape_of(ROWS, D)) + (shape_of(ROWS, RANK),) * 3
    outs += (shape_of(ROWS, D, F32), shape_of(ROWS, D))
    return mlp_call(mlp_fwd_kernel, args, outs, 10_000_000_000, limit=12)


def mlp_both(*args):
    outs = (shape_of(ROWS, D), shape_of(ROWS, D, F32), shape_of(ROWS, WIDE)) + (shape_of(RANK, D),) * 4
    outs += (shape_of(RANK, FF),) * 2
    return mlp_call(mlp_both_kernel, args, outs, 18_000_000_000, limit=20)


def mlp_back(*args):
    outs = (shape_of(ROWS, D, F32), shape_of(ROWS, WIDE)) + (shape_of(RANK, D),) * 4
    outs += (shape_of(RANK, FF),) * 2
    return mlp_call(mlp_back_kernel, args, outs, 16_000_000_000, 3, 56)


def qkv_back(*args):
    return pl.pallas_call(
        qkv_back_kernel,
        out_shape=(shape_of(ROWS, D, F32), shape_of(RANK, D), shape_of(RANK, WIDE), shape_of(RANK, 2 * WIDE)),
        in_specs=[HERE] * 11 + [ANYWHERE] * 2,
        out_specs=(HERE,) * 4,
        scratch_shapes=[
            pltpu.VMEM((D, WIDE), BF),
            pltpu.VMEM((D, 2 * WIDE), BF),
            pltpu.SemaphoreType.DMA((2,)),
        ],
        compiler_params=pltpu.CompilerParams(vmem_limit_bytes=20 * 1024 * 1024),
        cost_estimate=pl.CostEstimate(flops=5_000_000_000, bytes_accessed=10 << 20, transcendentals=0),
    )(*args)


def ring_start(block):
    return lax.ppermute(block, "seq", UP), lax.ppermute(block, "seq", DOWN)


def ring_far(block, before, after, beside=()):
    far_lo = lax.ppermute(before[0], "seq", UP)
    far_hi = lax.ppermute(after[1], "seq", DOWN)
    far_lo, far_hi, *beside = tie(far_lo, far_hi, *beside)
    own = jnp.stack([block, before, after, jnp.stack([far_lo, far_hi])])
    return (own, *beside) if beside else own


def other_core(own):
    return lax.ppermute(own, "seq", CORE)


def sum_sequence(parts, core, y):
    parts = parts.reshape((4, 2) + parts.shape[1:])
    mine = lax.dynamic_index_in_dim(parts, core, 1, keepdims=False)
    other = lax.dynamic_index_in_dim(parts, 1 - core, 1, keepdims=False)
    half = mine.astype(F32) + lax.ppermute(other, "seq", CORE).astype(F32)

    def of(step):
        return lax.dynamic_index_in_dim(half, (y + step) % 4, 0, keepdims=False)

    total = of(0)
    for step, route in ((1, UP), (3, DOWN), (2, FAR)):
        total = total + lax.ppermute(of(step).astype(BF), "seq", route).astype(F32)
    return total


def tie(*values):
    return lax.optimization_barrier(values)


def eighths(turned, straight):
    def cut(a, part):
        return jnp.pad(a, ((0, 0), (0, 8 * part - a.shape[1]))).reshape(RANK, 8, part)

    first = cut(jnp.concatenate(turned, axis=1), PART_A)
    return jnp.swapaxes(jnp.concatenate([first, cut(straight, PART_B)], axis=2), 0, 1)


def by_adapter_kernel(picks, *refs):
    parts, out_ref, acc = refs[:-2], refs[-2], refs[-1]
    acc[...] = jnp.zeros_like(acc)
    at = 0
    for ref in parts:
        for k in range(ref.shape[0]):
            rows = pl.ds(pl.multiple_of(picks[at] * RANK, RANK), RANK)
            acc[rows, :] = acc[rows, :] + ref[k].astype(F32)
            at += 1
    for j in range(PART // 128):
        square = acc[:, 128 * j : 128 * (j + 1)]
        square = square.T if 128 * j < PART_A else square
        out_ref[128 * j : 128 * (j + 1), :] = square.astype(BF)


def by_adapter(parts, picks):
    return pl.pallas_call(
        by_adapter_kernel,
        out_shape=jax.ShapeDtypeStruct((PART, 128), BF),
        in_specs=[pl.BlockSpec(memory_space=pltpu.SMEM)]
        + [pl.BlockSpec(memory_space=pltpu.VMEM)] * len(parts),
        out_specs=pl.BlockSpec(memory_space=pltpu.VMEM),
        scratch_shapes=[pltpu.VMEM((8 * RANK, PART), F32)],
        compiler_params=PARAMS,
        cost_estimate=pl.CostEstimate(flops=16 * RANK * PART, bytes_accessed=2 << 20, transcendentals=0),
    )(picks, *parts)


def unfold_rows(layer, rows, outs):
    turned, straight = outs[:-1], outs[-1]
    start = 0
    for out, width in zip(turned, TURNED):
        at = start
        while at < start + width:
            n = min(start + width, (at // PART_A + 1) * PART_A) - at
            out[layer, at - start : at - start + n, :] = rows(at // PART_A, at % PART_A, n)
            at += n
        start += width
    squares = PART_B // 128
    for t in range(FF // 128):
        value = rows(t // squares, PART_A + 128 * (t % squares), 128)
        straight[layer, :, 128 * t : 128 * (t + 1)] = value


def unfold_late_kernel(ref, *outs):
    unfold_rows(0, lambda e, at, n: ref[e, at : at + n, :].astype(F32), outs)


def unfold_kernel(place, own_ref, sib_ref, *refs):
    half = len(refs) // 2

    def rows(e, at, n):
        k = place[e]
        mine = own_ref[k % 4, at : at + n, :]
        other = sib_ref[k % 4, at : at + n, :]
        return jnp.where(k < 4, mine.astype(F32), other.astype(F32))

    unfold_rows(0, rows, refs[half:])


def one_layer(layer, *shape):
    return pl.BlockSpec((1,) + shape, lambda i: (layer, 0, 0))


def unfold(kernel, layer, *args):
    shapes = [(w, 128) for w in TURNED] + [(128, FF)]
    whole = [jax.ShapeDtypeStruct((2,) + shape, F32) for shape in shapes]
    first, earlier = (args, ()) if layer == 1 else (args[:3], args[3])
    specs = [pl.BlockSpec(memory_space=pltpu.SMEM)] if layer == 0 else []
    specs += [fixed(*a.shape) for a in first[len(specs) :]] + [ANYWHERE] * len(earlier)
    return pl.pallas_call(
        kernel,
        grid=(1,),
        out_shape=tuple(whole),
        in_specs=specs,
        out_specs=tuple(one_layer(layer, *shape) for shape in shapes),
        input_output_aliases={3 + n: n for n in range(len(earlier))},
        compiler_params=pltpu.CompilerParams(vmem_limit_bytes=40 * 1024 * 1024),
        cost_estimate=pl.CostEstimate(flops=0, bytes_accessed=14 << 20, transcendentals=0),
    )(*first, *earlier)


def fixed(*shape):
    return pl.BlockSpec(shape, lambda i: (0,) * len(shape))


def share(w_qkv, w_out, w_up, w_down, z_lo, spare):
    def half_row(w, front, lines):
        size = lines * 128 - w.shape[1]
        first = jnp.pad(w, ((0, 0), (0, size)))
        second = jnp.pad(w, ((0, 0), (front, size - front)))
        return jnp.where(z_lo == 0, first, second).reshape(-1, lines, 128)

    def put(a, room):
        return jnp.pad(a, ((0, 0), (0, room - a.shape[1]), (0, 0)))

    extra = jnp.broadcast_to(spare[None], (2, 1, 128))
    attention = [
        put(half_row(w_qkv, 32, N_QKV), AT_OUT),
        put(half_row(w_out, 32, N_OUT), LINES - AT_OUT - 1),
        extra,
    ]
    up, down = put(w_up.reshape(-1, N_UP, 128), LINES), put(w_down.reshape(-1, N_DOWN, 128), LINES - 1)
    return jnp.concatenate(attention, axis=1), jnp.concatenate([up, down, extra], axis=1)


def spin(a):
    return pltpu.roll(a, HEAD_DIM, 1)


def fill(ref, base, lines):
    ref[pl.ds(base, lines.shape[0], stride=2), :] = lines


def between(ref, base, n):
    now, later = ref[pl.ds(base, n, stride=2), :], ref[pl.ds(base + 2, n, stride=2), :]
    ref[pl.ds(base + 1, n, stride=2), :] = spin(jnp.where(lanes(n) < HEAD_DIM, later, now))


def columns(ref, dst, to, start, units, step=2):
    got = ref[pl.ds(start, dst.shape[0], stride=units), :].astype(BF)
    n = min(128, dst.shape[1] - to)
    dst[:, to : to + n] = got[:, :n]


def lines_of(ref, pair, zl, start, n):
    return ref[0, zl, 0, pair % 4, pair // 4, start : start + n, :].astype(F32)


def unpack_attention_kernel(g_ref, *refs):
    def lines(pair, zl):
        return lines_of(g_ref, pair, zl, 0, N_QKV), lines_of(g_ref, pair, zl, AT_OUT, N_OUT)

    unpack_attention_lines(lines, *refs)


def unpack_first_kernel(steps, own_1, sib_1, own_2, sib_2, *refs):
    def lines(pair, zl):
        x, core = pair % 4, pair // 4
        z_at, x_at = steps[4 + 2 * (pl.program_id(0) // 4) + zl], steps[8 + x]
        mine = steps[12] == core
        top = jnp.where(mine, own_1[z_at, 0, x_at], sib_1[z_at, 0, x_at])
        bottom = jnp.where(mine, own_2[0, z_at, x_at], sib_2[0, z_at, x_at])
        both = jnp.concatenate([top.astype(F32), bottom.astype(F32)], axis=0)
        return both[:N_QKV], both[AT_OUT : AT_OUT + N_OUT]

    unpack_attention_lines(lines, *refs)


def unpack_attention_lines(lines, q_ref, kv_ref, out_ref, s_qkv, s_out):
    low = lanes(1) < HEAD_DIM
    zero = jnp.zeros((1, 128), F32)
    for pair in range(8):
        (qkv0, out0), (qkv1, out1) = lines(pair, 0), lines(pair, 1)
        base, base_out = pair * 867, pair * 289
        fill(s_qkv, base, qkv0)
        fill(s_qkv, base + 433, qkv1)
        between(s_qkv, base, N_QKV - 1)
        between(s_qkv, base + 433, N_QKV)
        s_qkv[pl.ds(base + 432, 1), :] = qkv0[N_QKV - 1 :] + spin(jnp.where(low, qkv1[:1], zero))
        s_qkv[pl.ds(base + 433, 1), :] = qkv1[:1] + spin(jnp.where(low, zero, qkv0[N_QKV - 1 :]))
        fill(s_out, base_out, out0)
        fill(s_out, base_out + 144, out1)
        s_out[pl.ds(base_out + 144, 1), :] = out0[N_OUT - 1 :] + out1[:1]
        between(s_out, base_out, N_OUT - 1)
        between(s_out, base_out + 144, N_OUT - 1)
    half = lanes(BLOCK) < HEAD_DIM
    for dst, to, first in ((q_ref, 0, 0), (kv_ref, 0, 17), (kv_ref, WIDE, 34)):
        for j in range(8):
            columns(s_qkv, dst, to + 128 * j, first + 2 * j, 51)
        got = s_qkv[pl.ds(first + 16, BLOCK, stride=51), :]
        dst[:, to + D - HEAD_DIM : to + WIDE] = jnp.where(half, got, 0.0).astype(BF)
    for j in range(9):
        columns(s_out, out_ref, 128 * j, 2 * j, 17)


def unpack_mlp_kernel(g_up, g_down, up_ref, down_ref, s_up, s_down):
    for pair in range(8):
        for zl in range(2):
            at = pair * 2 + zl
            s_up[pl.ds(at * N_UP, N_UP), :] = lines_of(g_up, pair, zl, 0, N_UP)
            fill(s_down, at * 2 * N_DOWN, lines_of(g_down, pair, zl, 0, N_DOWN))
    for at in range(16):
        between(s_down, at * 2 * N_DOWN, N_DOWN)
    for j in range(34):
        columns(s_up, up_ref, 128 * j, j, 34)
    for j in range(9):
        columns(s_down, down_ref, 128 * j, 2 * j, 17)


def unpack(kernel, got, at, outs, scratch_lines, limit):
    g = got.reshape(2, 2, 4, 4, 2, -1, 128)

    def spec(k):
        return pl.BlockSpec((1, 2, 1, 4, 2, LINES, 128), lambda i: (i // 4, 0, i % 4, 0, 0, k, 0))

    return pl.pallas_call(
        kernel,
        grid=(8,),
        out_shape=tuple(jax.ShapeDtypeStruct((8 * r, w), BF) for r, w in outs),
        in_specs=[spec(k) for k in at],
        out_specs=tuple(pl.BlockSpec((r, w), lambda i: (i, 0)) for r, w in outs),
        scratch_shapes=[pltpu.VMEM((n, 128), F32) for n in scratch_lines],
        compiler_params=pltpu.CompilerParams(vmem_limit_bytes=limit * 1024 * 1024),
        cost_estimate=pl.CostEstimate(
            flops=0, bytes_accessed=len(at) * (20 << 20), transcendentals=0
        ),
    )(*[g] * len(at))


ATTENTION_OUTS = [(BLOCK, WIDE), (BLOCK, 2 * WIDE), (BLOCK, D)]
ATTENTION_LINES = [8 * 867 + 8, 8 * 289 + 8]


def unpack_attention(got, at):
    return unpack(unpack_attention_kernel, got, [at], ATTENTION_OUTS, ATTENTION_LINES, 36)


def along(axis, block, near):
    name, shift = SHIFTS[axis]
    before = lax.ppermute(block, name, shift(1))
    after = lax.ppermute(block, name, shift(-1))
    if near:
        far = lax.ppermute(block, name, shift(2))
    else:
        n = block.shape[0] // 2
        far = [lax.ppermute(before[:n], name, shift(1)), lax.ppermute(after[n:], name, shift(-1))]
        far = jnp.concatenate(far)
    return jnp.stack([block, before, after, far])


def gather_first(share, later):
    n = LINES // 2
    row = along("x", share, True)
    one, two = along("y", row[:, :n], True), along("z", row[:, n:], True)
    one, two, later = tie(one, two, later)
    one, two = along("z", one, False), along("y", two, False)
    return (one, other_core(one), two, other_core(two)), later


def unpack_first(one, sib_one, two, sib_two, steps):
    n = LINES // 2
    spec_one = pl.BlockSpec((4, 1, 4, n, 128), lambda i, steps: (0, steps[i % 4], 0, 0, 0))
    spec_two = pl.BlockSpec((1, 4, 4, n, 128), lambda i, steps: (steps[i % 4], 0, 0, 0, 0))
    return pl.pallas_call(
        unpack_first_kernel,
        grid_spec=pltpu.PrefetchScalarGridSpec(
            num_scalar_prefetch=1,
            grid=(8,),
            in_specs=[spec_one, spec_one, spec_two, spec_two],
            out_specs=tuple(pl.BlockSpec((r, w), lambda i, steps: (i, 0)) for r, w in ATTENTION_OUTS),
            scratch_shapes=[pltpu.VMEM((n, 128), F32) for n in ATTENTION_LINES],
        ),
        out_shape=tuple(jax.ShapeDtypeStruct((8 * r, w), BF) for r, w in ATTENTION_OUTS),
        compiler_params=pltpu.CompilerParams(vmem_limit_bytes=26 * 1024 * 1024),
        cost_estimate=pl.CostEstimate(flops=0, bytes_accessed=30 << 20, transcendentals=0),
    )(steps, one, sib_one, two, sib_two)


def unpack_mlp(got, at):
    outs = [(BLOCK, FF), (4 * BLOCK, D)]
    return unpack(unpack_mlp_kernel, got, [at, at + 1], outs, [16 * N_UP, 32 * N_DOWN + 8], 20)


def shards(
    tokens, segments, adapter_pick, norm_gain, w_qkv, w_out, w_up, w_down,
    a_qkv, b_qkv, a_out, b_out, a_up, b_up, a_down, b_down, grad_out
):
    layers = norm_gain.shape[0]
    index = lax.axis_index("seq")
    z_hi, place = index // 8, index % 8
    core, y = place % 2, place // 2

    def halves(own, other):
        return jnp.where(z_hi == 0, jnp.stack([own, other]), jnp.stack([other, own]))

    def mine(a):
        return lax.dynamic_index_in_dim(a, z_hi, 0, keepdims=False)

    def theirs(a):
        return lax.dynamic_index_in_dim(a, 1 - z_hi, 0, keepdims=False)

    batch = lax.axis_index("batch")
    spare = (segments.reshape(1, 128), jnp.pad(adapter_pick[None], ((0, 0), (0, 126))))
    attention, _ = share(w_qkv, w_out, w_up, w_down, batch % 2, spare[0].astype(BF))
    _, mlp = share(w_qkv, w_out, w_up, w_down, batch % 2, spare[1].astype(BF))

    def gather(a):
        return lax.all_gather(a, BOTH, axis=0, tiled=True, axis_index_groups=ALL)

    early = gather(jnp.concatenate([mlp[0], attention[1]], axis=0))
    late = gather(mlp[1])
    raw = (a_qkv, b_qkv, a_out, b_out, a_up, b_up, a_down, b_down, norm_gain)
    (one, sib_one, two, sib_two), raw = gather_first(attention[0], raw)
    a_qkv, b_qkv, a_out, b_out, a_up, b_up, a_down, b_down, norm_gain = raw

    sent = lax.ppermute(jnp.stack([theirs(tokens), theirs(grad_out)]), "seq", SWAP)
    hidden = halves(mine(tokens), sent[0]).reshape(2 * HALF, D).astype(F32)
    grad_hidden = halves(mine(grad_out), sent[1]).reshape(2 * HALF, D).astype(F32)
    pick = mine(adapter_pick)

    def segments_of(two):
        lines = two[:, :, 0, -1]
        lines = jnp.stack([lines[:, 0], lines[:, 3]])
        return lax.dynamic_slice(lines, (0, 0, z_hi * HALF), (2, 4, HALF))

    seg = jnp.stack([segments_of(two), segments_of(sib_two)], axis=1)
    seg = jnp.where(z_hi == 0, seg, seg[::-1]).astype(jnp.int32)
    offset = jnp.arange(HALF, dtype=jnp.int32)
    start = jnp.array([0, KEYS // 2], jnp.int32)[:, None]
    lpos = (start + place * HALF + offset[None]).reshape(2 * HALF, 1)
    lseg = seg[:, 0, 0].reshape(2 * HALF, 1)
    ys = (y + jnp.array([0, 3, 1, 2], jnp.int32)) % 4
    order = jnp.concatenate([2 * ys + core, 2 * ys + 1 - core])
    kpos = (start[:, :, None] + (order * HALF)[None, :, None] + offset).reshape(1, KEYS)
    where = (lpos, lseg, kpos, seg.reshape(1, KEYS))

    z_lo, x = batch % 2, batch // 2
    z = z_hi * 2 + z_lo
    picks = early.reshape(2, 2, 4, 4, 2, -1, 128)[0, :, 0, :, 0, 2 * LINES - 1, :2].astype(jnp.int32)
    picks = jnp.swapaxes(picks, 0, 1).reshape(16)
    steps = jnp.array([0, 3, 1, 2], jnp.int32)

    def sequence(zs, xs):
        return 2 * (2 * xs + zs % 2) + zs // 2

    four = jnp.arange(4, dtype=jnp.int32)
    picks_in_order = jnp.take(picks, sequence(four[:, None], four[None, :]).reshape(16))
    zs, xs = (z + steps) % 4, (x + steps) % 4
    picks_by_step = jnp.take(picks, sequence(zs[None, :], xs[:, None]).reshape(16))
    eight = jnp.arange(8, dtype=jnp.int32)
    back = jnp.array([0, 2, 3, 1], jnp.int32)
    place_by_step = 4 * ((eight % 2) ^ core) + jnp.take(back, (eight // 2 - y) % 4)
    arrival = [jnp.take(back, (four - at) % 4) for at in (y, z, x)]
    arrival = jnp.concatenate(arrival + [core[None]]).astype(jnp.int32)

    def low_in(a, l):
        return lax.dynamic_slice_in_dim(a[l], pick * RANK, RANK, 1)

    def low_out(b, l):
        return lax.dynamic_slice_in_dim(b[l], pick * RANK, RANK, 0)

    heads_of = (jnp.arange(D, dtype=jnp.int32) // HEAD_DIM)[:, None]
    spread = (heads_of == (jnp.arange(128, dtype=jnp.int32)[None, :] - HEAD_DIM) // 3).astype(BF)

    def adapters(l):
        b_first = low_out(b_qkv, l)
        b_kv = jnp.concatenate([widen(b_first[:, D : 2 * D]), widen(b_first[:, 2 * D :])], axis=1)
        rest = [f(a, l) for pair in ((a_out, b_out), (a_up, b_up), (a_down, b_down)) for f, a in zip((low_in, low_out), pair)]
        return [low_in(a_qkv, l), widen(b_first[:, :D]), b_kv] + rest

    n1 = (norm_stats(hidden)[0] * norm_gain[0, 0]).astype(BF)
    ahead = (where, spread, n1, grad_hidden, [adapters(l) for l in range(layers)])
    sib_one, (where, spread, n1, grad_hidden, adapter_parts) = tie(sib_one, ahead)
    first = unpack_first(one, sib_one, two, sib_two, arrival)
    saved, queries = [], []
    for l in range(layers):
        a_first, b_q, b_kv, a_o, b_o, a_u, b_u, a_d, b_d = adapter_parts[l]
        wq, wkv, wout = first
        low_qkv = dot(n1, a_first).astype(BF)
        kv = (dot(n1, wkv) + dot(low_qkv, b_kv)).astype(BF).reshape(2, HALF, 2 * WIDE)
        q = (dot(n1, wq) + dot(low_qkv, b_q)).astype(BF) * jnp.asarray(0.125, BF)
        before, after = ring_start(kv)
        if l == 0:
            before, after, q, wup, wdown = tie(before, after, q, *unpack_mlp(early, 0))
        else:
            before, after, q, late = tie(before, after, q, late)
        if l == 0:
            kv_own, *first = ring_far(kv, before, after, unpack_attention(early, 2))
        else:
            kv_own, wup, wdown = ring_far(kv, before, after, unpack_mlp(late, 0))
        kv_sib = other_core(kv_own)
        ctx, qe = attend_fwd(q, kv_own, kv_sib, where)
        queries.append(qe.reshape(2, HALF, WIDE))
        gains = norm_gain[l, 1][None], norm_gain[(l + 1) % layers, 0][None]
        small, large = (a_o, b_o, a_u, b_d), (b_u, a_d, wout, wup, wdown)
        rows, hidden_next, n1_next = None, None, None
        if l < layers - 1:
            middle, n2, low_o, low_u, low_d, hidden_next, n1_next = mlp_fwd(ctx, hidden, *gains, *small, *large)
            rows = (ctx, middle, gains[0], n2, low_o, low_u, low_d)
        else:
            starts = [ring_start(a) for a in queries]
            result, *back = mlp_both(ctx, hidden, gains[0], grad_hidden, *small, spread, *large)
            starts, back = tie(starts, back)
            queries = [ring_far(a, *start) for a, start in zip(queries, starts)]
        saved.append(
            (hidden, n1, low_qkv, kv, kv_own, kv_sib, qe)
            + (rows, small, large, a_first, b_q, b_kv, wq, wkv)
        )
        hidden, n1 = hidden_next, n1_next

    behind = None
    for l in reversed(range(layers)):
        hidden_in, n1, low_qkv, kv, kv_own, kv_sib, qe, rows, small, large, a_first, b_q, b_kv, wq, wkv = saved[l]
        if l < layers - 1:
            back = mlp_back(g, *rows, *small, spread, *large)
        gh2, ge, ga_o, gb_o, ga_u, gb_d, ga_d, gb_u = back
        if l == layers - 1:
            queries, ge = tie(queries, ge)
        qe_own, qe_sib = queries[l], other_core(queries[l])
        g_block = ge.reshape(2, HALF, WIDE)
        g_before, g_after = ring_start(g_block)
        if behind is not None:
            behind, ge = tie(behind, ge)
            behind = lax.all_gather(behind, BOTH, axis=0, axis_index_groups=SAME_PLACE)
        gq = attend_dq(qe, ge, kv_own, kv_sib, where)
        g_before, g_after, gq = tie(g_before, g_after, gq)
        ge_own = ring_far(g_block, g_before, g_after)
        ge_sib = other_core(ge_own)
        gk, gv = attend_dkv(kv, qe_own, qe_sib, ge_own, ge_sib, where)
        g, ga_q, gb_q, gb_kv = qkv_back(
            gq, gk, gv, low_qkv, n1, a_first, b_q, b_kv, hidden_in, norm_gain[l, 0][None], gh2, wq, wkv
        )
        gb_q = [gb_q[:, :D], gb_kv[:, :D], gb_kv[:, WIDE : WIDE + D]]
        parts = eighths([ga_q, ga_o, ga_u, ga_d] + gb_q + [gb_o, gb_d], gb_u)
        if l > 0:
            parts, g = tie(parts, g)
            behind = sum_sequence(parts, core, y)

    got = lax.all_to_all(parts, BOTH, 0, 0, axis_index_groups=SAME_SEQUENCE)
    part = jnp.sum(got.astype(F32), axis=0).astype(BF)
    along_z = [lax.ppermute(part, BOTH, z_shift(by)) for by in (1, -1, 2)]
    behind, part = tie(behind, part)
    one = by_adapter([behind], picks_in_order)
    one, *along_z = tie(one, *along_z)
    one = lax.all_gather(one, BOTH, axis=0, axis_index_groups=SAME_SEQUENCE)
    along_z = jnp.stack([part] + along_z)
    before = lax.ppermute(along_z, "batch", x_shift(1))
    after = lax.ppermute(along_z, "batch", x_shift(-1))
    sent_home = theirs(g.reshape(2, HALF, D)), theirs(result.reshape(2, HALF, D))
    back_home = [lax.ppermute(a, "seq", SWAP) for a in sent_home]
    far = [lax.ppermute(before[:2], "batch", x_shift(1)), lax.ppermute(after[2:], "batch", x_shift(-1))]
    whole = by_adapter([along_z, before, after] + far, picks_by_step)
    whole = whole.reshape(2, -1, 128)
    own = ring_far(whole, *ring_start(whole))
    one = unfold(unfold_late_kernel, 1, one)
    grad_tokens = halves(mine(g.reshape(2, HALF, D)), back_home[0])
    result = halves(mine(result.reshape(2, HALF, D)), back_home[1])
    own, grad_tokens, result = tie(own, grad_tokens, result)
    sib = other_core(own)
    sib, *one = tie(sib, *one)
    sib = sib.reshape(4, PART, 128)
    ga_q, ga_o, ga_u, ga_d, gb_q, gb_o, gb_d, gb_u = unfold(
        unfold_kernel, 0, place_by_step, own.reshape(4, PART, 128), sib, one
    )
    gb_q, gb_o, gb_d = (jnp.swapaxes(a, 1, 2) for a in (gb_q, gb_o, gb_d))

    return result, grad_tokens, ga_q, gb_q, ga_o, gb_o, ga_u, gb_u, ga_d, gb_d


def solution(mesh):
    rows, flat, whole = P("batch", "seq", None), P(None, ("seq", "batch")), P()
    in_specs = (rows, P("batch", "seq"), P("batch"), whole) + (flat,) * 4 + (whole,) * 8 + (rows,)
    out_specs = (rows, rows) + (whole,) * 8
    return jax.shard_map(shards, mesh=mesh, in_specs=in_specs, out_specs=out_specs, check_vma=False)
```
